128 devices in a mesh: region: 8 (over y, core), sub: 16 (over x, z).
Axes of the slice: x: 4, y: 4, z: 4, core: 2. Of those that a mesh axis runs over, the one named last changes fastest.
Arguments:
- orbitals: bfloat16 [512, 48, 2304], P(('region', 'sub')), may hold values from -6 to 6
- trial_set: bfloat16 [512, 48, 2304], P(('region', 'sub')), may hold values from -6 to 6
- own_slot: int32 [512], P(('region', 'sub')), may hold values from 0 to 3
- partner_route: int32 [512, 1], P(('region', 'sub')), may hold values from 0 to 16; in each aligned block of 4 rows (0 to 3, 4 to 7, ...) at most 2 rows name the same one
- partner_slot: int32 [512], P(('region', 'sub')), may hold values from 0 to 3
- offsets: int32 [512, 3], replicated, may hold values from 0 to 23
Outputs:
- fock_orbitals: bfloat16 [512, 48, 2304], P(('region', 'sub'))
- fock_trial: bfloat16 [512, 48, 2304], P(('region', 'sub'))
The draws below stay inside these ranges and needn't reach their ends.
Inputs may be any that keep to these rules, and one draw needn't show every extreme that they name: `partner_route`: values below 16 name the device of the same region with that sub index; 16 names the device of the next region (after the last comes the first) with the same sub index. Among the 4 pairs of one device no value occurs more than 2 times, and some device has a value exactly 2 times.
All inputs are finite; a program needn't handle non-finite values.
Results may differ from the reference program's by a relative error of at most 0.0042.
Values may be sent and summed in bfloat16 or wider, within the bound.
No kernel may reach another device: no remote copies, remote signals or barrier semaphores. Data moves between devices by JAX's collectives and lax.ppermute only.
A program may use at most 192 MiB of HBM per device.

```python
import math
import jax
import jax.numpy as jnp
import numpy as np
from jax import lax

BOX = 48
PLANE = 2304
SHIFT = 24
ORB_DEV = 4
ORBITALS = 512
PAIRS_DEV = 4
PAIRS = 512
CAP = 2
N_REGION = 8
N_SUB = 16


def touch_ends(entries, stream_key, low, high):
    longest = entries.shape.index(max(entries.shape))
    spots = []
    for shift in (0, 1):
        where = [jax.random.randint(jax.random.fold_in(stream_key, axis), (), 0, length) for axis, length in enumerate(entries.shape)]
        where[longest] = (where[longest] + shift) % entries.shape[longest]
        spots.append(tuple(where))
    return entries.at[spots[0]].set(low).at[spots[1]].set(high)


def levels(rng, dims, cuts, low, largest):
    gain, own = 1.0, jax.random.fold_in(rng, 6)
    for position, blocks in cuts:
        draws = jnp.exp(jax.random.uniform(jax.random.fold_in(own, position), (blocks,), jnp.float32, low / len(cuts), largest / len(cuts)))
        gain = gain * jnp.repeat(draws, dims[position] // blocks).reshape([-1 if axis == position else 1 for axis in range(len(dims))])
    return gain


def routed_block(stream_key, own, number, rows, number_of, top, limit, lean):
    ranking = jax.random.permutation(stream_key, number_of)
    crowded, usual = load_shares(number_of, rows * top, limit, lean, True), load_shares(number_of, rows * top, limit, lean, False)
    places = jnp.arange(number_of)

    def named(lengths, rotation):
        used = int((lengths > 0).sum())
        fixed = max(1, used // 4)
        passed = fixed + (places - fixed + rotation * (used - fixed)) % max(1, number_of - fixed)
        return jnp.zeros((number_of,), jnp.int32).at[ranking[jnp.where(places < fixed, places, passed)]].set(jnp.asarray(lengths, jnp.int32))

    lengths = jnp.where(number % 4 == 0, named(crowded, number // 4), named(usual, number - number // 4 - 1))
    mixed = jax.random.permutation(jax.random.fold_in(own, 3), number_of)
    source_of, receiver = mixed[0:number_of // 2 * 2:2], mixed[1:number_of // 2 * 2:2]
    room = jnp.minimum(lengths[source_of] - 1, limit - lengths[receiver]) // 2
    room = jnp.where((source_of == ranking[0]) | (receiver == ranking[0]) | (lengths[receiver] == 0), 0, jnp.maximum(room, 0))
    passed = jax.random.randint(jax.random.fold_in(own, 4), (number_of // 2,), 0, 1 << 20) % (room + 1)
    lengths = lengths.at[source_of].add(-passed).at[receiver].add(passed)
    members = jnp.searchsorted(jnp.cumsum(lengths), jnp.arange(rows * top), side="right").astype(jnp.int32)
    listing = members.reshape(top, rows).T
    listing = listing[jax.random.permutation(jax.random.fold_in(own, 1), rows)]
    rotation = jax.random.randint(jax.random.fold_in(own, 2), (rows, 1), 0, top)
    return jnp.take_along_axis(listing, (jnp.arange(top)[None, :] + rotation) % top, axis=1)


def load_shares(amount, total, most, slope, full):
    loads = [(1 << 20) // math.isqrt(standing ** slope) + 1 for standing in range(1, amount + 1)]
    largest = most if full else min(most, max(-(-total // amount), total * loads[0] // sum(loads)))
    least = 1 if total - largest >= amount - 1 else 0
    given, surplus = [largest] + [least] * (amount - 1), total - largest - least * (amount - 1)
    while surplus > 0:
        movable = [i for i in range(1, amount) if given[i] < largest] or [i for i in range(1, amount) if given[i] < most]
        mass, left = sum([loads[i] for i in movable]), surplus
        for i in movable:
            addition = min(most - given[i], max(1, left * loads[i] // mass), surplus)
            given[i] = given[i] + addition
            surplus = surplus - addition
    return np.array(given)


def scatter_about(key, dims, deviation, reach, cuts=(), held_as=jnp.bfloat16):
    factor_of = levels(key, dims, cuts, -0.22, 0.18) if cuts else 1.0
    array = jax.random.normal(key, dims, jnp.float32) * deviation * factor_of
    return jnp.minimum(jnp.maximum(array, -reach), reach).astype(held_as)


def setup_inputs(seed: int = 0) -> dict:
    seeds = jax.random.split(jax.random.key(seed), 7)
    orbitals = scatter_about(seeds[0], (ORBITALS, BOX, PLANE), 1.0, 6.0, ((0, 128),))
    trial_set = scatter_about(seeds[1], (ORBITALS, BOX, PLANE), 1.0, 6.0, ((0, 128),))
    own_slot = touch_ends(jax.random.randint(seeds[2], (PAIRS,), 0, ORB_DEV), jax.random.fold_in(seeds[2], 1), 0, ORB_DEV - 1).astype(jnp.int32)
    partner_route_keys = jax.random.split(jax.random.fold_in(seeds[3], 1), PAIRS // PAIRS_DEV)
    partner_route_turns = jax.random.permutation(jax.random.fold_in(seeds[3], 3), PAIRS // PAIRS_DEV)
    partner_route = jax.vmap(lambda own, number: routed_block(jax.random.fold_in(seeds[3], 2), own, number, PAIRS_DEV, N_SUB + 1, 1, CAP, 2))(partner_route_keys, partner_route_turns).reshape((PAIRS, 1))
    partner_slot = touch_ends(jax.random.randint(seeds[4], (PAIRS,), 0, ORB_DEV), jax.random.fold_in(seeds[4], 1), 0, ORB_DEV - 1).astype(jnp.int32)
    offsets = touch_ends(jax.random.randint(seeds[5], (ORBITALS, 3), 0, SHIFT), jax.random.fold_in(seeds[5], 1), 0, SHIFT - 1).astype(jnp.int32)
    return {"orbitals": orbitals, "trial_set": trial_set, "own_slot": own_slot, "partner_route": partner_route, "partner_slot": partner_slot, "offsets": offsets}


SCREEN = 0.5


def kernel_table(box_edge):
    wave_no = jnp.arange(box_edge).astype(jnp.float32)
    eigen = 4.0 * jnp.sin(math.pi * wave_no / box_edge) ** 2
    spectrum = eigen[:, None, None] + eigen[None, :, None] + eigen[None, None, :] + SCREEN
    return 4.0 * math.pi / spectrum


def solve_box(density, green):
    return jnp.real(jnp.fft.ifftn(green * jnp.fft.fftn(density))).astype(jnp.float32)


def shift_box(cells, displace):
    box_edge = cells.shape[0]
    margin = box_edge // 2
    padded = jnp.pad(cells, margin)
    corner = (displace + margin).astype(jnp.int32)
    return lax.dynamic_slice(padded, (corner[0], corner[1], corner[2]), (box_edge, box_edge, box_edge))


def reference(orbitals, trial_set, own_slot, partner_route, partner_slot, offsets):
    phi_cubes = orbitals.reshape(ORBITALS, BOX, BOX, BOX)
    trial_cubes = trial_set.reshape(ORBITALS, BOX, BOX, BOX)
    green = kernel_table(BOX)
    pair_ids = jnp.arange(PAIRS).astype(jnp.int32)
    device = pair_ids // PAIRS_DEV
    region = device // N_SUB
    sub_no = device % N_SUB
    routes = partner_route[:, 0]
    partner_dev = jnp.where(routes < N_SUB, region * N_SUB + routes, ((region + 1) % N_REGION) * N_SUB + sub_no)
    first_ids = (device * ORB_DEV + own_slot).astype(jnp.int32)
    second_ids = (partner_dev * ORB_DEV + partner_slot).astype(jnp.int32)
    zeros_acc = jnp.zeros((ORBITALS, BOX, BOX, BOX), jnp.float32)

    def add_pair(running, pair_no):
        sums_orb, sums_trial = running
        first_id = first_ids[pair_no]
        second_id = second_ids[pair_no]
        displace = (offsets[first_id] - offsets[second_id]).astype(jnp.int32)
        local_box = phi_cubes[first_id].astype(jnp.float32)
        local_trial = trial_cubes[first_id].astype(jnp.float32)
        theirs = shift_box(phi_cubes[second_id], displace).astype(jnp.float32)
        their_trial = shift_box(trial_cubes[second_id], displace).astype(jnp.float32)
        potential = solve_box(local_box * theirs, green)
        near_one = lax.optimization_barrier((potential * theirs).astype(jnp.bfloat16))
        far_one = lax.optimization_barrier(shift_box((potential * local_box).astype(jnp.bfloat16), -displace))
        sums_orb = sums_orb.at[first_id].add(near_one.astype(jnp.float32))
        sums_orb = sums_orb.at[second_id].add(far_one.astype(jnp.float32))
        pot_near = solve_box(theirs * local_trial, green)
        near_two = lax.optimization_barrier((pot_near * theirs).astype(jnp.bfloat16))
        pot_far = solve_box(local_box * their_trial, green)
        far_two = lax.optimization_barrier(shift_box((pot_far * local_box).astype(jnp.bfloat16), -displace))
        sums_trial = sums_trial.at[first_id].add(near_two.astype(jnp.float32))
        sums_trial = sums_trial.at[second_id].add(far_two.astype(jnp.float32))
        return (sums_orb, sums_trial), None

    (sums_orb, sums_trial), unused = lax.scan(add_pair, (zeros_acc, zeros_acc), pair_ids)
    fock_orbitals = (-sums_orb).astype(jnp.bfloat16).reshape(ORBITALS, BOX, BOX * BOX)
    fock_trial = (-sums_trial).astype(jnp.bfloat16).reshape(ORBITALS, BOX, BOX * BOX)
    return (fock_orbitals, fock_trial)
```

```python
import math

import jax
import jax.numpy as jnp
import ml_dtypes
import numpy as np
from jax import lax
from jax.experimental import pallas as pl
from jax.experimental.pallas import tpu as pltpu
from jax.sharding import PartitionSpec as P

BOX = 48
PLANE = BOX * BOX
CHUNK = PLANE // 6
SCREEN = 0.5
GRID = 4
N_SUB = GRID * GRID
ORB_DEV = 4
PAIRS_DEV = 4
N_PAIRS = N_SUB * PAIRS_DEV

PLACES = ((0, 0), (0, 1), (1, 0), (1, 1), (1, 3), (3, 1))
REGION_SOURCE = len(PLACES)
SOURCES = len(PLACES) + 1
LIST_WIDTH = 8

HALF_ROOT3 = math.sqrt(3.0) / 2.0
F32 = jnp.float32
BF16 = jnp.bfloat16


def meeting_table():
    found = [[] for _ in range(N_SUB)]
    for i, (ax, az) in enumerate(PLACES):
        for j, (bx, bz) in enumerate(PLACES):
            delta = (ax - bx) % GRID * GRID + (az - bz) % GRID
            found[delta].append(i + 8 * j + 64 * ax + 512 * az)
    most = max(len(f) for f in found)
    codes = np.array([f + [f[-1]] * (most - len(f)) for f in found], np.int32)
    counts = np.array([len(f) for f in found], np.int32)
    return np.concatenate([counts, codes.reshape(-1)]), most


def high_low(matrix):
    high = matrix.astype(ml_dtypes.bfloat16)
    low = (matrix - high.astype(np.float64)).astype(ml_dtypes.bfloat16)
    return np.stack([high, low])


def cas(angles):
    return np.cos(angles) + np.sin(angles)


def transform_tables():
    turn = 2.0 * math.pi / BOX
    n = np.arange(BOX)
    line = cas(turn * (n[:, None] * n[None, :] % BOX))
    q = np.arange(8)[:, None]
    m = np.arange(8)[None, :]

    def real_part(j):
        return np.kron(cas(turn * (q * (6 * m + j) % BOX)), line)

    def complex_part(j):
        angle = turn * (q * (6 * m + j) % BOX)
        c, s = np.cos(angle), np.sin(angle)
        return np.kron(np.block([[c, -s], [s, c]]), line)

    small = np.stack([real_part(0), real_part(3)])
    large = np.stack([complex_part(1), complex_part(2)])
    lam = 4.0 * np.sin(math.pi * n / BOX) ** 2

    def spectrum(j, weight):
        ky = 6 * np.arange(8) + j
        total = lam[:, None, None] + lam[ky][None, :, None] + lam[None, None, :] + SCREEN
        return (weight * 4.0 * math.pi / total / float(BOX**3)).reshape(BOX, CHUNK)

    one, two = spectrum(1, 2.0), spectrum(2, 2.0)
    green = np.concatenate([spectrum(0, 1.0), spectrum(3, 1.0), one, one, two, two], axis=1)
    rows = high_low(line)
    rows = np.concatenate([rows[0], rows[1], rows[0]], axis=1)
    return dict(
        small=high_low(small),
        large=high_low(large),
        small_back=high_low(small.transpose(0, 2, 1)),
        large_back=high_low(large.transpose(0, 2, 1)),
        green=green.astype(np.float32),
        rows=rows,
    )


def plan_kernel(most, where, meta, offsets, table, listing, loads):
    region, sub, n_region = where[0], where[1], where[2]
    sign = 1 - 2 * (region & 1)
    next_region = jnp.where(region + 1 == n_region, 0, region + 1)
    for i in range(N_SUB):
        loads[i] = 0
    listing[0] = 0

    def place(pair, turn):
        home = pair >> 2
        lane = pair & 3
        own_slot = meta[home * 12 + lane]
        route = meta[home * 12 + 4 + lane]
        partner_slot = meta[home * 12 + 8 + lane]
        abroad = route == N_SUB
        other = jnp.where(abroad, home, route)
        hx, hz = home >> 2, home & 3
        dx = (sign * ((other >> 2) - hx)) & 3
        dz = (sign * ((other & 3) - hz)) & 3
        delta = dx * GRID + dz
        count = jnp.where(abroad, 1, table[delta])
        mine_now = jnp.where(count == 1, 0, 1) == turn

        @pl.when(mine_now)
        def _():
            best_load = jnp.int32(1 << 20)
            best_code = jnp.int32(0)
            best_dev = home
            for k in range(most):
                code = table[N_SUB + delta * most + k]
                sx, sz = (code >> 6) & 7, (code >> 9) & 7
                dev = ((hx + sign * sx) & 3) * GRID + ((hz + sign * sz) & 3)
                load = loads[dev]
                better = load < best_load
                best_load = jnp.where(better, load, best_load)
                best_code = jnp.where(better, code, best_code)
                best_dev = jnp.where(better, dev, best_dev)
            dev = jnp.where(abroad, home, best_dev)
            loads[dev] = loads[dev] + 1

            @pl.when(dev == sub)
            def _():
                at = listing[0]
                listing[0] = at + 1
                row = (at + 1) * LIST_WIDTH
                first = (region * N_SUB + home) * ORB_DEV + own_slot
                second_region = jnp.where(abroad, next_region, region)
                second = (second_region * N_SUB + other) * ORB_DEV + partner_slot
                listing[row] = jnp.where(abroad, 0, best_code & 7)
                listing[row + 1] = own_slot
                listing[row + 2] = jnp.where(abroad, REGION_SOURCE, (best_code >> 3) & 7)
                listing[row + 3] = partner_slot
                for c in range(3):
                    listing[row + 4 + c] = offsets[first * 3 + c] - offsets[second * 3 + c]

    for turn in range(2):

        def body(pair, carry, turn=turn):
            place(pair, turn)
            return carry

        lax.fori_loop(0, N_PAIRS, body, 0)


def split_store(high_ref, low_ref, rows, lanes, value):
    high = value.astype(BF16)
    high_ref[rows, lanes] = high
    low_ref[rows, lanes] = (value - high.astype(F32)).astype(BF16)


def three_dots(high, low, weights, index, columns):
    w_high = weights[0, index, :, columns]
    w_low = weights[1, index, :, columns]
    total = jnp.dot(high, w_high, preferred_element_type=F32)
    total += jnp.dot(low, w_high, preferred_element_type=F32)
    return total + jnp.dot(high, w_low, preferred_element_type=F32)


def solve(density, high, low, work, small, large, small_back, large_back, green, rows, boxes):
    groups = ((0, 0), (0, 1), (1, 0), (1, 1))
    starts = (0, CHUNK, 2 * CHUNK, 4 * CHUNK)
    for b in range(boxes):
        at = pl.ds(b * BOX, BOX)
        for c in range(CHUNK // 128):
            x = [density(b, pl.ds(r * CHUNK + c * 128, 128)) for r in range(6)]
            u = [x[r] + x[r + 3] for r in range(3)]
            v = [x[r] - x[r + 3] for r in range(3)]
            parts = (
                u[0] + u[1] + u[2],
                v[0] - v[1] + v[2],
                v[0] + 0.5 * (v[1] - v[2]),
                -HALF_ROOT3 * (v[1] + v[2]),
                u[0] - 0.5 * (u[1] + u[2]),
                -HALF_ROOT3 * (u[1] - u[2]),
            )
            for j, part in enumerate(parts):
                split_store(high, low, at, pl.ds(j * CHUNK + c * 128, 128), part)

    def plane_pass(small_w, large_w):
        for (is_large, index), start in zip(groups, starts):
            depth = 2 * CHUNK if is_large else CHUNK
            weights = large_w if is_large else small_w
            h = high[:, pl.ds(start, depth)]
            l = low[:, pl.ds(start, depth)]
            for c in range(depth // CHUNK):
                work[:, pl.ds(start + c * CHUNK, CHUNK)] = three_dots(
                    h, l, weights, index, pl.ds(c * CHUNK, CHUNK)
                )

    plane_pass(small, large)

    def row_pass(value):
        h = value.astype(BF16)
        l = (value - h.astype(F32)).astype(BF16)
        return jnp.dot(
            rows[...], jnp.concatenate([h, h, l], axis=0), preferred_element_type=F32
        )

    for b in range(boxes):
        at = pl.ds(b * BOX, BOX)
        for c in range(PLANE // 256):
            lanes = pl.ds(c * 256, 256)
            waves = row_pass(work[at, lanes]) * green[:, lanes]
            split_store(high, low, at, lanes, row_pass(waves))

    plane_pass(small_back, large_back)
    for b in range(boxes):
        at = pl.ds(b * BOX, BOX)
        for c in range(CHUNK // 128):
            t0, t3, t1r, t1i, t2r, t2i = [
                work[at, pl.ds(j * CHUNK + c * 128, 128)] for j in range(6)
            ]
            a0 = t0 + t2r
            t2h = t0 - 0.5 * t2r
            a1 = t2h - HALF_ROOT3 * t2i
            a2 = t2h + HALF_ROOT3 * t2i
            t1s = HALF_ROOT3 * t1i
            b0 = t3 + t1r
            b1 = 0.5 * t1r - t3 - t1s
            b2 = t3 - 0.5 * t1r - t1s
            values = (a0 + b0, a1 + b1, a2 + b2, a0 - b0, a1 - b1, a2 - b2)
            for r, value in enumerate(values):
                work[at, pl.ds(r * CHUNK + c * 128, 128)] = value


def shift_box(value, dx, dy, dz):
    steps = dy * BOX + dz
    value = pltpu.roll(value, jnp.where(dx > 0, BOX - dx, -dx), 0)
    value = pltpu.roll(value, jnp.where(steps > 0, PLANE - steps, -steps), 1)
    lane = lax.broadcasted_iota(jnp.int32, (1, PLANE), 1)
    y = (lane * 43691) >> 21
    z = lane - BOX * y
    x = lax.broadcasted_iota(jnp.int32, (BOX, 1), 0)

    def inside(place, step):
        return ((place + step >= 0) & (place + step < BOX)).astype(F32)

    keep = inside(y, dy) * inside(z, dz)
    return jnp.where(inside(x, dx) * keep > 0.5, value, 0.0)


def rounded(value):
    return value.astype(BF16).astype(F32)


def exchange_kernel(second, *refs):
    sets = 2 if second else 1
    listing = refs[0]
    refs = refs[1:]
    n_in = sets * (SOURCES + 1)
    boxes_in = refs[:n_in]
    small, large, small_back, large_back, green, rows = refs[n_in : n_in + 6]
    outs = refs[n_in + 6 : n_in + 6 + SOURCES + 1]
    acc, held, theirs, high, low, work, sems = refs[n_in + 6 + SOURCES + 1 :]
    per_step = 1 if second else 2
    loads_per_step = 4 if second else 4
    count = listing[0]
    steps = (count + per_step - 1) // per_step

    def fetch(group, source, slot, target, sem):
        refs_of = boxes_in[group * (SOURCES + 1) : (group + 1) * (SOURCES + 1)]
        for s in range(SOURCES):
            if s == 3:
                for half in range(2):

                    @pl.when((source == s) & ((slot >> 1) == half))
                    def _(half=half):
                        pltpu.make_async_copy(
                            refs_of[3 + half].at[slot & 1], target, sem
                        ).start()
            else:
                at = s if s < 3 else s + 1

                @pl.when(source == s)
                def _(at=at):
                    pltpu.make_async_copy(refs_of[at].at[slot], target, sem).start()

    def wanted(step, i):
        if second:
            row = (step + 1) * LIST_WIDTH
            side = i & 1
            return i >> 1, listing[row + 2 * side], listing[row + 2 * side + 1], None
        pair = step * 2 + (i >> 1)
        row = (pair + 1) * LIST_WIDTH
        side = i & 1
        return 0, listing[row + 2 * side], listing[row + 2 * side + 1], pair < count

    def start_loads(step, buffer):
        for i in range(loads_per_step):
            group, source, slot, there = wanted(step, i)
            if there is None:
                fetch(group, source, slot, held.at[buffer, i], sems.at[buffer, i])
            else:

                @pl.when(there)
                def _():
                    fetch(group, source, slot, held.at[buffer, i], sems.at[buffer, i])

    def wait_loads(step, buffer):
        for i in range(loads_per_step):
            there = wanted(step, i)[3]

            def wait():
                pltpu.make_async_copy(
                    boxes_in[0].at[0], held.at[buffer, i], sems.at[buffer, i]
                ).wait()

            if there is None:
                wait()
            else:
                pl.when(there)(wait)

    @pl.when(steps > 0)
    def _():
        start_loads(0, 0)

    def clear(i, carry):
        acc[i] = jnp.zeros((BOX, PLANE), F32)
        return carry

    lax.fori_loop(0, SOURCES * ORB_DEV, clear, 0)

    def add(source, slot, value):
        at = source * ORB_DEV + slot
        acc[at] = acc[at] + value

    def one_step(step, carry):
        buffer = step & 1

        @pl.when(step + 1 < steps)
        def _():
            start_loads(step + 1, 1 - buffer)

        wait_loads(step, buffer)
        consts = (small, large, small_back, large_back, green, rows)
        if second:
            row = (step + 1) * LIST_WIDTH
            dx, dy, dz = listing[row + 4], listing[row + 5], listing[row + 6]
            theirs[0] = shift_box(held[buffer, 1].astype(F32), dx, dy, dz)
            theirs[1] = shift_box(held[buffer, 3].astype(F32), dx, dy, dz)

            def density(b, lanes):
                mine = held[buffer, 2 - 2 * b, :, lanes].astype(F32)
                return mine * theirs[b, :, lanes]

            solve(density, high, low, work, *consts, 2)
            near = rounded(work[pl.ds(0, BOX), :] * theirs[0])
            add(listing[row], listing[row + 1], near)
            far = rounded(work[pl.ds(BOX, BOX), :] * held[buffer, 0].astype(F32))
            add(listing[row + 2], listing[row + 3], shift_box(far, -dx, -dy, -dz))
        else:
            for i in range(2):
                row = (step * 2 + i + 1) * LIST_WIDTH

                @pl.when(step * 2 + i < count)
                def _(i=i, row=row):
                    theirs[i] = shift_box(
                        held[buffer, 2 * i + 1].astype(F32),
                        listing[row + 4],
                        listing[row + 5],
                        listing[row + 6],
                    )

            def density(b, lanes):
                return held[buffer, 2 * b, :, lanes].astype(F32) * theirs[b, :, lanes]

            solve(density, high, low, work, *consts, 2)
            for i in range(2):
                row = (step * 2 + i + 1) * LIST_WIDTH

                @pl.when(step * 2 + i < count)
                def _(i=i, row=row):
                    potential = work[pl.ds(i * BOX, BOX), :]
                    add(listing[row], listing[row + 1], rounded(potential * theirs[i]))
                    far = rounded(potential * held[buffer, 2 * i].astype(F32))
                    far = shift_box(far, -listing[row + 4], -listing[row + 5], -listing[row + 6])
                    add(listing[row + 2], listing[row + 3], far)

        return carry

    lax.fori_loop(0, steps, one_step, 0)

    sizes = (4, 4, 4, 2, 2, 4, 4, 4)
    at = 0
    for out, size in zip(outs, sizes):

        def put(i, carry, out=out, at=at):
            out[i] = acc[at + i].astype(out.dtype)
            return carry

        lax.fori_loop(0, size, put, 0)
        at += size


def exchange(second, listing, boxes, tables):
    sizes = (4, 4, 4, 2, 2, 4, 4, 4)
    any_space = pl.BlockSpec(memory_space=pl.ANY)
    vmem = pl.BlockSpec(memory_space=pltpu.VMEM)
    smem = pl.BlockSpec(memory_space=pltpu.SMEM)
    outs = [
        jax.ShapeDtypeStruct((size, BOX, PLANE), F32 if i == 0 else BF16)
        for i, size in enumerate(sizes)
    ]

    def kernel(*refs):
        exchange_kernel(second, *refs)

    return pl.pallas_call(
        kernel,
        out_shape=outs,
        in_specs=[smem] + [any_space] * len(boxes) + [vmem] * len(tables),
        out_specs=[vmem] * len(outs),
        scratch_shapes=[
            pltpu.VMEM((SOURCES * ORB_DEV, BOX, PLANE), F32),
            pltpu.VMEM((2, 4, BOX, PLANE), BF16),
            pltpu.VMEM((2, BOX, PLANE), F32),
            pltpu.VMEM((2 * BOX, PLANE), BF16),
            pltpu.VMEM((2 * BOX, PLANE), BF16),
            pltpu.VMEM((2 * BOX, PLANE), F32),
            pltpu.SemaphoreType.DMA((2, 4)),
        ],
        compiler_params=pltpu.CompilerParams(vmem_limit_bytes=56 * 1024 * 1024),
        cost_estimate=pl.CostEstimate(
            flops=(2 if second else 1) * 10_000_000_000,
            bytes_accessed=30_000_000,
            transcendentals=0,
        ),
        name="second_application" if second else "first_application",
    )(listing, *boxes, *tables)


def moves(n_region):
    def step(dx, dz):
        pairs = []
        for region in range(n_region):
            sign = 1 - 2 * (region % 2)
            for x in range(GRID):
                for z in range(GRID):
                    to = (x + sign * dx) % GRID * GRID + (z + sign * dz) % GRID
                    pairs.append((region * N_SUB + x * GRID + z, region * N_SUB + to))

        def move(block):
            return lax.ppermute(block, ("region", "sub"), pairs)

        return move

    def across(distance):
        pairs = [(i, (i + distance) % n_region) for i in range(n_region)]

        def move(block):
            return lax.ppermute(block, "region", pairs)

        return move

    return step, across


def per_device(orbitals, trial_set, own_slot, partner_route, partner_slot, offsets):
    n_region = lax.axis_size("region")
    region = lax.axis_index("region")
    sub = lax.axis_index("sub")
    step, across = moves(n_region)
    tables = transform_tables()
    tables = [
        jnp.asarray(tables[k])
        for k in ("small", "large", "small_back", "large_back", "green", "rows")
    ]
    table, most = meeting_table()
    meta = jnp.concatenate([own_slot, partner_route[:, 0], partner_slot])
    meta = lax.all_gather(meta, "sub").reshape(-1)
    where = jnp.stack([region, sub, jnp.int32(n_region)]).astype(jnp.int32)
    smem = pl.BlockSpec(memory_space=pltpu.SMEM)

    def planner(*refs):
        plan_kernel(most, *refs)

    listing = pl.pallas_call(
        planner,
        out_shape=jax.ShapeDtypeStruct(((N_PAIRS + 1) * LIST_WIDTH,), jnp.int32),
        in_specs=[smem] * 4,
        out_specs=smem,
        scratch_shapes=[pltpu.SMEM((N_SUB,), jnp.int32)],
        name="plan",
    )(where, meta, offsets.reshape(-1), jnp.asarray(table))

    def spread(boxes):
        b01 = step(0, 1)(boxes)
        b10 = step(1, 0)(boxes)
        abroad = across(-1)(boxes)
        b13 = step(0, -1)(b10)
        b31 = step(-1, 0)(b01)
        b11_low = step(1, 0)(b01[:2])
        b11_high = step(0, 1)(b10[2:])
        return [boxes, b01, b10, b11_low, b11_high, b13, b31, abroad]

    def gather_back(parts):
        own, c01, c10, c11_low, c11_high, c13, c31, c_abroad = parts
        r13 = step(0, 1)(c13)
        r31 = step(1, 0)(c31)
        r11_low = step(-1, 0)(c11_low)
        r11_high = step(0, -1)(c11_high)
        r_abroad = across(1)(c_abroad)
        none = jnp.zeros_like(r11_low)
        m01 = (
            c01.astype(F32) + r31.astype(F32) + jnp.concatenate([r11_low, none]).astype(F32)
        ).astype(BF16)
        m10 = (
            c10.astype(F32) + r13.astype(F32) + jnp.concatenate([none, r11_high]).astype(F32)
        ).astype(BF16)
        f01 = step(0, -1)(m01)
        f10 = step(-1, 0)(m10)
        total = own + r_abroad.astype(F32) + f01.astype(F32) + f10.astype(F32)
        return (-total).astype(BF16)

    orbital_boxes = spread(orbitals)
    trial_boxes = spread(trial_set)
    first = exchange(False, listing, orbital_boxes, tables)
    second = exchange(True, listing, orbital_boxes + trial_boxes, tables)
    return gather_back(first), gather_back(second)


def solution(mesh):
    in_specs = (
        P(("region", "sub"), None, None),
        P(("region", "sub"), None, None),
        P(("region", "sub")),
        P(("region", "sub"), None),
        P(("region", "sub")),
        P(),
    )
    out_specs = (P(("region", "sub"), None, None), P(("region", "sub"), None, None))
    return jax.shard_map(
        per_device, mesh=mesh, in_specs=in_specs, out_specs=out_specs, check_vma=False
    )
```

```python
import math

import jax
import jax.numpy as jnp
import ml_dtypes
import numpy as np
from jax import lax
from jax.experimental import pallas as pl
from jax.experimental.pallas import tpu as pltpu
from jax.sharding import PartitionSpec as P

BOX = 48
PLANE = BOX * BOX
CHUNK = PLANE // 6
SCREEN = 0.5
GRID = 4
N_SUB = GRID * GRID
ORB_DEV = 4
PAIRS_DEV = 4
N_PAIRS = N_SUB * PAIRS_DEV

PLACES = ((0, 0), (0, 1), (1, 0), (1, 1), (1, 3), (3, 1))
REGION_SOURCE = len(PLACES)
SOURCES = len(PLACES) + 1
LIST_WIDTH = 16
TASK_WIDTH = 8
LISTED = PAIRS_DEV * LIST_WIDTH
NOTE_ROWS = 16
SIZES = (4, 4, 4, 2, 2, 4, 4, 4)
N_OUT = len(SIZES)
N_TABLES = 4
BLOCKS_Y = 6
BLOCKS_Z = 3
MARGIN = 24
ROWS_PADDED = BOX + 2 * MARGIN
SIDE_Y = 3
SIDE_Z = 2
WIDE_Y = BLOCKS_Y + 2 * SIDE_Y
WIDE_Z = BLOCKS_Z + 2 * SIDE_Z
MAX_TASKS = 2 * len(PLACES) * PAIRS_DEV
HALF_ROOT3 = math.sqrt(3.0) / 2.0
F32 = jnp.float32
BF16 = jnp.bfloat16


def meeting_table():
    found = [[] for _ in range(N_SUB)]
    for i, (ax, az) in enumerate(PLACES):
        for j, (bx, bz) in enumerate(PLACES):
            delta = (ax - bx) % GRID * GRID + (az - bz) % GRID
            found[delta].append(i + 8 * j)
    most = max(len(f) for f in found)
    codes = np.array([f + [f[-1]] * (most - len(f)) for f in found], np.int32)
    counts = np.array([len(f) for f in found], np.int32)
    return np.concatenate([counts, codes.reshape(-1)]), most


def high_low(matrix):
    high = matrix.astype(ml_dtypes.bfloat16)
    low = (matrix - high.astype(np.float64)).astype(ml_dtypes.bfloat16)
    return np.stack([high, low])


def cas(angles):
    return np.cos(angles) + np.sin(angles)


def transform_tables():
    turn = 2.0 * math.pi / BOX
    n = np.arange(BOX)
    line = cas(turn * (n[:, None] * n[None, :] % BOX))
    q, w = np.arange(8), np.arange(16)

    def angle_y(j):
        return turn * (q[:, None] * (6 * q[None, :] + j) % BOX)

    def angle_z(j):
        return turn * (w[:, None] * (3 * w[None, :] + j) % BOX)

    def both_parts(angle):
        c, s = np.cos(angle), np.sin(angle)
        return np.block([[c, -s], [s, c]])

    def planes(y, z, sign):
        whole = angle_y(y)[:, None, :, None] + sign * angle_z(z)[None, :, None, :]
        return both_parts(whole.reshape(128, 128))

    def real_complex(y):
        z = both_parts(angle_z(1)).reshape(2, 16, 2, 16)
        return np.einsum("qm,awbn->aqwbmn", cas(angle_y(y)), z).reshape(256, 256)

    def complex_real(y):
        return np.kron(both_parts(angle_y(y)), cas(angle_z(0)))

    zero = np.zeros((128, 128))
    real = [np.kron(cas(angle_y(y)), cas(angle_z(0))) for y in (0, 3)]
    waves = [np.block([[real[0], zero], [zero, real[1]]]), real_complex(0), real_complex(3)]
    waves += [complex_real(1), complex_real(2)]
    for y in (1, 2):
        waves += [planes(y, 1, 1), planes(y, 1, -1)]
    waves = np.stack(waves)
    lam = 4.0 * np.sin(math.pi * n / BOX) ** 2

    def spectrum(y, z, weight):
        ky, kz = 6 * q + y, 3 * w + z
        total = lam[:, None, None] + lam[ky][None, :, None] + lam[kz][None, None, :] + SCREEN
        return (weight * 4.0 * math.pi / total / float(BOX**3)).reshape(BOX, 128)

    order = [(0, 0, 1.0), (3, 0, 1.0)]
    for y, z in ((0, 1), (3, 1), (1, 0), (2, 0), (1, 1), (1, 1), (2, 1), (2, 1)):
        order += [(y, z, 2.0)] * 2
    green = np.concatenate([spectrum(*o) for o in order], axis=1)
    rows = high_low(line)
    rows = np.concatenate([rows[0], rows[1], rows[0]], axis=1)
    return dict(
        waves=high_low(waves),
        waves_back=high_low(waves.transpose(0, 2, 1)),
        green=green.astype(np.float32),
        rows=rows,
    )


TABLES = ("waves", "waves_back", "green", "rows")


def order_table():
    lane = np.arange(8 * BOX)
    q, c, w = lane // BOX, lane % BOX // 16, lane % 16
    table = np.zeros((8 * BOX, 8 * BOX), np.float32)
    table[lane, c * 128 + q * 16 + w] = 1.0
    return table.astype(ml_dtypes.bfloat16)


def plan_kernel(most, where, meta, offsets, table, chosen, used):
    region, sub, n_region = where[0], where[1], where[2]
    sign = 1 - 2 * (region & 1)
    next_region = jnp.where(region + 1 == n_region, 0, region + 1)
    for i in range(2 * len(PLACES)):
        used[i] = 0

    def place(pair, turn):
        own_slot = meta[pair]
        route = meta[PAIRS_DEV + pair]
        partner_slot = meta[2 * PAIRS_DEV + pair]
        abroad = route == N_SUB
        other = jnp.where(abroad, sub, route)
        dx = (sign * ((other >> 2) - (sub >> 2))) & 3
        dz = (sign * ((other & 3) - (sub & 3))) & 3
        delta = dx * GRID + dz
        count = jnp.where(abroad, 1, table[delta])

        @pl.when(jnp.where(count == 1, 0, 1) == turn)
        def _():
            row = pair * LIST_WIDTH
            for kind in range(3):
                load_of = len(PLACES) * min(kind, 1)
                best_load = jnp.int32(1 << 20)
                best_code = jnp.int32(0)
                for k in range(most):
                    code = table[N_SUB + delta * most + k]
                    load = used[load_of + (code & 7)]
                    better = load < best_load
                    best_load = jnp.where(better, load, best_load)
                    best_code = jnp.where(better, code, best_code)
                at = jnp.where(abroad, 0, best_code & 7)
                used[load_of + at] = used[load_of + at] + 1
                chosen[row + 2 * kind] = at
                chosen[row + 2 * kind + 1] = jnp.where(
                    abroad, REGION_SOURCE, (best_code >> 3) & 7
                )
            first = (region * N_SUB + sub) * ORB_DEV + own_slot
            second_region = jnp.where(abroad, next_region, region)
            second = (second_region * N_SUB + other) * ORB_DEV + partner_slot
            chosen[row + 6] = own_slot
            chosen[row + 7] = partner_slot
            for c in range(3):
                chosen[row + 8 + c] = offsets[first * 3 + c] - offsets[second * 3 + c]
            for c in range(11, LIST_WIDTH):
                chosen[row + c] = 0

    for turn in range(2):
        for pair in range(PAIRS_DEV):
            place(pair, turn)


def three_dots(high, low, weights, index):
    boxes_high = jnp.concatenate([high, low], axis=0)
    half = high.shape[0]
    wide = jnp.dot(boxes_high, weights[0, index], preferred_element_type=F32)
    rest = jnp.dot(high, weights[1, index], preferred_element_type=F32)
    return wide[:half] + wide[half:] + rest


def split(value):
    high = value.astype(BF16)
    return high, (value - high.astype(F32)).astype(BF16)


def six_points(x):
    u = [x[r] + x[r + 3] for r in range(3)]
    v = [x[r] - x[r + 3] for r in range(3)]
    return (
        u[0] + u[1] + u[2],
        v[0] - v[1] + v[2],
        v[0] + 0.5 * (v[1] - v[2]),
        -HALF_ROOT3 * (v[1] + v[2]),
        u[0] - 0.5 * (u[1] + u[2]),
        -HALF_ROOT3 * (u[1] - u[2]),
    )


def six_points_back(t0, t3, t1r, t1i, t2r, t2i):
    a0 = t0 + t2r
    t2h = t0 - 0.5 * t2r
    t2s = HALF_ROOT3 * t2i
    a1 = t2h - t2s
    a2 = t2h + t2s
    t1s = HALF_ROOT3 * t1i
    b0 = t3 + t1r
    b1 = 0.5 * t1r - t3 - t1s
    b2 = t3 - 0.5 * t1r - t1s
    return a0 + b0, a1 + b1, a2 + b2, a0 - b0, a1 - b1, a2 - b2


def three_points(x):
    total = x[1] + x[2]
    return x[0] + total, x[0] - 0.5 * total, -HALF_ROOT3 * (x[1] - x[2])


def three_points_back(s0, s1r, s1i):
    low = s0 - 0.5 * s1r
    turned = HALF_ROOT3 * s1i
    return s0 + s1r, low - turned, low + turned


def solve(density, both, work, waves, waves_back, green, rows, boxes):
    for b in range(boxes):
        for g in range(BOX // 16):
            some = pl.ds(b * BOX + g * 16, 16)
            low_some = pl.ds((boxes + b) * BOX + g * 16, 16)
            columns = []
            for c in range(BLOCKS_Z):
                x = [density(b, pl.ds(g * 16, 16), r, c) for r in range(BLOCKS_Y)]
                columns.append(six_points(x))
            t = [three_points([columns[c][j] for c in range(BLOCKS_Z)]) for j in range(6)]
            parts = [t[0][0], t[1][0], t[0][1], t[0][2], t[1][1], t[1][2]]
            parts += [t[2][0], t[3][0], t[4][0], t[5][0]]
            for j in (2, 4):
                (_, rr, ri), (_, ir, ii) = t[j], t[j + 1]
                parts += [rr - ii, ri + ir, rr + ii, ir - ri]
            for i, part in enumerate(parts):
                high, low = split(part)
                both[some, pl.ds(i * 128, 128)] = high
                both[low_some, pl.ds(i * 128, 128)] = low

    def row_pass(value):
        high, low = split(value)
        stacked = jnp.concatenate([high, high, low], axis=0)
        return jnp.dot(rows[...], stacked, preferred_element_type=F32)

    def plane_pass(weights):
        for group in range(9):
            lanes = pl.ds(group * 256, 256)
            high = both[pl.ds(0, boxes * BOX), lanes]
            low = both[pl.ds(boxes * BOX, boxes * BOX), lanes]
            work[:, lanes] = three_dots(high, low, weights, group)

    places = [
        (pl.ds(b * BOX, BOX), pl.ds((boxes + b) * BOX, BOX), pl.ds(group * 256, 256))
        for b in range(boxes)
        for group in range(9)
    ]
    plane_pass(waves)
    for some, _, lanes in places:
        work[some, lanes] = row_pass(work[some, lanes]) * green[:, lanes]
    for some, low_some, lanes in places:
        both[some, lanes], both[low_some, lanes] = split(row_pass(work[some, lanes]))
    plane_pass(waves_back)

    for b in range(boxes):
        for g in range(BOX // 16):
            some = pl.ds(b * BOX + g * 16, 16)
            p = [work[some, pl.ds(i * 128, 128)] for i in range(18)]
            t = [[p[0], p[2], p[3]], [p[1], p[4], p[5]]]
            for j in range(2):
                pr, pi, mr, mi = p[10 + 4 * j : 14 + 4 * j]
                t.append([p[6 + 2 * j], pr + mr, pi - mi])
                t.append([p[7 + 2 * j], pi + mi, mr - pr])
            t = [three_points_back(*parts) for parts in t]
            for c in range(BLOCKS_Z):
                values = six_points_back(*[t[j][c] for j in range(6)])
                for r, value in enumerate(values):
                    work[some, pl.ds((r * BLOCKS_Z + c) * 128, 128)] = value


def rounded(value):
    return value.astype(BF16).astype(F32)


def shift_box(padded, value, put, dx, dy, dz):
    for r in range(BLOCKS_Y):
        for c in range(BLOCKS_Z):
            at = ((r + SIDE_Y) * WIDE_Z + c + SIDE_Z) * ROWS_PADDED + MARGIN
            padded[pl.ds(at, BOX), :] = value(pl.ds((r * BLOCKS_Z + c) * 128, 128))
    fine_y, fine_z = dy & 7, dz & 15
    start = ((dy >> 3) + SIDE_Y) * WIDE_Z + (dz >> 4) + SIDE_Z
    base = start * ROWS_PADDED + MARGIN + dx
    lane = lax.broadcasted_iota(jnp.int32, (1, 128), 1)
    next_y = (lane >> 4) < fine_y
    next_z = (lane & 15) < fine_z
    carried = (lane & 15) + fine_z >= 16
    ahead = fine_y * 16 + fine_z
    turn = (128 - ahead) & 127
    turn_carried = (128 + 16 - ahead) & 127

    def block(r, c):
        return padded[pl.ds(base + (r * WIDE_Z + c) * ROWS_PADDED, BOX), :]

    for r in range(BLOCKS_Y):
        mixed = [jnp.where(next_y, block(r + 1, c), block(r, c)) for c in range(BLOCKS_Z + 1)]
        for c in range(BLOCKS_Z):
            source = jnp.where(next_z, mixed[c + 1], mixed[c])
            out = jnp.where(
                carried, pltpu.roll(source, turn_carried, 1), pltpu.roll(source, turn, 1)
            )
            put(pl.ds((r * BLOCKS_Z + c) * 128, 128), out)


def exchange_kernel(part, *refs):
    second = part > 0
    sets = 2 if second else 1
    carried = N_OUT if part == 2 else 0
    n_in = sets * (SOURCES + 1)
    listing, *refs = refs
    boxes_in, refs = refs[:n_in], refs[n_in:]
    tables_in, refs = refs[:N_TABLES], refs[N_TABLES:]
    sums_in, refs = refs[:carried], refs[carried:]
    outs, refs = refs[:N_OUT], refs[N_OUT:]
    tables, refs = refs[:N_TABLES], refs[N_TABLES:]
    acc, stage, held, theirs, both, work, padded, mine, sems, table_sems, out_sems = refs

    mine[0] = 0
    for home in range(len(PLACES)):

        def check(pair, carry, home=home):
            row = (home * PAIRS_DEV + pair) * LIST_WIDTH
            for kind in (1, 2) if second else (0,):

                @pl.when(listing[row + 2 * kind] == home)
                def _(kind=kind):
                    at = mine[0]
                    mine[0] = at + 1
                    task = (at + 1) * TASK_WIDTH
                    mine[task] = home
                    mine[task + 1] = listing[row + 2 * kind + 1]
                    for c in range(5):
                        mine[task + 2 + c] = listing[row + 6 + c]
                    mine[task + 7] = kind

            return carry

        lax.fori_loop(0, PAIRS_DEV, check, 0)

    count = mine[0]
    steps = (count + 1) >> 1
    half = (steps + 1) >> 1
    begin = half if part == 2 else 0
    end = half if part == 1 else steps

    def table_copies():
        return [
            pltpu.make_async_copy(tables_in[i], tables[i], table_sems.at[i])
            for i in range(N_TABLES)
        ]

    def fetch(group, source, slot, target, sem):
        refs_of = boxes_in[group * (SOURCES + 1) : (group + 1) * (SOURCES + 1)]

        def start(ref, row):
            row = pl.multiple_of(row, 16)
            pltpu.make_async_copy(ref.at[pl.ds(row, BOX)], target, sem).start()

        for s in range(SOURCES):
            if s == 3:
                for part_of in range(2):

                    @pl.when((source == s) & ((slot >> 1) == part_of))
                    def _(part_of=part_of):
                        start(refs_of[3 + part_of], (slot & 1) * BOX)
            else:
                at = s if s < 3 else s + 1

                @pl.when(source == s)
                def _(at=at):
                    start(refs_of[at], slot * BOX)

    def each_load(step, act):
        for i in range(2):
            task = (step * 2 + i + 1) * TASK_WIDTH

            @pl.when(step * 2 + i < count)
            def _(i=i, task=task):
                kind = mine[task + 7]
                act(kind == 1, mine[task], mine[task + 2], 2 * i)
                act(kind == 2, mine[task + 1], mine[task + 3], 2 * i + 1)

    def start_loads(step, buffer):
        def act(of_trial, source, slot, i):
            if second:

                @pl.when(of_trial)
                def _():
                    fetch(1, source, slot, held.at[buffer, i], sems.at[buffer, i])

                @pl.when(jnp.logical_not(of_trial))
                def _():
                    fetch(0, source, slot, held.at[buffer, i], sems.at[buffer, i])
            else:
                fetch(0, source, slot, held.at[buffer, i], sems.at[buffer, i])

        each_load(step, act)

    def wait_loads(step, buffer):
        def act(of_trial, source, slot, i):
            pltpu.make_async_copy(
                boxes_in[0].at[pl.ds(0, BOX)], held.at[buffer, i], sems.at[buffer, i]
            ).wait()

        each_load(step, act)

    def sum_copies(into):
        copies = []
        for i, size in enumerate(SIZES):
            low = sum(SIZES[:i]) * BOX
            vmem = (acc if i == 0 else stage).at[pl.ds(low, size * BOX)]
            if into:
                copies.append(pltpu.make_async_copy(sums_in[i], vmem, out_sems.at[i]))
            else:
                copies.append(pltpu.make_async_copy(vmem, outs[i], out_sems.at[i]))
        return copies

    @pl.when(begin < end)
    def _():
        start_loads(begin, begin & 1)
        for copy in table_copies():
            copy.start()

    if carried:
        for copy in sum_copies(True):
            copy.start()
    padded[...] = jnp.zeros(padded.shape, F32)

    def box_rows(i):
        return pl.ds(pl.multiple_of(i * BOX, BOX), BOX)

    if carried:
        for copy in sum_copies(True):
            copy.wait()

    def prepare(i, carry):
        if carried:
            acc[box_rows(i), :] = stage[box_rows(i), :].astype(F32)
        else:
            acc[box_rows(i), :] = jnp.zeros((BOX, PLANE), F32)
        return carry

    lax.fori_loop(ORB_DEV if carried else 0, SOURCES * ORB_DEV, prepare, 0)

    def add(source, slot, lanes, value):
        at = box_rows(source * ORB_DEV + slot)
        acc[at, lanes] = acc[at, lanes] + value

    def one_step(step, carry):
        buffer = step & 1

        @pl.when(step + 1 < end)
        def _():
            start_loads(step + 1, 1 - buffer)

        wait_loads(step, buffer)
        for i in range(2):
            task = (step * 2 + i + 1) * TASK_WIDTH

            @pl.when(step * 2 + i < count)
            def _(i=i, task=task):
                def value(lanes):
                    return held[buffer, 2 * i + 1, :, lanes].astype(F32)

                def put(lanes, block):
                    theirs[i, :, lanes] = block

                shift_box(padded, value, put, mine[task + 4], mine[task + 5], mine[task + 6])

        @pl.when(step == begin)
        def _():
            for copy in table_copies():
                copy.wait()

        def density(b, some, r, c):
            lanes = pl.ds((r * BLOCKS_Z + c) * 128, 128)
            return held[buffer, 2 * b, some, lanes].astype(F32) * theirs[b, some, lanes]

        solve(density, both, work, *tables, 2)
        for i in range(2):
            task = (step * 2 + i + 1) * TASK_WIDTH
            there = step * 2 + i < count
            kind = mine[task + 7]

            @pl.when(there & (kind != 2))
            def _(i=i, task=task):
                near = rounded(work[pl.ds(i * BOX, BOX), :] * theirs[i])
                add(mine[task], mine[task + 2], pl.ds(0, PLANE), near)

            @pl.when(there & (kind != 1))
            def _(i=i, task=task):
                def value(lanes):
                    mine_box = held[buffer, 2 * i, :, lanes].astype(F32)
                    return rounded(work[pl.ds(i * BOX, BOX), lanes] * mine_box)

                def put(lanes, block):
                    add(mine[task + 1], mine[task + 3], lanes, block)

                shift_box(padded, value, put, -mine[task + 4], -mine[task + 5], -mine[task + 6])

        return carry

    lax.fori_loop(begin, end, one_step, 0)

    copies = sum_copies(False)
    copies[0].start()
    at = ORB_DEV
    for copy, size in zip(copies[1:], SIZES[1:]):

        def put(i, carry):
            stage[box_rows(i), :] = acc[box_rows(i), :].astype(BF16)
            return carry

        lax.fori_loop(at, at + size, put, 0)
        copy.start()
        at += size
    for copy in copies:
        copy.wait()


def exchange(part, listing, boxes, tables, sums=()):
    any_space = pl.BlockSpec(memory_space=pl.ANY)
    smem = pl.BlockSpec(memory_space=pltpu.SMEM)
    outs = [
        jax.ShapeDtypeStruct((size * BOX, PLANE), F32 if i == 0 else BF16)
        for i, size in enumerate(SIZES)
    ]

    def kernel(*refs):
        exchange_kernel(part, *refs)

    return pl.pallas_call(
        kernel,
        out_shape=outs,
        in_specs=[smem] + [any_space] * (len(boxes) + len(tables) + len(sums)),
        out_specs=[any_space] * len(outs),
        scratch_shapes=[
            *[pltpu.VMEM(t.shape, t.dtype) for t in tables],
            pltpu.VMEM((SOURCES * ORB_DEV * BOX, PLANE), F32),
            pltpu.VMEM((SOURCES * ORB_DEV * BOX, PLANE), BF16),
            pltpu.VMEM((2, 4, BOX, PLANE), BF16),
            pltpu.VMEM((2, BOX, PLANE), F32),
            pltpu.VMEM((4 * BOX, PLANE), BF16),
            pltpu.VMEM((2 * BOX, PLANE), F32),
            pltpu.VMEM((WIDE_Y * WIDE_Z * ROWS_PADDED, 128), F32),
            pltpu.SMEM(((MAX_TASKS + 3) * TASK_WIDTH,), jnp.int32),
            pltpu.SemaphoreType.DMA((2, 4)),
            pltpu.SemaphoreType.DMA((N_TABLES,)),
            pltpu.SemaphoreType.DMA((N_OUT,)),
        ],
        compiler_params=pltpu.CompilerParams(vmem_limit_bytes=56 * 1024 * 1024),
        cost_estimate=pl.CostEstimate(
            flops=10_000_000_000, bytes_accessed=30_000_000, transcendentals=0
        ),
        name=("first_application", "second_early", "second_late")[part],
    )(listing, *boxes, *tables, *sums)


def reorder_kernel(box, order, out):
    for r in range(BLOCKS_Y):
        lanes = pl.ds(r * CHUNK, CHUNK)
        moved = jnp.dot(box[:, lanes], order[...], preferred_element_type=F32)
        out[:, lanes] = moved.astype(BF16)


def reorder(boxes, order):
    rows = boxes.shape[0]
    whole = pl.BlockSpec((CHUNK, CHUNK), lambda i: (0, 0))
    some = pl.BlockSpec((rows // 2, PLANE), lambda i: (i, 0))
    return pl.pallas_call(
        reorder_kernel,
        grid=(2,),
        out_shape=jax.ShapeDtypeStruct((rows, PLANE), BF16),
        in_specs=[some, whole],
        out_specs=some,
        name="reorder",
    )(boxes, order)


def total_kernel(own, abroad, first, second, order, out):
    for r in range(BLOCKS_Y):
        lanes = pl.ds(r * CHUNK, CHUNK)
        result = own[:, lanes] + abroad[:, lanes].astype(F32)
        result += first[:, lanes].astype(F32) + second[:, lanes].astype(F32)
        moved = jnp.dot((-result).astype(BF16), order[...], preferred_element_type=F32)
        out[:, lanes] = moved.astype(BF16)


def total(own, abroad, first, second, order):
    rows = own.shape[0]
    whole = pl.BlockSpec((CHUNK, CHUNK), lambda i: (0, 0))
    some = pl.BlockSpec((rows // 2, PLANE), lambda i: (i, 0))
    return pl.pallas_call(
        total_kernel,
        grid=(2,),
        out_shape=jax.ShapeDtypeStruct((rows, PLANE), BF16),
        in_specs=[some] * 4 + [whole],
        out_specs=some,
        name="total",
    )(own, abroad, first, second, order)


def moves(n_region):
    def step(dx, dz):
        pairs = []
        for region in range(n_region):
            sign = 1 - 2 * (region % 2)
            for x in range(GRID):
                for z in range(GRID):
                    to = (x + sign * dx) % GRID * GRID + (z + sign * dz) % GRID
                    pairs.append((region * N_SUB + x * GRID + z, region * N_SUB + to))

        def move(block):
            return lax.ppermute(block, ("region", "sub"), pairs)

        return move

    def across(distance):
        pairs = [(i, (i + distance) % n_region) for i in range(n_region)]

        def move(block):
            return lax.ppermute(block, "region", pairs)

        return move

    return step, across


def per_device(orbitals, trial_set, own_slot, partner_route, partner_slot, offsets):
    n_region = lax.axis_size("region")
    region = lax.axis_index("region")
    sub = lax.axis_index("sub")
    step, across = moves(n_region)
    tables = transform_tables()
    tables = [
        jnp.asarray(tables[k])
        for k in TABLES
    ]
    order, order_back = jnp.asarray(order_table()), jnp.asarray(order_table().T.copy())
    table, most = meeting_table()
    meta = jnp.concatenate([own_slot, partner_route[:, 0], partner_slot])
    where = jnp.stack([region, sub, jnp.int32(n_region)]).astype(jnp.int32)
    smem = pl.BlockSpec(memory_space=pltpu.SMEM)

    def planner(*refs):
        plan_kernel(most, *refs)

    chosen = pl.pallas_call(
        planner,
        out_shape=jax.ShapeDtypeStruct((LISTED,), jnp.int32),
        in_specs=[smem] * 4,
        out_specs=smem,
        scratch_shapes=[pltpu.SMEM((2 * len(PLACES),), jnp.int32)],
        name="plan",
    )(where, meta, offsets.reshape(-1), jnp.asarray(table))

    def near_places(boxes):
        return step(0, 1)(boxes), step(1, 0)(boxes), across(-1)(boxes)

    def cut(b01, b10):
        return b01[: 2 * BOX], b10[2 * BOX :]

    def far_places(b01, b10, halves):
        low, high = halves
        return step(1, 0)(low), step(0, 1)(high), step(0, -1)(b10), step(-1, 0)(b01)

    def begin_back(parts):
        own, c01, c10, c11_low, c11_high, c13, c31, c_abroad = parts
        return (
            step(0, 1)(c13),
            step(1, 0)(c31),
            step(-1, 0)(c11_low),
            step(0, -1)(c11_high),
            across(1)(c_abroad),
        )

    def merge(parts, arrived):
        r13, r31, r11_low, r11_high, _ = arrived
        none = jnp.zeros_like(r11_low)
        low = jnp.concatenate([r11_low, none])
        high = jnp.concatenate([none, r11_high])
        m01 = (parts[1].astype(F32) + r31.astype(F32) + low.astype(F32)).astype(BF16)
        m10 = (parts[2].astype(F32) + r13.astype(F32) + high.astype(F32)).astype(BF16)
        return step(0, -1)(m01), step(-1, 0)(m10)

    def finish(parts, arrived, merged):
        result = total(parts[0], arrived[4], *merged, order_back)
        return result.reshape(ORB_DEV, BOX, PLANE)

    ordered = lax.optimization_barrier
    notes = jnp.pad(chosen.astype(BF16)[None], ((0, NOTE_ROWS - 1), (0, PLANE - LISTED)))
    boxes = reorder(orbitals.reshape(ORB_DEV * BOX, PLANE), order)
    trials = reorder(trial_set.reshape(ORB_DEV * BOX, PLANE), order)
    boxes = jnp.concatenate([boxes, notes])
    t01, t10, t_abroad = near_places(trials)
    boxes, t01, t10, t_abroad = ordered((boxes, t01, t10, t_abroad))
    t_cut = cut(t01, t10)
    o01, o10, o_abroad = near_places(boxes)
    o01, o10, o_abroad, t_cut = ordered((o01, o10, o_abroad, t_cut))
    o_far = far_places(o01, o10, cut(o01, o10))
    t01, t10, t_cut, o_far = ordered((t01, t10, t_cut, o_far))
    t_far = far_places(t01, t10, t_cut)
    orbital_boxes = [boxes, o01, o10, *o_far, o_abroad]
    notes = [boxes, o01, o10, o_far[1], o_far[2], o_far[3]]
    listing = jnp.concatenate([n[-NOTE_ROWS, :LISTED] for n in notes]).astype(jnp.int32)
    first = exchange(0, listing, orbital_boxes, tables)
    arrived_first = begin_back(first)
    first, listing, t_far = ordered((first, listing, t_far))
    all_boxes = orbital_boxes + [trials, t01, t10, *t_far, t_abroad]
    early = exchange(1, listing, all_boxes, tables)
    early, first, arrived_first = ordered((early, first, arrived_first))
    merged_first = merge(first, arrived_first)
    late = exchange(2, listing, all_boxes, tables, early)
    late, merged_first = ordered((late, merged_first))
    result_first = finish(first, arrived_first, merged_first)
    arrived_late = begin_back(late)
    result_second = finish(late, arrived_late, merge(late, arrived_late))
    return result_first, result_second


def solution(mesh):
    in_specs = (
        P(("region", "sub"), None, None),
        P(("region", "sub"), None, None),
        P(("region", "sub")),
        P(("region", "sub"), None),
        P(("region", "sub")),
        P(),
    )
    out_specs = (P(("region", "sub"), None, None), P(("region", "sub"), None, None))
    return jax.shard_map(
        per_device, mesh=mesh, in_specs=in_specs, out_specs=out_specs, check_vma=False
    )
```

```python
import math

import jax
import jax.numpy as jnp
import ml_dtypes
import numpy as np
from jax import lax
from jax.experimental import pallas as pl
from jax.experimental.pallas import tpu as pltpu
from jax.sharding import PartitionSpec as P

BOX = 48
PLANE = BOX * BOX
CHUNK = PLANE // 6
SCREEN = 0.5
GRID = 4
N_SUB = GRID * GRID
ORB_DEV = 4
PAIRS_DEV = 4
N_PAIRS = N_SUB * PAIRS_DEV

PLACES = ((0, 0), (0, 1), (1, 0), (1, 1), (1, 3), (3, 1))
REGION_SOURCE = len(PLACES)
SOURCES = len(PLACES) + 1
LIST_WIDTH = 16
TASK_WIDTH = 8
LISTED = PAIRS_DEV * LIST_WIDTH
NOTE = 1024
SIZES = (4, 4, 4, 2, 2, 4, 4, 4)
N_OUT = len(SIZES)
N_TABLES = 4
BLOCKS_Y = 6
BLOCKS_Z = 3
MARGIN = 24
ROWS_PADDED = BOX + 2 * MARGIN
SIDE_Y = 3
SIDE_Z = 2
WIDE_Y = BLOCKS_Y + 2 * SIDE_Y
WIDE_Z = BLOCKS_Z + 2 * SIDE_Z
MAX_TASKS = 2 * len(PLACES) * PAIRS_DEV
HALF_ROOT3 = math.sqrt(3.0) / 2.0
F32 = jnp.float32
BF16 = jnp.bfloat16


def meeting_table():
    found = [[] for _ in range(N_SUB)]
    for i, (ax, az) in enumerate(PLACES):
        for j, (bx, bz) in enumerate(PLACES):
            delta = (ax - bx) % GRID * GRID + (az - bz) % GRID
            found[delta].append(i + 8 * j)
    most = max(len(f) for f in found)
    codes = np.array([f + [f[-1]] * (most - len(f)) for f in found], np.int32)
    counts = np.array([len(f) for f in found], np.int32)
    return np.concatenate([counts, codes.reshape(-1)]), most


def high_low(matrix):
    high = matrix.astype(ml_dtypes.bfloat16)
    low = (matrix - high.astype(np.float64)).astype(ml_dtypes.bfloat16)
    return np.stack([high, low])


def cas(angles):
    return np.cos(angles) + np.sin(angles)


def transform_tables():
    turn = 2.0 * math.pi / BOX
    n = np.arange(BOX)
    line = cas(turn * (n[:, None] * n[None, :] % BOX))
    q, w = np.arange(8), np.arange(16)

    def angle_y(j):
        return turn * (q[:, None] * (6 * q[None, :] + j) % BOX)

    def angle_z(j):
        return turn * (w[:, None] * (3 * w[None, :] + j) % BOX)

    def both_parts(angle):
        c, s = np.cos(angle), np.sin(angle)
        return np.block([[c, -s], [s, c]])

    def planes(y, z, sign):
        whole = angle_y(y)[:, None, :, None] + sign * angle_z(z)[None, :, None, :]
        return both_parts(whole.reshape(128, 128))

    def real_complex(y):
        z = both_parts(angle_z(1)).reshape(2, 16, 2, 16)
        return np.einsum("qm,awbn->aqwbmn", cas(angle_y(y)), z).reshape(256, 256)

    def complex_real(y):
        return np.kron(both_parts(angle_y(y)), cas(angle_z(0)))

    zero = np.zeros((128, 128))
    real = [np.kron(cas(angle_y(y)), cas(angle_z(0))) for y in (0, 3)]
    waves = [np.block([[real[0], zero], [zero, real[1]]]), real_complex(0), real_complex(3)]
    waves += [complex_real(1), complex_real(2)]
    for y in (1, 2):
        waves += [planes(y, 1, 1), planes(y, 1, -1)]
    waves = np.stack(waves)
    lam = 4.0 * np.sin(math.pi * n / BOX) ** 2

    def spectrum(y, z, weight):
        ky, kz = 6 * q + y, 3 * w + z
        total = lam[:, None, None] + lam[ky][None, :, None] + lam[kz][None, None, :] + SCREEN
        return (weight * 4.0 * math.pi / total / float(BOX**3)).reshape(BOX, 128)

    order = [(0, 0, 1.0), (3, 0, 1.0)]
    for y, z in ((0, 1), (3, 1), (1, 0), (2, 0), (1, 1), (1, 1), (2, 1), (2, 1)):
        order += [(y, z, 2.0)] * 2
    green = np.concatenate([spectrum(*o) for o in order], axis=1)
    rows = high_low(line)
    rows = np.concatenate([rows[0], rows[1], rows[0]], axis=1)
    return dict(
        waves=high_low(waves),
        waves_back=high_low(waves.transpose(0, 2, 1)),
        green=green.astype(np.float32),
        rows=rows,
    )


TABLES = ("waves", "waves_back", "green", "rows")


def order_table():
    lane = np.arange(8 * BOX)
    q, c, w = lane // BOX, lane % BOX // 16, lane % 16
    table = np.zeros((8 * BOX, 8 * BOX), np.float32)
    table[lane, c * 128 + q * 16 + w] = 1.0
    return table.astype(ml_dtypes.bfloat16)


def plan_kernel(most, where, meta, offsets, table, chosen, used):
    region, sub, n_region = where[0], where[1], where[2]
    sign = 1 - 2 * (region & 1)
    next_region = jnp.where(region + 1 == n_region, 0, region + 1)
    for i in range(2 * len(PLACES)):
        used[i] = 0

    def place(pair, turn):
        own_slot = meta[pair]
        route = meta[PAIRS_DEV + pair]
        partner_slot = meta[2 * PAIRS_DEV + pair]
        abroad = route == N_SUB
        other = jnp.where(abroad, sub, route)
        dx = (sign * ((other >> 2) - (sub >> 2))) & 3
        dz = (sign * ((other & 3) - (sub & 3))) & 3
        delta = dx * GRID + dz
        count = jnp.where(abroad, 1, table[delta])

        @pl.when(jnp.where(count == 1, 0, 1) == turn)
        def _():
            row = pair * LIST_WIDTH
            for kind in range(3):
                load_of = len(PLACES) * min(kind, 1)
                best_load = jnp.int32(1 << 20)
                best_code = jnp.int32(0)
                for k in range(most):
                    code = table[N_SUB + delta * most + k]
                    load = used[load_of + (code & 7)]
                    better = load < best_load
                    best_load = jnp.where(better, load, best_load)
                    best_code = jnp.where(better, code, best_code)
                at = jnp.where(abroad, 0, best_code & 7)
                used[load_of + at] = used[load_of + at] + 1
                chosen[row + 2 * kind] = at
                chosen[row + 2 * kind + 1] = jnp.where(
                    abroad, REGION_SOURCE, (best_code >> 3) & 7
                )
            first = (region * N_SUB + sub) * ORB_DEV + own_slot
            second_region = jnp.where(abroad, next_region, region)
            second = (second_region * N_SUB + other) * ORB_DEV + partner_slot
            chosen[row + 6] = own_slot
            chosen[row + 7] = partner_slot
            for c in range(3):
                chosen[row + 8 + c] = offsets[first * 3 + c] - offsets[second * 3 + c]
            for c in range(11, LIST_WIDTH):
                chosen[row + c] = 0

    for turn in range(2):
        for pair in range(PAIRS_DEV):
            place(pair, turn)


def three_dots(high, low, weights, index):
    boxes_high = jnp.concatenate([high, low], axis=0)
    half = high.shape[0]
    wide = jnp.dot(boxes_high, weights[0, index], preferred_element_type=F32)
    rest = jnp.dot(high, weights[1, index], preferred_element_type=F32)
    return wide[:half] + wide[half:] + rest


def split(value):
    high = value.astype(BF16)
    return high, (value - high.astype(F32)).astype(BF16)


def six_points(x):
    u = [x[r] + x[r + 3] for r in range(3)]
    v = [x[r] - x[r + 3] for r in range(3)]
    return (
        u[0] + u[1] + u[2],
        v[0] - v[1] + v[2],
        v[0] + 0.5 * (v[1] - v[2]),
        -HALF_ROOT3 * (v[1] + v[2]),
        u[0] - 0.5 * (u[1] + u[2]),
        -HALF_ROOT3 * (u[1] - u[2]),
    )


def six_points_back(t0, t3, t1r, t1i, t2r, t2i):
    a0 = t0 + t2r
    t2h = t0 - 0.5 * t2r
    t2s = HALF_ROOT3 * t2i
    a1 = t2h - t2s
    a2 = t2h + t2s
    t1s = HALF_ROOT3 * t1i
    b0 = t3 + t1r
    b1 = 0.5 * t1r - t3 - t1s
    b2 = t3 - 0.5 * t1r - t1s
    return a0 + b0, a1 + b1, a2 + b2, a0 - b0, a1 - b1, a2 - b2


def three_points(x):
    total = x[1] + x[2]
    return x[0] + total, x[0] - 0.5 * total, -HALF_ROOT3 * (x[1] - x[2])


def three_points_back(s0, s1r, s1i):
    low = s0 - 0.5 * s1r
    turned = HALF_ROOT3 * s1i
    return s0 + s1r, low - turned, low + turned


def solve(density, both, work, waves, waves_back, green, rows, boxes):
    for b in range(boxes):
        for g in range(BOX // 16):
            some = pl.ds(b * BOX + g * 16, 16)
            low_some = pl.ds((boxes + b) * BOX + g * 16, 16)
            columns = []
            for c in range(BLOCKS_Z):
                x = [density(b, pl.ds(g * 16, 16), r, c) for r in range(BLOCKS_Y)]
                columns.append(six_points(x))
            t = [three_points([columns[c][j] for c in range(BLOCKS_Z)]) for j in range(6)]
            parts = [t[0][0], t[1][0], t[0][1], t[0][2], t[1][1], t[1][2]]
            parts += [t[2][0], t[3][0], t[4][0], t[5][0]]
            for j in (2, 4):
                (_, rr, ri), (_, ir, ii) = t[j], t[j + 1]
                parts += [rr - ii, ri + ir, rr + ii, ir - ri]
            for i, part in enumerate(parts):
                high, low = split(part)
                both[some, pl.ds(i * 128, 128)] = high
                both[low_some, pl.ds(i * 128, 128)] = low

    def row_pass(value):
        high, low = split(value)
        stacked = jnp.concatenate([high, high, low], axis=0)
        return jnp.dot(rows[...], stacked, preferred_element_type=F32)

    def plane_pass(weights):
        for group in range(9):
            lanes = pl.ds(group * 256, 256)
            high = both[pl.ds(0, boxes * BOX), lanes]
            low = both[pl.ds(boxes * BOX, boxes * BOX), lanes]
            work[:, lanes] = three_dots(high, low, weights, group)

    places = [
        (pl.ds(b * BOX, BOX), pl.ds((boxes + b) * BOX, BOX), pl.ds(group * 256, 256))
        for b in range(boxes)
        for group in range(9)
    ]
    plane_pass(waves)
    for some, _, lanes in places:
        work[some, lanes] = row_pass(work[some, lanes]) * green[:, lanes]
    for some, low_some, lanes in places:
        both[some, lanes], both[low_some, lanes] = split(row_pass(work[some, lanes]))
    plane_pass(waves_back)

    for b in range(boxes):
        for g in range(BOX // 16):
            some = pl.ds(b * BOX + g * 16, 16)
            p = [work[some, pl.ds(i * 128, 128)] for i in range(18)]
            t = [[p[0], p[2], p[3]], [p[1], p[4], p[5]]]
            for j in range(2):
                pr, pi, mr, mi = p[10 + 4 * j : 14 + 4 * j]
                t.append([p[6 + 2 * j], pr + mr, pi - mi])
                t.append([p[7 + 2 * j], pi + mi, mr - pr])
            t = [three_points_back(*parts) for parts in t]
            for c in range(BLOCKS_Z):
                values = six_points_back(*[t[j][c] for j in range(6)])
                for r, value in enumerate(values):
                    work[some, pl.ds((r * BLOCKS_Z + c) * 128, 128)] = value


def rounded(value):
    return value.astype(BF16).astype(F32)


def shift_box(padded, value, put, dx, dy, dz):
    for r in range(BLOCKS_Y):
        for c in range(BLOCKS_Z):
            at = ((r + SIDE_Y) * WIDE_Z + c + SIDE_Z) * ROWS_PADDED + MARGIN
            padded[pl.ds(at, BOX), :] = value(pl.ds((r * BLOCKS_Z + c) * 128, 128))
    fine_y, fine_z = dy & 7, dz & 15
    start = ((dy >> 3) + SIDE_Y) * WIDE_Z + (dz >> 4) + SIDE_Z
    base = start * ROWS_PADDED + MARGIN + dx
    lane = lax.broadcasted_iota(jnp.int32, (1, 128), 1)
    next_y = (lane >> 4) < fine_y
    next_z = (lane & 15) < fine_z
    carried = (lane & 15) + fine_z >= 16
    ahead = fine_y * 16 + fine_z
    turn = (128 - ahead) & 127
    turn_carried = (128 + 16 - ahead) & 127

    def block(r, c):
        return padded[pl.ds(base + (r * WIDE_Z + c) * ROWS_PADDED, BOX), :]

    for r in range(BLOCKS_Y):
        mixed = [jnp.where(next_y, block(r + 1, c), block(r, c)) for c in range(BLOCKS_Z + 1)]
        for c in range(BLOCKS_Z):
            source = jnp.where(next_z, mixed[c + 1], mixed[c])
            out = jnp.where(
                carried, pltpu.roll(source, turn_carried, 1), pltpu.roll(source, turn, 1)
            )
            put(pl.ds((r * BLOCKS_Z + c) * 128, 128), out)


def exchange_kernel(part, *refs):
    second = part > 0
    sets = 2 if second else 1
    carried = N_OUT if part == 2 else 0
    n_in = sets * (SOURCES + 1)
    listing, *refs = refs
    boxes_in, refs = refs[:n_in], refs[n_in:]
    tables_in, refs = refs[:N_TABLES], refs[N_TABLES:]
    sums_in, refs = refs[:carried], refs[carried:]
    outs, refs = refs[:N_OUT], refs[N_OUT:]
    tables, refs = refs[:N_TABLES], refs[N_TABLES:]
    acc, stage, nothing, held, theirs, both, work, padded, *refs = refs
    mine, touched, sems, table_sems, out_sems = refs

    mine[0] = 0
    for home in range(len(PLACES)):

        def check(pair, carry, home=home):
            row = (home * PAIRS_DEV + pair) * LIST_WIDTH
            for kind in (1, 2) if second else (0,):

                @pl.when(listing[row + 2 * kind] == home)
                def _(kind=kind):
                    at = mine[0]
                    mine[0] = at + 1
                    task = (at + 1) * TASK_WIDTH
                    mine[task] = home
                    mine[task + 1] = listing[row + 2 * kind + 1]
                    for c in range(5):
                        mine[task + 2 + c] = listing[row + 6 + c]
                    mine[task + 7] = kind

            return carry

        lax.fori_loop(0, PAIRS_DEV, check, 0)

    count = mine[0]
    steps = (count + 1) >> 1
    half = (steps + 1) >> 1
    begin = half if part == 2 else 0
    end = half if part == 1 else steps

    def table_copies():
        return [
            pltpu.make_async_copy(tables_in[i], tables[i], table_sems.at[i])
            for i in range(N_TABLES)
        ]

    def fetch(group, source, slot, target, sem):
        refs_of = boxes_in[group * (SOURCES + 1) : (group + 1) * (SOURCES + 1)]

        def start(ref, row):
            row = pl.multiple_of(row, 16)
            pltpu.make_async_copy(ref.at[pl.ds(row, BOX)], target, sem).start()

        for s in range(SOURCES):
            if s == 3:
                for part_of in range(2):

                    @pl.when((source == s) & ((slot >> 1) == part_of))
                    def _(part_of=part_of):
                        start(refs_of[3 + part_of], (slot & 1) * BOX)
            else:
                at = s if s < 3 else s + 1

                @pl.when(source == s)
                def _(at=at):
                    start(refs_of[at], slot * BOX)

    def each_load(step, act):
        for i in range(2):
            task = (step * 2 + i + 1) * TASK_WIDTH

            @pl.when(step * 2 + i < count)
            def _(i=i, task=task):
                kind = mine[task + 7]
                act(kind == 1, mine[task], mine[task + 2], 2 * i)
                act(kind == 2, mine[task + 1], mine[task + 3], 2 * i + 1)

    def start_loads(step, buffer):
        def act(of_trial, source, slot, i):
            if second:

                @pl.when(of_trial)
                def _():
                    fetch(1, source, slot, held.at[buffer, i], sems.at[buffer, i])

                @pl.when(jnp.logical_not(of_trial))
                def _():
                    fetch(0, source, slot, held.at[buffer, i], sems.at[buffer, i])
            else:
                fetch(0, source, slot, held.at[buffer, i], sems.at[buffer, i])

        each_load(step, act)

    def wait_loads(step, buffer):
        def act(of_trial, source, slot, i):
            pltpu.make_async_copy(
                boxes_in[0].at[pl.ds(0, BOX)], held.at[buffer, i], sems.at[buffer, i]
            ).wait()

        each_load(step, act)

    def box_rows(i):
        return pl.ds(pl.multiple_of(i * BOX, BOX), BOX)

    n_slots = SOURCES * ORB_DEV
    for i in range(n_slots):
        touched[i] = 0

    def mark(i, carry):
        task = (i + 1) * TASK_WIDTH
        kind = mine[task + 7]

        @pl.when(kind != 2)
        def _():
            touched[mine[task] * ORB_DEV + mine[task + 2]] = 1

        @pl.when(kind != 1)
        def _():
            touched[mine[task + 1] * ORB_DEV + mine[task + 3]] = 1

        return carry

    lax.fori_loop(2 * begin, jnp.minimum(2 * end, count), mark, 0)

    places = []
    for i, size in enumerate(SIZES):
        for k in range(size):
            places.append((sum(SIZES[:i]) + k, i, pl.ds(k * BOX, BOX)))
    places = places[ORB_DEV:]

    def keep(slot, i, some):
        source = sums_in[i].at[some] if carried else nothing
        return pltpu.make_async_copy(source, outs[i].at[some], out_sems.at[slot])

    def take(slot, i, some):
        return pltpu.make_async_copy(sums_in[i].at[some], stage.at[box_rows(slot)], out_sems.at[slot])

    def send(slot, i, some):
        return pltpu.make_async_copy(stage.at[box_rows(slot)], outs[i].at[some], out_sems.at[slot])

    own_rows = pl.ds(0, ORB_DEV * BOX)

    @pl.when(begin < end)
    def _():
        start_loads(begin, begin & 1)
        for copy in table_copies():
            copy.start()

    if carried:
        pltpu.make_async_copy(sums_in[0], acc.at[own_rows], out_sems.at[0]).start()
    else:
        nothing[...] = jnp.zeros(nothing.shape, BF16)
        acc[own_rows, :] = jnp.zeros((ORB_DEV * BOX, PLANE), F32)
    for place in places:

        @pl.when(touched[place[0]] == 0)
        def _(place=place):
            keep(*place).start()

        if carried:

            @pl.when(touched[place[0]] == 1)
            def _(place=place):
                take(*place).start()

    padded[...] = jnp.zeros(padded.shape, F32)
    if carried:
        pltpu.make_async_copy(sums_in[0], acc.at[own_rows], out_sems.at[0]).wait()
    for place in places:

        @pl.when(touched[place[0]] == 1)
        def _(place=place):
            some = box_rows(place[0])
            if carried:
                take(*place).wait()
                acc[some, :] = stage[some, :].astype(F32)
            else:
                acc[some, :] = jnp.zeros((BOX, PLANE), F32)

    def add(source, slot, lanes, value):
        at = box_rows(source * ORB_DEV + slot)
        acc[at, lanes] = acc[at, lanes] + value

    def one_step(step, carry):
        buffer = step & 1

        @pl.when(step + 1 < end)
        def _():
            start_loads(step + 1, 1 - buffer)

        wait_loads(step, buffer)
        for i in range(2):
            task = (step * 2 + i + 1) * TASK_WIDTH

            @pl.when(step * 2 + i < count)
            def _(i=i, task=task):
                def value(lanes):
                    return held[buffer, 2 * i + 1, :, lanes].astype(F32)

                def put(lanes, block):
                    theirs[i, :, lanes] = block

                shift_box(padded, value, put, mine[task + 4], mine[task + 5], mine[task + 6])

        @pl.when(step == begin)
        def _():
            for copy in table_copies():
                copy.wait()

        def density(b, some, r, c):
            lanes = pl.ds((r * BLOCKS_Z + c) * 128, 128)
            return held[buffer, 2 * b, some, lanes].astype(F32) * theirs[b, some, lanes]

        solve(density, both, work, *tables, 2)
        for i in range(2):
            task = (step * 2 + i + 1) * TASK_WIDTH
            there = step * 2 + i < count
            kind = mine[task + 7]

            @pl.when(there & (kind != 2))
            def _(i=i, task=task):
                near = rounded(work[pl.ds(i * BOX, BOX), :] * theirs[i])
                add(mine[task], mine[task + 2], pl.ds(0, PLANE), near)

            @pl.when(there & (kind != 1))
            def _(i=i, task=task):
                def value(lanes):
                    mine_box = held[buffer, 2 * i, :, lanes].astype(F32)
                    return rounded(work[pl.ds(i * BOX, BOX), lanes] * mine_box)

                def put(lanes, block):
                    add(mine[task + 1], mine[task + 3], lanes, block)

                shift_box(padded, value, put, -mine[task + 4], -mine[task + 5], -mine[task + 6])

        return carry

    lax.fori_loop(begin, end, one_step, 0)

    own = pltpu.make_async_copy(acc.at[own_rows], outs[0], out_sems.at[0])
    own.start()
    for place in places:

        @pl.when(touched[place[0]] == 1)
        def _(place=place):
            some = box_rows(place[0])
            stage[some, :] = acc[some, :].astype(BF16)
            send(*place).start()

    own.wait()
    for place in places:
        send(*place).wait()


def exchange(part, listing, boxes, tables, sums=()):
    any_space = pl.BlockSpec(memory_space=pl.ANY)
    smem = pl.BlockSpec(memory_space=pltpu.SMEM)
    outs = [
        jax.ShapeDtypeStruct((size * BOX, PLANE), F32 if i == 0 else BF16)
        for i, size in enumerate(SIZES)
    ]

    def kernel(*refs):
        exchange_kernel(part, *refs)

    return pl.pallas_call(
        kernel,
        out_shape=outs,
        in_specs=[smem] + [any_space] * (len(boxes) + len(tables) + len(sums)),
        out_specs=[any_space] * len(outs),
        scratch_shapes=[
            *[pltpu.VMEM(t.shape, t.dtype) for t in tables],
            pltpu.VMEM((SOURCES * ORB_DEV * BOX, PLANE), F32),
            pltpu.VMEM((SOURCES * ORB_DEV * BOX, PLANE), BF16),
            pltpu.VMEM((BOX, PLANE), BF16),
            pltpu.VMEM((2, 4, BOX, PLANE), BF16),
            pltpu.VMEM((2, BOX, PLANE), F32),
            pltpu.VMEM((4 * BOX, PLANE), BF16),
            pltpu.VMEM((2 * BOX, PLANE), F32),
            pltpu.VMEM((WIDE_Y * WIDE_Z * ROWS_PADDED, 128), F32),
            pltpu.SMEM(((MAX_TASKS + 3) * TASK_WIDTH,), jnp.int32),
            pltpu.SMEM((SOURCES * ORB_DEV,), jnp.int32),
            pltpu.SemaphoreType.DMA((2, 4)),
            pltpu.SemaphoreType.DMA((N_TABLES,)),
            pltpu.SemaphoreType.DMA((SOURCES * ORB_DEV,)),
        ],
        compiler_params=pltpu.CompilerParams(vmem_limit_bytes=56 * 1024 * 1024),
        cost_estimate=pl.CostEstimate(
            flops=10_000_000_000, bytes_accessed=30_000_000, transcendentals=0
        ),
        name=("first_application", "second_early", "second_late")[part],
    )(listing, *boxes, *tables, *sums)


def reorder_kernel(box, order, out):
    moved = jnp.dot(box[...], order[...], preferred_element_type=F32)
    out[...] = moved.astype(BF16)


def total_kernel(own, abroad, first, second, order, out):
    result = own[...] + abroad[...].astype(F32)
    result += first[...].astype(F32) + second[...].astype(F32)
    moved = jnp.dot((-result).astype(BF16), order[...], preferred_element_type=F32)
    out[...] = moved.astype(BF16)


def by_chunks(kernel, name, arrays, order):
    rows = arrays[0].shape[0]
    whole = pl.BlockSpec((CHUNK, CHUNK), lambda i: (0, 0))
    some = pl.BlockSpec((rows, CHUNK), lambda i: (0, i))
    return pl.pallas_call(
        kernel,
        grid=(BLOCKS_Y,),
        out_shape=jax.ShapeDtypeStruct((rows, PLANE), BF16),
        in_specs=[some] * len(arrays) + [whole],
        out_specs=some,
        name=name,
    )(*arrays, order)


def reorder(boxes, order):
    return by_chunks(reorder_kernel, "reorder", [boxes], order)


def total(own, abroad, first, second, order):
    return by_chunks(total_kernel, "total", [own, abroad, first, second], order)


def moves(n_region):
    def step(dx, dz):
        pairs = []
        for region in range(n_region):
            sign = 1 - 2 * (region % 2)
            for x in range(GRID):
                for z in range(GRID):
                    to = (x + sign * dx) % GRID * GRID + (z + sign * dz) % GRID
                    pairs.append((region * N_SUB + x * GRID + z, region * N_SUB + to))

        def move(block):
            return lax.ppermute(block, ("region", "sub"), pairs)

        return move

    def across(distance):
        pairs = [(i, (i + distance) % n_region) for i in range(n_region)]

        def move(block):
            return lax.ppermute(block, "region", pairs)

        return move

    return step, across


def per_device(orbitals, trial_set, own_slot, partner_route, partner_slot, offsets):
    n_region = lax.axis_size("region")
    region = lax.axis_index("region")
    sub = lax.axis_index("sub")
    step, across = moves(n_region)
    tables = transform_tables()
    tables = [
        jnp.asarray(tables[k])
        for k in TABLES
    ]
    order, order_back = jnp.asarray(order_table()), jnp.asarray(order_table().T.copy())
    table, most = meeting_table()
    meta = jnp.concatenate([own_slot, partner_route[:, 0], partner_slot])
    where = jnp.stack([region, sub, jnp.int32(n_region)]).astype(jnp.int32)
    smem = pl.BlockSpec(memory_space=pltpu.SMEM)

    def planner(*refs):
        plan_kernel(most, *refs)

    chosen = pl.pallas_call(
        planner,
        out_shape=jax.ShapeDtypeStruct((NOTE,), jnp.int32),
        in_specs=[smem] * 4,
        out_specs=smem,
        scratch_shapes=[pltpu.SMEM((2 * len(PLACES),), jnp.int32)],
        name="plan",
    )(where, meta, offsets.reshape(-1), jnp.asarray(table))

    def near_places(boxes):
        return step(0, 1)(boxes), step(1, 0)(boxes), across(-1)(boxes)

    def cut(b01, b10):
        return b01[: 2 * BOX], b10[2 * BOX :]

    def far_places(b01, b10, halves):
        low, high = halves
        return step(1, 0)(low), step(0, 1)(high), step(0, -1)(b10), step(-1, 0)(b01)

    def begin_back(parts):
        own, c01, c10, c11_low, c11_high, c13, c31, c_abroad = parts
        return (
            step(0, 1)(c13),
            step(1, 0)(c31),
            step(-1, 0)(c11_low),
            step(0, -1)(c11_high),
            across(1)(c_abroad),
        )

    def merge(parts, arrived):
        r13, r31, r11_low, r11_high, _ = arrived
        none = jnp.zeros_like(r11_low)
        low = jnp.concatenate([r11_low, none])
        high = jnp.concatenate([none, r11_high])
        m01 = (parts[1].astype(F32) + r31.astype(F32) + low.astype(F32)).astype(BF16)
        m10 = (parts[2].astype(F32) + r13.astype(F32) + high.astype(F32)).astype(BF16)
        return step(0, -1)(m01), step(-1, 0)(m10)

    def finish(parts, arrived, merged):
        result = total(parts[0], arrived[4], *merged, order_back)
        return result.reshape(ORB_DEV, BOX, PLANE)

    ordered = lax.optimization_barrier
    boxes = reorder(orbitals.reshape(ORB_DEV * BOX, PLANE), order)
    o01, o10, o_abroad = near_places(boxes)
    trials = reorder(trial_set.reshape(ORB_DEV * BOX, PLANE), order)
    t01, t10, t_abroad = near_places(trials)
    notes = [chosen] + [step(*place)(chosen) for place in PLACES[1:]]
    o01, o10, o_abroad, notes = ordered((o01, o10, o_abroad, notes))
    o_far = far_places(o01, o10, cut(o01, o10))
    listing = jnp.concatenate([n[:LISTED] for n in notes])
    t_cut = cut(t01, t10)
    t01, t10, t_cut, t_abroad, o_far, listing = ordered((t01, t10, t_cut, t_abroad, o_far, listing))
    t_far = far_places(t01, t10, t_cut)
    orbital_boxes = [boxes, o01, o10, *o_far, o_abroad]
    first = exchange(0, listing, orbital_boxes, tables)
    arrived_first = begin_back(first)
    first, listing, t_far = ordered((first, listing, t_far))
    all_boxes = orbital_boxes + [trials, t01, t10, *t_far, t_abroad]
    early = exchange(1, listing, all_boxes, tables)
    early, first, arrived_first = ordered((early, first, arrived_first))
    merged_first = merge(first, arrived_first)
    late = exchange(2, listing, all_boxes, tables, early)
    late, merged_first = ordered((late, merged_first))
    result_first = finish(first, arrived_first, merged_first)
    arrived_late = begin_back(late)
    result_second = finish(late, arrived_late, merge(late, arrived_late))
    return result_first, result_second


def solution(mesh):
    in_specs = (
        P(("region", "sub"), None, None),
        P(("region", "sub"), None, None),
        P(("region", "sub")),
        P(("region", "sub"), None),
        P(("region", "sub")),
        P(),
    )
    out_specs = (P(("region", "sub"), None, None), P(("region", "sub"), None, None))
    return jax.shard_map(
        per_device, mesh=mesh, in_specs=in_specs, out_specs=out_specs, check_vma=False
    )
```

```python
import math

import jax
import jax.numpy as jnp
import ml_dtypes
import numpy as np
from jax import lax
from jax.experimental import pallas as pl
from jax.experimental.pallas import tpu as pltpu
from jax.sharding import PartitionSpec as P

BOX = 48
PLANE = BOX * BOX
CHUNK = PLANE // 6
SCREEN = 0.5
GRID = 4
N_SUB = GRID * GRID
ORB_DEV = 4
PAIRS_DEV = 4
N_PAIRS = N_SUB * PAIRS_DEV

PLACES = ((0, 0), (0, 1), (1, 0), (1, 1), (1, 3), (3, 1))
REGION_SOURCE = len(PLACES)
SOURCES = len(PLACES) + 1
LIST_WIDTH = 16
TASK_WIDTH = 8
LISTED = PAIRS_DEV * LIST_WIDTH
NOTE_ROWS = 16
SETS = 2
SET_ROWS = ORB_DEV * BOX
SOURCE_SLOTS = SETS * ORB_DEV
FAR_PLACES = (3, 4, 5)
GIVEN = (
    ((0, 0, 8), (1, 0, 8), (2, 0, 8), (6, 0, 8)),
    ((0, 0, 8), (1, 0, 8), (2, 0, 8), (3, 0, 4), (3, 4, 4), (4, 0, 8), (5, 0, 8)),
    ((0, 0, 8), (1, 0, 8), (2, 0, 8)),
)
N_TABLES = 4
BLOCKS_Y = 6
BLOCKS_Z = 3
MARGIN = 24
ROWS_PADDED = BOX + 2 * MARGIN
SIDE_Y = 3
SIDE_Z = 2
WIDE_Y = BLOCKS_Y + 2 * SIDE_Y
WIDE_Z = BLOCKS_Z + 2 * SIDE_Z
MAX_TASKS = 3 * len(PLACES) * PAIRS_DEV
HALF_ROOT3 = math.sqrt(3.0) / 2.0
F32 = jnp.float32
BF16 = jnp.bfloat16


def meeting_table():
    found = [[] for _ in range(N_SUB)]
    for i, (ax, az) in enumerate(PLACES):
        for j, (bx, bz) in enumerate(PLACES):
            delta = (ax - bx) % GRID * GRID + (az - bz) % GRID
            found[delta].append(i + 8 * j)
    most = max(len(f) for f in found)
    codes = np.array([f + [f[-1]] * (most - len(f)) for f in found], np.int32)
    counts = np.array([len(f) for f in found], np.int32)
    return np.concatenate([counts, codes.reshape(-1)]), most


def high_low(matrix):
    high = matrix.astype(ml_dtypes.bfloat16)
    low = (matrix - high.astype(np.float64)).astype(ml_dtypes.bfloat16)
    return np.stack([high, low])


def cas(angles):
    return np.cos(angles) + np.sin(angles)


def transform_tables():
    turn = 2.0 * math.pi / BOX
    n = np.arange(BOX)
    line = cas(turn * (n[:, None] * n[None, :] % BOX))
    q, w = np.arange(8), np.arange(16)

    def angle_y(j):
        return turn * (q[:, None] * (6 * q[None, :] + j) % BOX)

    def angle_z(j):
        return turn * (w[:, None] * (3 * w[None, :] + j) % BOX)

    def both_parts(angle):
        c, s = np.cos(angle), np.sin(angle)
        return np.block([[c, -s], [s, c]])

    def planes(y, z, sign):
        whole = angle_y(y)[:, None, :, None] + sign * angle_z(z)[None, :, None, :]
        return both_parts(whole.reshape(128, 128))

    def real_complex(y):
        z = both_parts(angle_z(1)).reshape(2, 16, 2, 16)
        return np.einsum("qm,awbn->aqwbmn", cas(angle_y(y)), z).reshape(256, 256)

    def complex_real(y):
        return np.kron(both_parts(angle_y(y)), cas(angle_z(0)))

    zero = np.zeros((128, 128))
    real = [np.kron(cas(angle_y(y)), cas(angle_z(0))) for y in (0, 3)]
    waves = [np.block([[real[0], zero], [zero, real[1]]]), real_complex(0), real_complex(3)]
    waves += [complex_real(1), complex_real(2)]
    for y in (1, 2):
        waves += [planes(y, 1, 1), planes(y, 1, -1)]
    waves = np.stack(waves)
    lam = 4.0 * np.sin(math.pi * n / BOX) ** 2

    def spectrum(y, z, weight):
        ky, kz = 6 * q + y, 3 * w + z
        total = lam[:, None, None] + lam[ky][None, :, None] + lam[kz][None, None, :] + SCREEN
        return (weight * 4.0 * math.pi / total / float(BOX**3)).reshape(BOX, 128)

    order = [(0, 0, 1.0), (3, 0, 1.0)]
    for y, z in ((0, 1), (3, 1), (1, 0), (2, 0), (1, 1), (1, 1), (2, 1), (2, 1)):
        order += [(y, z, 2.0)] * 2
    green = np.concatenate([spectrum(*o) for o in order], axis=1)
    rows = high_low(line)
    rows = np.concatenate([rows[0], rows[1], rows[0]], axis=1)
    return dict(
        waves=high_low(waves),
        waves_back=high_low(waves.transpose(0, 2, 1)),
        green=green.astype(np.float32),
        rows=rows,
    )


TABLES = ("waves", "waves_back", "green", "rows")


def order_table():
    lane = np.arange(8 * BOX)
    q, c, w = lane // BOX, lane % BOX // 16, lane % 16
    table = np.zeros((8 * BOX, 8 * BOX), np.float32)
    table[lane, c * 128 + q * 16 + w] = 1.0
    return table.astype(ml_dtypes.bfloat16)


def plan_kernel(most, where, meta, offsets, table, chosen, used):
    region, sub, n_region = where[0], where[1], where[2]
    sign = 1 - 2 * (region & 1)
    next_region = jnp.where(region + 1 == n_region, 0, region + 1)
    for i in range(2 * len(PLACES)):
        used[i] = 0

    def place(pair, turn):
        own_slot = meta[pair]
        route = meta[PAIRS_DEV + pair]
        partner_slot = meta[2 * PAIRS_DEV + pair]
        abroad = route == N_SUB
        other = jnp.where(abroad, sub, route)
        dx = (sign * ((other >> 2) - (sub >> 2))) & 3
        dz = (sign * ((other & 3) - (sub & 3))) & 3
        delta = dx * GRID + dz
        count = jnp.where(abroad, 1, table[delta])

        @pl.when(jnp.where(count == 1, 0, 1) == turn)
        def _():
            row = pair * LIST_WIDTH
            for kind in range(3):
                load_of = len(PLACES) * min(kind, 1)
                best_load = jnp.int32(1 << 20)
                best_code = jnp.int32(0)
                for k in range(most):
                    code = table[N_SUB + delta * most + k]
                    load = used[load_of + (code & 7)]
                    better = load < best_load
                    best_load = jnp.where(better, load, best_load)
                    best_code = jnp.where(better, code, best_code)
                at = jnp.where(abroad, 0, best_code & 7)
                used[load_of + at] = used[load_of + at] + 1
                chosen[row + 2 * kind] = at
                chosen[row + 2 * kind + 1] = jnp.where(
                    abroad, REGION_SOURCE, (best_code >> 3) & 7
                )
            first = (region * N_SUB + sub) * ORB_DEV + own_slot
            second_region = jnp.where(abroad, next_region, region)
            second = (second_region * N_SUB + other) * ORB_DEV + partner_slot
            chosen[row + 6] = own_slot
            chosen[row + 7] = partner_slot
            for c in range(3):
                chosen[row + 8 + c] = offsets[first * 3 + c] - offsets[second * 3 + c]
            for c in range(11, LIST_WIDTH):
                chosen[row + c] = 0

    for turn in range(2):
        for pair in range(PAIRS_DEV):
            place(pair, turn)


def three_dots(high, low, weights, index):
    boxes_high = jnp.concatenate([high, low], axis=0)
    half = high.shape[0]
    wide = jnp.dot(boxes_high, weights[0, index], preferred_element_type=F32)
    rest = jnp.dot(high, weights[1, index], preferred_element_type=F32)
    return wide[:half] + wide[half:] + rest


def split(value):
    high = value.astype(BF16)
    return high, (value - high.astype(F32)).astype(BF16)


def six_points(x):
    u = [x[r] + x[r + 3] for r in range(3)]
    v = [x[r] - x[r + 3] for r in range(3)]
    return (
        u[0] + u[1] + u[2],
        v[0] - v[1] + v[2],
        v[0] + 0.5 * (v[1] - v[2]),
        -HALF_ROOT3 * (v[1] + v[2]),
        u[0] - 0.5 * (u[1] + u[2]),
        -HALF_ROOT3 * (u[1] - u[2]),
    )


def six_points_back(t0, t3, t1r, t1i, t2r, t2i):
    a0 = t0 + t2r
    t2h = t0 - 0.5 * t2r
    t2s = HALF_ROOT3 * t2i
    a1 = t2h - t2s
    a2 = t2h + t2s
    t1s = HALF_ROOT3 * t1i
    b0 = t3 + t1r
    b1 = 0.5 * t1r - t3 - t1s
    b2 = t3 - 0.5 * t1r - t1s
    return a0 + b0, a1 + b1, a2 + b2, a0 - b0, a1 - b1, a2 - b2


def three_points(x):
    total = x[1] + x[2]
    return x[0] + total, x[0] - 0.5 * total, -HALF_ROOT3 * (x[1] - x[2])


def three_points_back(s0, s1r, s1i):
    low = s0 - 0.5 * s1r
    turned = HALF_ROOT3 * s1i
    return s0 + s1r, low - turned, low + turned


def solve(density, both, work, waves, waves_back, green, rows, boxes):
    for b in range(boxes):
        for g in range(BOX // 16):
            some = pl.ds(b * BOX + g * 16, 16)
            low_some = pl.ds((boxes + b) * BOX + g * 16, 16)
            columns = []
            for c in range(BLOCKS_Z):
                x = [density(b, pl.ds(g * 16, 16), r, c) for r in range(BLOCKS_Y)]
                columns.append(six_points(x))
            t = [three_points([columns[c][j] for c in range(BLOCKS_Z)]) for j in range(6)]
            parts = [t[0][0], t[1][0], t[0][1], t[0][2], t[1][1], t[1][2]]
            parts += [t[2][0], t[3][0], t[4][0], t[5][0]]
            for j in (2, 4):
                (_, rr, ri), (_, ir, ii) = t[j], t[j + 1]
                parts += [rr - ii, ri + ir, rr + ii, ir - ri]
            for i, part in enumerate(parts):
                high, low = split(part)
                both[some, pl.ds(i * 128, 128)] = high
                both[low_some, pl.ds(i * 128, 128)] = low

    def row_pass(value):
        high, low = split(value)
        stacked = jnp.concatenate([high, high, low], axis=0)
        return jnp.dot(rows[...], stacked, preferred_element_type=F32)

    def plane_pass(weights):
        for group in range(9):
            lanes = pl.ds(group * 256, 256)
            high = both[pl.ds(0, boxes * BOX), lanes]
            low = both[pl.ds(boxes * BOX, boxes * BOX), lanes]
            work[:, lanes] = three_dots(high, low, weights, group)

    places = [
        (pl.ds(b * BOX, BOX), pl.ds((boxes + b) * BOX, BOX), pl.ds(group * 256, 256))
        for b in range(boxes)
        for group in range(9)
    ]
    plane_pass(waves)
    for some, _, lanes in places:
        work[some, lanes] = row_pass(work[some, lanes]) * green[:, lanes]
    for some, low_some, lanes in places:
        both[some, lanes], both[low_some, lanes] = split(row_pass(work[some, lanes]))
    plane_pass(waves_back)

    for b in range(boxes):
        for g in range(BOX // 16):
            some = pl.ds(b * BOX + g * 16, 16)
            p = [work[some, pl.ds(i * 128, 128)] for i in range(18)]
            t = [[p[0], p[2], p[3]], [p[1], p[4], p[5]]]
            for j in range(2):
                pr, pi, mr, mi = p[10 + 4 * j : 14 + 4 * j]
                t.append([p[6 + 2 * j], pr + mr, pi - mi])
                t.append([p[7 + 2 * j], pi + mi, mr - pr])
            t = [three_points_back(*parts) for parts in t]
            for c in range(BLOCKS_Z):
                values = six_points_back(*[t[j][c] for j in range(6)])
                for r, value in enumerate(values):
                    work[some, pl.ds((r * BLOCKS_Z + c) * 128, 128)] = value


def rounded(value):
    return value.astype(BF16).astype(F32)


def shift_box(padded, value, put, dx, dy, dz):
    for r in range(BLOCKS_Y):
        for c in range(BLOCKS_Z):
            at = ((r + SIDE_Y) * WIDE_Z + c + SIDE_Z) * ROWS_PADDED + MARGIN
            padded[pl.ds(at, BOX), :] = value(pl.ds((r * BLOCKS_Z + c) * 128, 128))
    fine_y, fine_z = dy & 7, dz & 15
    start = ((dy >> 3) + SIDE_Y) * WIDE_Z + (dz >> 4) + SIDE_Z
    base = start * ROWS_PADDED + MARGIN + dx
    lane = lax.broadcasted_iota(jnp.int32, (1, 128), 1)
    next_y = (lane >> 4) < fine_y
    next_z = (lane & 15) < fine_z
    carried = (lane & 15) + fine_z >= 16
    ahead = fine_y * 16 + fine_z
    turn = (128 - ahead) & 127
    turn_carried = (128 + 16 - ahead) & 127

    def block(r, c):
        return padded[pl.ds(base + (r * WIDE_Z + c) * ROWS_PADDED, BOX), :]

    for r in range(BLOCKS_Y):
        mixed = [jnp.where(next_y, block(r + 1, c), block(r, c)) for c in range(BLOCKS_Z + 1)]
        for c in range(BLOCKS_Z):
            source = jnp.where(next_z, mixed[c + 1], mixed[c])
            out = jnp.where(
                carried, pltpu.roll(source, turn_carried, 1), pltpu.roll(source, turn, 1)
            )
            put(pl.ds((r * BLOCKS_Z + c) * 128, 128), out)


def exchange_kernel(part, *refs):
    n_in = 4 if part == 0 else SOURCES + 1
    n_out = len(GIVEN[part])
    listing, *refs = refs
    boxes_in, refs = refs[:n_in], refs[n_in:]
    tables_in, refs = refs[:N_TABLES], refs[N_TABLES:]
    outs, refs = refs[:n_out], refs[n_out:]
    tables, refs = refs[:N_TABLES], refs[N_TABLES:]
    acc, stage, nothing, held, theirs, both, work, padded, *refs = refs
    mine, touched, sems, table_sems, out_sems = refs

    def is_far(source):
        return (source >= FAR_PLACES[0]) & (source <= FAR_PLACES[-1])

    mine[0] = 0
    for home in range(len(PLACES)):
        if part == 0 and home in FAR_PLACES:
            continue

        def check(pair, carry, home=home):
            row = (home * PAIRS_DEV + pair) * LIST_WIDTH
            for kind in range(3):
                source = listing[row + 2 * kind + 1]
                far = is_far(source)
                if part == 0:
                    now = jnp.logical_not(far)
                elif home in FAR_PLACES:
                    gives_far = far if kind == 2 else jnp.bool_(True)
                    now = gives_far if part == 1 else jnp.logical_not(gives_far)
                elif kind == 1:
                    now = far if part == 2 else jnp.bool_(False)
                else:
                    now = far if part == 1 else jnp.bool_(False)

                @pl.when((listing[row + 2 * kind] == home) & now)
                def _(kind=kind):
                    at = mine[0]
                    mine[0] = at + 1
                    task = (at + 1) * TASK_WIDTH
                    mine[task] = home
                    mine[task + 1] = listing[row + 2 * kind + 1]
                    for c in range(5):
                        mine[task + 2 + c] = listing[row + 6 + c]
                    mine[task + 7] = kind

            return carry

        lax.fori_loop(0, PAIRS_DEV, check, 0)

    count = mine[0]
    begin, end = 0, (count + 1) >> 1

    def table_copies():
        return [
            pltpu.make_async_copy(tables_in[i], tables[i], table_sems.at[i])
            for i in range(N_TABLES)
        ]

    def fetch(of_trial, source, slot, target, sem):
        def start(ref, row):
            row = pl.multiple_of(row, 16)
            pltpu.make_async_copy(ref.at[pl.ds(row, BOX)], target, sem).start()

        slot_row = slot * BOX
        whole_row = jnp.where(of_trial, SET_ROWS, 0) + slot_row
        for s in range(SOURCES):
            if part == 0 and s in FAR_PLACES:
                continue
            if s == 3:

                @pl.when((source == s) & jnp.logical_not(of_trial))
                def _():
                    start(boxes_in[3], slot_row)

                @pl.when((source == s) & of_trial)
                def _():
                    start(boxes_in[4], slot_row)
            else:
                at = s if s < 3 else (3 if part == 0 else s + 1)

                @pl.when(source == s)
                def _(at=at):
                    start(boxes_in[at], whole_row)

    def each_load(step, act):
        for i in range(2):
            task = (step * 2 + i + 1) * TASK_WIDTH

            @pl.when(step * 2 + i < count)
            def _(i=i, task=task):
                kind = mine[task + 7]
                act(kind == 1, mine[task], mine[task + 2], 2 * i)
                act(kind == 2, mine[task + 1], mine[task + 3], 2 * i + 1)

    def start_loads(step, buffer):
        def act(of_trial, source, slot, i):
            fetch(of_trial, source, slot, held.at[buffer, i], sems.at[buffer, i])

        each_load(step, act)

    def wait_loads(step, buffer):
        def act(of_trial, source, slot, i):
            pltpu.make_async_copy(
                boxes_in[0].at[pl.ds(0, BOX)], held.at[buffer, i], sems.at[buffer, i]
            ).wait()

        each_load(step, act)

    def box_rows(i):
        return pl.ds(pl.multiple_of(i * BOX, BOX), BOX)

    def sum_slot(task, which, kind):
        of_set = jnp.where(kind == 0, 0, ORB_DEV)
        return mine[task + which] * SOURCE_SLOTS + of_set + mine[task + 2 + which]

    places = []
    for i, (source, low, size) in enumerate(GIVEN[part]):
        for k in range(size):
            places.append((source * SOURCE_SLOTS + low + k, i, pl.ds(k * BOX, BOX)))

    def keep(slot, i, some):
        return pltpu.make_async_copy(nothing, outs[i].at[some], out_sems.at[slot])

    def send(slot, i, some):
        return pltpu.make_async_copy(stage.at[box_rows(slot)], outs[i].at[some], out_sems.at[slot])

    @pl.when(begin < end)
    def _():
        start_loads(begin, begin & 1)
        for copy in table_copies():
            copy.start()

    for i in range(SOURCES * SOURCE_SLOTS):
        touched[i] = 0

    def mark(i, carry):
        task = (i + 1) * TASK_WIDTH
        kind = mine[task + 7]

        @pl.when(kind != 2)
        def _():
            touched[sum_slot(task, 0, kind)] = 1

        @pl.when(kind != 1)
        def _():
            touched[sum_slot(task, 1, kind)] = 1

        return carry

    lax.fori_loop(0, count, mark, 0)
    nothing[...] = jnp.zeros(nothing.shape, BF16)
    for place in places:

        @pl.when(touched[place[0]] == 0)
        def _(place=place):
            keep(*place).start()

    padded[...] = jnp.zeros(padded.shape, F32)

    def clear(i, carry):
        @pl.when(touched[i] == 1)
        def _():
            acc[box_rows(i), :] = jnp.zeros((BOX, PLANE), F32)

        return carry

    lax.fori_loop(0, SOURCES * SOURCE_SLOTS, clear, 0)

    def add(slot, lanes, value):
        at = box_rows(slot)
        acc[at, lanes] = acc[at, lanes] + value

    def one_step(step, carry):
        buffer = step & 1

        @pl.when(step + 1 < end)
        def _():
            start_loads(step + 1, 1 - buffer)

        wait_loads(step, buffer)
        for i in range(2):
            task = (step * 2 + i + 1) * TASK_WIDTH

            @pl.when(step * 2 + i < count)
            def _(i=i, task=task):
                def value(lanes):
                    return held[buffer, 2 * i + 1, :, lanes].astype(F32)

                def put(lanes, block):
                    theirs[i, :, lanes] = block

                shift_box(padded, value, put, mine[task + 4], mine[task + 5], mine[task + 6])

        @pl.when(step == begin)
        def _():
            for copy in table_copies():
                copy.wait()

        def density(b, some, r, c):
            lanes = pl.ds((r * BLOCKS_Z + c) * 128, 128)
            return held[buffer, 2 * b, some, lanes].astype(F32) * theirs[b, some, lanes]

        solve(density, both, work, *tables, 2)
        for i in range(2):
            task = (step * 2 + i + 1) * TASK_WIDTH
            there = step * 2 + i < count
            kind = mine[task + 7]

            @pl.when(there & (kind != 2))
            def _(i=i, task=task, kind=kind):
                near = rounded(work[pl.ds(i * BOX, BOX), :] * theirs[i])
                add(sum_slot(task, 0, kind), pl.ds(0, PLANE), near)

            @pl.when(there & (kind != 1))
            def _(i=i, task=task, kind=kind):
                slot = sum_slot(task, 1, kind)

                def value(lanes):
                    mine_box = held[buffer, 2 * i, :, lanes].astype(F32)
                    return rounded(work[pl.ds(i * BOX, BOX), lanes] * mine_box)

                def put(lanes, block):
                    add(slot, lanes, block)

                shift_box(padded, value, put, -mine[task + 4], -mine[task + 5], -mine[task + 6])

        return carry

    lax.fori_loop(begin, end, one_step, 0)

    def put(i, carry):
        @pl.when(touched[i] == 1)
        def _():
            some = box_rows(i)
            stage[some, :] = acc[some, :].astype(BF16)

        return carry

    lax.fori_loop(0, SOURCES * SOURCE_SLOTS, put, 0)
    for place in places:

        @pl.when(touched[place[0]] == 1)
        def _(place=place):
            send(*place).start()

    for place in places:
        send(*place).wait()


def exchange(part, listing, boxes, tables):
    any_space = pl.BlockSpec(memory_space=pl.ANY)
    smem = pl.BlockSpec(memory_space=pltpu.SMEM)
    outs = [
        jax.ShapeDtypeStruct((size * BOX, PLANE), BF16) for _, _, size in GIVEN[part]
    ]
    slots = SOURCES * SOURCE_SLOTS

    def kernel(*refs):
        exchange_kernel(part, *refs)

    return pl.pallas_call(
        kernel,
        out_shape=outs,
        in_specs=[smem] + [any_space] * (len(boxes) + len(tables)),
        out_specs=[any_space] * len(outs),
        scratch_shapes=[
            *[pltpu.VMEM(t.shape, t.dtype) for t in tables],
            pltpu.VMEM((slots * BOX, PLANE), F32),
            pltpu.VMEM((slots * BOX, PLANE), BF16),
            pltpu.VMEM((BOX, PLANE), BF16),
            pltpu.VMEM((2, 4, BOX, PLANE), BF16),
            pltpu.VMEM((2, BOX, PLANE), F32),
            pltpu.VMEM((4 * BOX, PLANE), BF16),
            pltpu.VMEM((2 * BOX, PLANE), F32),
            pltpu.VMEM((WIDE_Y * WIDE_Z * ROWS_PADDED, 128), F32),
            pltpu.SMEM(((MAX_TASKS + 3) * TASK_WIDTH,), jnp.int32),
            pltpu.SMEM((slots,), jnp.int32),
            pltpu.SemaphoreType.DMA((2, 4)),
            pltpu.SemaphoreType.DMA((N_TABLES,)),
            pltpu.SemaphoreType.DMA((slots,)),
        ],
        compiler_params=pltpu.CompilerParams(vmem_limit_bytes=56 * 1024 * 1024),
        cost_estimate=pl.CostEstimate(
            flops=15_000_000_000, bytes_accessed=30_000_000, transcendentals=0
        ),
        name=("near_tasks", "far_tasks", "other_tasks")[part],
    )(listing, *boxes, *tables)


def reorder_kernel(orbitals, trials, notes, order, out):
    for r in range(BLOCKS_Y):
        lanes = pl.ds(r * CHUNK, CHUNK)
        for at, box in ((0, orbitals), (SET_ROWS, trials)):
            moved = jnp.dot(box[:, lanes], order[...], preferred_element_type=F32)
            out[pl.ds(at, SET_ROWS), lanes] = moved.astype(BF16)
    out[pl.ds(SETS * SET_ROWS, NOTE_ROWS), :] = notes[...]


def reorder(orbitals, trials, notes, order):
    return pl.pallas_call(
        reorder_kernel,
        out_shape=jax.ShapeDtypeStruct((SETS * SET_ROWS + NOTE_ROWS, PLANE), BF16),
        name="reorder",
        compiler_params=pltpu.CompilerParams(vmem_limit_bytes=32 * 1024 * 1024),
    )(orbitals, trials, notes, order)


def total_kernel(*refs):
    *parts, order, out_orbitals, out_trials = refs
    i = pl.program_id(0)
    for out, now in ((out_orbitals, i < 2), (out_trials, i >= 2)):

        @pl.when(now)
        def _(out=out):
            for r in range(BLOCKS_Y):
                lanes = pl.ds(r * CHUNK, CHUNK)
                result = parts[0][:, lanes].astype(F32)
                for part in parts[1:]:
                    result += part[:, lanes].astype(F32)
                moved = jnp.dot((-result).astype(BF16), order[...], preferred_element_type=F32)
                out[:, lanes] = moved.astype(BF16)


def total(parts, order):
    half = SET_ROWS // 2
    whole = pl.BlockSpec((CHUNK, CHUNK), lambda i: (0, 0))
    some = pl.BlockSpec((half, PLANE), lambda i: (i, 0))
    out = jax.ShapeDtypeStruct((SET_ROWS, PLANE), BF16)
    return pl.pallas_call(
        total_kernel,
        grid=(4,),
        out_shape=[out, out],
        in_specs=[some] * len(parts) + [whole],
        out_specs=[
            pl.BlockSpec((half, PLANE), lambda i: (jnp.minimum(i, 1), 0)),
            pl.BlockSpec((half, PLANE), lambda i: (jnp.maximum(i - 2, 0), 0)),
        ],
        name="total",
        compiler_params=pltpu.CompilerParams(vmem_limit_bytes=32 * 1024 * 1024),
    )(*parts, order)


def moves(n_region):
    def step(dx, dz):
        pairs = []
        for region in range(n_region):
            sign = 1 - 2 * (region % 2)
            for x in range(GRID):
                for z in range(GRID):
                    to = (x + sign * dx) % GRID * GRID + (z + sign * dz) % GRID
                    pairs.append((region * N_SUB + x * GRID + z, region * N_SUB + to))

        def move(block):
            return lax.ppermute(block, ("region", "sub"), pairs)

        return move

    def across(distance):
        pairs = [(i, (i + distance) % n_region) for i in range(n_region)]

        def move(block):
            return lax.ppermute(block, "region", pairs)

        return move

    return step, across


def per_device(orbitals, trial_set, own_slot, partner_route, partner_slot, offsets):
    n_region = lax.axis_size("region")
    region = lax.axis_index("region")
    sub = lax.axis_index("sub")
    step, across = moves(n_region)
    tables = transform_tables()
    tables = [
        jnp.asarray(tables[k])
        for k in TABLES
    ]
    order, order_back = jnp.asarray(order_table()), jnp.asarray(order_table().T.copy())
    table, most = meeting_table()
    meta = jnp.concatenate([own_slot, partner_route[:, 0], partner_slot])
    where = jnp.stack([region, sub, jnp.int32(n_region)]).astype(jnp.int32)
    smem = pl.BlockSpec(memory_space=pltpu.SMEM)

    def planner(*refs):
        plan_kernel(most, *refs)

    chosen = pl.pallas_call(
        planner,
        out_shape=jax.ShapeDtypeStruct((LISTED,), jnp.int32),
        in_specs=[smem] * 4,
        out_specs=smem,
        scratch_shapes=[pltpu.SMEM((2 * len(PLACES),), jnp.int32)],
        name="plan",
    )(where, meta, offsets.reshape(-1), jnp.asarray(table))

    ordered = lax.optimization_barrier
    notes = jnp.pad(chosen.astype(BF16)[None], ((0, NOTE_ROWS - 1), (0, PLANE - LISTED)))
    boxes = reorder(
        orbitals.reshape(SET_ROWS, PLANE), trial_set.reshape(SET_ROWS, PLANE), notes, order
    )
    b01, b10, abroad = ordered((step(0, 1)(boxes), step(1, 0)(boxes), across(-1)(boxes)))
    b13, b31 = step(0, -1)(b10), step(-1, 0)(b01)
    b11_orbitals, b11_trials = step(1, 0)(b01[:SET_ROWS]), step(0, 1)(b10[SET_ROWS:])

    def list_of(arrays):
        return jnp.concatenate([n[-NOTE_ROWS, :LISTED] for n in arrays]).astype(jnp.int32)

    near = exchange(0, list_of([boxes, b01, b10]), [boxes, b01, b10, abroad], tables)
    far_boxes = (b11_orbitals, b11_trials, b13, b31)
    near, far_boxes = ordered((near, far_boxes))
    b11_orbitals, b11_trials, b13, b31 = far_boxes
    listing = list_of([boxes, b01, b10, b11_trials, b13, b31])
    all_boxes = [boxes, b01, b10, *far_boxes, abroad]
    far = exchange(1, listing, all_boxes, tables)
    far, listing, to_next = ordered((far, listing, near[3]))
    r13, r31 = step(0, 1)(far[5]), step(1, 0)(far[6])
    r11_orbitals, r11_trials = step(-1, 0)(far[3]), step(0, -1)(far[4])
    r_abroad = across(1)(to_next)
    other = exchange(2, listing, all_boxes, tables)
    other, r13, r31, r11_orbitals, r11_trials, r_abroad = ordered(
        (other, r13, r31, r11_orbitals, r11_trials, r_abroad)
    )
    none = jnp.zeros_like(r11_orbitals)

    def add_up(arrays):
        return sum(a.astype(F32) for a in arrays).astype(BF16)

    low, high = jnp.concatenate([r11_orbitals, none]), jnp.concatenate([none, r11_trials])
    f01 = step(0, -1)(add_up([near[1], far[1], other[1], r31, low]))
    f10 = step(-1, 0)(add_up([near[2], far[2], other[2], r13, high]))
    results = total([near[0], far[0], other[0], r_abroad, f01, f10], order_back)
    return tuple(r.reshape(ORB_DEV, BOX, PLANE) for r in results)


def solution(mesh):
    in_specs = (
        P(("region", "sub"), None, None),
        P(("region", "sub"), None, None),
        P(("region", "sub")),
        P(("region", "sub"), None),
        P(("region", "sub")),
        P(),
    )
    out_specs = (P(("region", "sub"), None, None), P(("region", "sub"), None, None))
    return jax.shard_map(
        per_device, mesh=mesh, in_specs=in_specs, out_specs=out_specs, check_vma=False
    )
```

```python
import math

import jax
import jax.numpy as jnp
import ml_dtypes
import numpy as np
from jax import lax
from jax.experimental import pallas as pl
from jax.experimental.pallas import tpu as pltpu
from jax.sharding import PartitionSpec as P

BOX = 48
PLANE = BOX * BOX
CHUNK = PLANE // 6
SCREEN = 0.5
GRID = 4
N_SUB = GRID * GRID
ORB_DEV = 4
PAIRS_DEV = 4
N_PAIRS = N_SUB * PAIRS_DEV

PLACES = ((0, 0), (0, 1), (1, 0), (1, 1), (1, 3), (3, 1))
REGION_SOURCE = len(PLACES)
SOURCES = len(PLACES) + 1
LIST_WIDTH = 16
TASK_WIDTH = 8
LISTED = PAIRS_DEV * LIST_WIDTH
NOTE_ROWS = 16
SETS = 2
SET_ROWS = ORB_DEV * BOX
SOURCE_SLOTS = SETS * ORB_DEV
FAR_PLACES = (3, 4, 5)
GIVEN = (
    ((0, 0, 4), (0, 4, 4), (1, 0, 4), (1, 4, 4), (2, 0, 4), (2, 4, 4), (6, 0, 8)),
    tuple((source, low, 4) for source in range(6) for low in (0, 4)),
    ((0, 0, 4), (0, 4, 4), (1, 0, 4), (1, 4, 4), (2, 0, 4), (2, 4, 4)),
)
N_TABLES = 4
BLOCKS_Y = 6
BLOCKS_Z = 3
MARGIN = 24
ROWS_PADDED = BOX + 2 * MARGIN
SIDE_Y = 3
SIDE_Z = 2
WIDE_Y = BLOCKS_Y + 2 * SIDE_Y
WIDE_Z = BLOCKS_Z + 2 * SIDE_Z
MAX_TASKS = 3 * len(PLACES) * PAIRS_DEV
HALF_ROOT3 = math.sqrt(3.0) / 2.0
F32 = jnp.float32
BF16 = jnp.bfloat16


def meeting_table():
    found = [[] for _ in range(N_SUB)]
    for i, (ax, az) in enumerate(PLACES):
        for j, (bx, bz) in enumerate(PLACES):
            delta = (ax - bx) % GRID * GRID + (az - bz) % GRID
            found[delta].append(i + 8 * j)
    most = max(len(f) for f in found)
    codes = np.array([f + [f[-1]] * (most - len(f)) for f in found], np.int32)
    counts = np.array([len(f) for f in found], np.int32)
    return np.concatenate([counts, codes.reshape(-1)]), most


def high_low(matrix):
    high = matrix.astype(ml_dtypes.bfloat16)
    low = (matrix - high.astype(np.float64)).astype(ml_dtypes.bfloat16)
    return np.stack([high, low])


def cas(angles):
    return np.cos(angles) + np.sin(angles)


def transform_tables():
    turn = 2.0 * math.pi / BOX
    n = np.arange(BOX)
    line = cas(turn * (n[:, None] * n[None, :] % BOX))
    q, w = np.arange(8), np.arange(16)

    def angle_y(j):
        return turn * (q[:, None] * (6 * q[None, :] + j) % BOX)

    def angle_z(j):
        return turn * (w[:, None] * (3 * w[None, :] + j) % BOX)

    def both_parts(angle):
        c, s = np.cos(angle), np.sin(angle)
        return np.block([[c, -s], [s, c]])

    def planes(y, z, sign):
        whole = angle_y(y)[:, None, :, None] + sign * angle_z(z)[None, :, None, :]
        return both_parts(whole.reshape(128, 128))

    def real_complex(y):
        z = both_parts(angle_z(1)).reshape(2, 16, 2, 16)
        return np.einsum("qm,awbn->aqwbmn", cas(angle_y(y)), z).reshape(256, 256)

    def complex_real(y):
        return np.kron(both_parts(angle_y(y)), cas(angle_z(0)))

    zero = np.zeros((128, 128))
    real = [np.kron(cas(angle_y(y)), cas(angle_z(0))) for y in (0, 3)]
    waves = [np.block([[real[0], zero], [zero, real[1]]]), real_complex(0), real_complex(3)]
    waves += [complex_real(1), complex_real(2)]
    for y in (1, 2):
        waves += [planes(y, 1, 1), planes(y, 1, -1)]
    waves = np.stack(waves)
    lam = 4.0 * np.sin(math.pi * n / BOX) ** 2

    def spectrum(y, z, weight):
        ky, kz = 6 * q + y, 3 * w + z
        total = lam[:, None, None] + lam[ky][None, :, None] + lam[kz][None, None, :] + SCREEN
        return (weight * 4.0 * math.pi / total / float(BOX**3)).reshape(BOX, 128)

    order = [(0, 0, 1.0), (3, 0, 1.0)]
    for y, z in ((0, 1), (3, 1), (1, 0), (2, 0), (1, 1), (1, 1), (2, 1), (2, 1)):
        order += [(y, z, 2.0)] * 2
    green = np.concatenate([spectrum(*o) for o in order], axis=1)
    rows = high_low(line)
    rows = np.concatenate([rows[0], rows[1], rows[0]], axis=1)
    return dict(
        waves=high_low(waves),
        waves_back=high_low(waves.transpose(0, 2, 1)),
        green=green.astype(np.float32),
        rows=rows,
    )


TABLES = ("waves", "waves_back", "green", "rows")


def order_table():
    lane = np.arange(8 * BOX)
    q, c, w = lane // BOX, lane % BOX // 16, lane % 16
    table = np.zeros((8 * BOX, 8 * BOX), np.float32)
    table[lane, c * 128 + q * 16 + w] = 1.0
    return table.astype(ml_dtypes.bfloat16)


def plan_kernel(most, where, meta, offsets, table, chosen, used):
    region, sub, n_region = where[0], where[1], where[2]
    sign = 1 - 2 * (region & 1)
    next_region = jnp.where(region + 1 == n_region, 0, region + 1)
    for i in range(3 * len(PLACES)):
        used[i] = 0

    def place(pair, turn):
        own_slot = meta[pair]
        route = meta[PAIRS_DEV + pair]
        partner_slot = meta[2 * PAIRS_DEV + pair]
        abroad = route == N_SUB
        other = jnp.where(abroad, sub, route)
        dx = (sign * ((other >> 2) - (sub >> 2))) & 3
        dz = (sign * ((other & 3) - (sub & 3))) & 3
        delta = dx * GRID + dz
        count = jnp.where(abroad, 1, table[delta])

        @pl.when(jnp.where(count == 1, 0, 1) == turn)
        def _():
            row = pair * LIST_WIDTH
            for kind in range(3):
                best_load = jnp.int32(1 << 20)
                best_code = jnp.int32(0)
                best_count = jnp.int32(0)
                for k in range(most):
                    code = table[N_SUB + delta * most + k]
                    home_near = (code & 7) < FAR_PLACES[0]
                    source_near = ((code >> 3) & 7) < FAR_PLACES[0]
                    gives_near = (home_near & source_near, home_near, source_near)[kind]
                    rank = jnp.where(home_near & source_near, 0, jnp.where(gives_near, 1, 2))
                    counter = rank * len(PLACES) + (code & 7)
                    load = rank * 64 + used[counter]
                    better = load < best_load
                    best_load = jnp.where(better, load, best_load)
                    best_code = jnp.where(better, code, best_code)
                    best_count = jnp.where(better, counter, best_count)
                at = jnp.where(abroad, 0, best_code & 7)
                counter = jnp.where(abroad, 0, best_count)
                used[counter] = used[counter] + 1
                chosen[row + 2 * kind] = at
                chosen[row + 2 * kind + 1] = jnp.where(
                    abroad, REGION_SOURCE, (best_code >> 3) & 7
                )
            first = (region * N_SUB + sub) * ORB_DEV + own_slot
            second_region = jnp.where(abroad, next_region, region)
            second = (second_region * N_SUB + other) * ORB_DEV + partner_slot
            chosen[row + 6] = own_slot
            chosen[row + 7] = partner_slot
            for c in range(3):
                chosen[row + 8 + c] = offsets[first * 3 + c] - offsets[second * 3 + c]
            for c in range(11, LIST_WIDTH):
                chosen[row + c] = 0

    for turn in range(2):
        for pair in range(PAIRS_DEV):
            place(pair, turn)


def three_dots(high, low, weights, index):
    boxes_high = jnp.concatenate([high, low], axis=0)
    half = high.shape[0]
    wide = jnp.dot(boxes_high, weights[0, index], preferred_element_type=F32)
    rest = jnp.dot(high, weights[1, index], preferred_element_type=F32)
    return wide[:half] + wide[half:] + rest


def split(value):
    high = value.astype(BF16)
    return high, (value - high.astype(F32)).astype(BF16)


def six_points(x):
    u = [x[r] + x[r + 3] for r in range(3)]
    v = [x[r] - x[r + 3] for r in range(3)]
    return (
        u[0] + u[1] + u[2],
        v[0] - v[1] + v[2],
        v[0] + 0.5 * (v[1] - v[2]),
        -HALF_ROOT3 * (v[1] + v[2]),
        u[0] - 0.5 * (u[1] + u[2]),
        -HALF_ROOT3 * (u[1] - u[2]),
    )


def six_points_back(t0, t3, t1r, t1i, t2r, t2i):
    a0 = t0 + t2r
    t2h = t0 - 0.5 * t2r
    t2s = HALF_ROOT3 * t2i
    a1 = t2h - t2s
    a2 = t2h + t2s
    t1s = HALF_ROOT3 * t1i
    b0 = t3 + t1r
    b1 = 0.5 * t1r - t3 - t1s
    b2 = t3 - 0.5 * t1r - t1s
    return a0 + b0, a1 + b1, a2 + b2, a0 - b0, a1 - b1, a2 - b2


def three_points(x):
    total = x[1] + x[2]
    return x[0] + total, x[0] - 0.5 * total, -HALF_ROOT3 * (x[1] - x[2])


def three_points_back(s0, s1r, s1i):
    low = s0 - 0.5 * s1r
    turned = HALF_ROOT3 * s1i
    return s0 + s1r, low - turned, low + turned


def solve(density, both, work, waves, waves_back, green, rows, boxes):
    for b in range(boxes):
        for g in range(BOX // 16):
            some = pl.ds(b * BOX + g * 16, 16)
            low_some = pl.ds((boxes + b) * BOX + g * 16, 16)
            columns = []
            for c in range(BLOCKS_Z):
                x = [density(b, pl.ds(g * 16, 16), r, c) for r in range(BLOCKS_Y)]
                columns.append(six_points(x))
            t = [three_points([columns[c][j] for c in range(BLOCKS_Z)]) for j in range(6)]
            parts = [t[0][0], t[1][0], t[0][1], t[0][2], t[1][1], t[1][2]]
            parts += [t[2][0], t[3][0], t[4][0], t[5][0]]
            for j in (2, 4):
                (_, rr, ri), (_, ir, ii) = t[j], t[j + 1]
                parts += [rr - ii, ri + ir, rr + ii, ir - ri]
            for i, part in enumerate(parts):
                high, low = split(part)
                both[some, pl.ds(i * 128, 128)] = high
                both[low_some, pl.ds(i * 128, 128)] = low

    def row_pass(value):
        high, low = split(value)
        stacked = jnp.concatenate([high, high, low], axis=0)
        return jnp.dot(rows[...], stacked, preferred_element_type=F32)

    def plane_pass(weights):
        for group in range(9):
            lanes = pl.ds(group * 256, 256)
            high = both[pl.ds(0, boxes * BOX), lanes]
            low = both[pl.ds(boxes * BOX, boxes * BOX), lanes]
            work[:, lanes] = three_dots(high, low, weights, group)

    places = [
        (pl.ds(b * BOX, BOX), pl.ds((boxes + b) * BOX, BOX), pl.ds(group * 256, 256))
        for b in range(boxes)
        for group in range(9)
    ]
    plane_pass(waves)
    for some, _, lanes in places:
        work[some, lanes] = row_pass(work[some, lanes]) * green[:, lanes]
    for some, low_some, lanes in places:
        both[some, lanes], both[low_some, lanes] = split(row_pass(work[some, lanes]))
    plane_pass(waves_back)

    for b in range(boxes):
        for g in range(BOX // 16):
            some = pl.ds(b * BOX + g * 16, 16)
            p = [work[some, pl.ds(i * 128, 128)] for i in range(18)]
            t = [[p[0], p[2], p[3]], [p[1], p[4], p[5]]]
            for j in range(2):
                pr, pi, mr, mi = p[10 + 4 * j : 14 + 4 * j]
                t.append([p[6 + 2 * j], pr + mr, pi - mi])
                t.append([p[7 + 2 * j], pi + mi, mr - pr])
            t = [three_points_back(*parts) for parts in t]
            for c in range(BLOCKS_Z):
                values = six_points_back(*[t[j][c] for j in range(6)])
                for r, value in enumerate(values):
                    work[some, pl.ds((r * BLOCKS_Z + c) * 128, 128)] = value


def rounded(value):
    return value.astype(BF16).astype(F32)


def shift_box(padded, value, put, dx, dy, dz):
    for r in range(BLOCKS_Y):
        for c in range(BLOCKS_Z):
            at = ((r + SIDE_Y) * WIDE_Z + c + SIDE_Z) * ROWS_PADDED + MARGIN
            padded[pl.ds(at, BOX), :] = value(pl.ds((r * BLOCKS_Z + c) * 128, 128))
    fine_y, fine_z = dy & 7, dz & 15
    start = ((dy >> 3) + SIDE_Y) * WIDE_Z + (dz >> 4) + SIDE_Z
    base = start * ROWS_PADDED + MARGIN + dx
    lane = lax.broadcasted_iota(jnp.int32, (1, 128), 1)
    next_y = (lane >> 4) < fine_y
    next_z = (lane & 15) < fine_z
    carried = (lane & 15) + fine_z >= 16
    ahead = fine_y * 16 + fine_z
    turn = (128 - ahead) & 127
    turn_carried = (128 + 16 - ahead) & 127

    def block(r, c):
        return padded[pl.ds(base + (r * WIDE_Z + c) * ROWS_PADDED, BOX), :]

    for r in range(BLOCKS_Y):
        mixed = [jnp.where(next_y, block(r + 1, c), block(r, c)) for c in range(BLOCKS_Z + 1)]
        for c in range(BLOCKS_Z):
            source = jnp.where(next_z, mixed[c + 1], mixed[c])
            out = jnp.where(
                carried, pltpu.roll(source, turn_carried, 1), pltpu.roll(source, turn, 1)
            )
            put(pl.ds((r * BLOCKS_Z + c) * 128, 128), out)


def exchange_kernel(part, *refs):
    n_in = SETS * (4 if part == 0 else SOURCES)
    n_out = len(GIVEN[part])
    listing, *refs = refs
    boxes_in, refs = refs[:n_in], refs[n_in:]
    tables_in, refs = refs[:N_TABLES], refs[N_TABLES:]
    outs, refs = refs[:n_out], refs[n_out:]
    tables, refs = refs[:N_TABLES], refs[N_TABLES:]
    acc, stage, nothing, held, theirs, both, work, padded, *refs = refs
    mine, touched, sems, table_sems, out_sems = refs

    def is_far(source):
        return (source >= FAR_PLACES[0]) & (source <= FAR_PLACES[-1])

    mine[0] = 0
    for home in range(len(PLACES)):
        if part == 0 and home in FAR_PLACES:
            continue

        def check(pair, carry, home=home):
            row = (home * PAIRS_DEV + pair) * LIST_WIDTH
            for kind in range(3):
                source = listing[row + 2 * kind + 1]
                far = is_far(source)
                if part == 0:
                    now = jnp.logical_not(far)
                elif home in FAR_PLACES:
                    gives_far = far if kind == 2 else jnp.bool_(True)
                    now = gives_far if part == 1 else jnp.logical_not(gives_far)
                elif kind == 1:
                    now = far if part == 2 else jnp.bool_(False)
                else:
                    now = far if part == 1 else jnp.bool_(False)

                @pl.when((listing[row + 2 * kind] == home) & now)
                def _(kind=kind):
                    at = mine[0]
                    mine[0] = at + 1
                    task = (at + 1) * TASK_WIDTH
                    mine[task] = home
                    mine[task + 1] = listing[row + 2 * kind + 1]
                    for c in range(5):
                        mine[task + 2 + c] = listing[row + 6 + c]
                    mine[task + 7] = kind

            return carry

        lax.fori_loop(0, PAIRS_DEV, check, 0)

    count = mine[0]
    begin, end = 0, (count + 1) >> 1

    def table_copies():
        return [
            pltpu.make_async_copy(tables_in[i], tables[i], table_sems.at[i])
            for i in range(N_TABLES)
        ]

    def fetch(of_trial, source, slot, target, sem):
        row = pl.multiple_of(slot * BOX, 16)
        sources = [s for s in range(SOURCES) if part > 0 or s not in FAR_PLACES]
        code = source * 2 + jnp.where(of_trial, 1, 0)
        for at, s in enumerate(sources):
            for k in range(SETS):

                @pl.when(code == 2 * s + k)
                def _(ref=boxes_in[2 * at + k]):
                    pltpu.make_async_copy(ref.at[pl.ds(row, BOX)], target, sem).start()

    def each_load(step, act):
        for i in range(2):
            task = (step * 2 + i + 1) * TASK_WIDTH

            @pl.when(step * 2 + i < count)
            def _(i=i, task=task):
                kind = mine[task + 7]
                act(kind == 1, mine[task], mine[task + 2], 2 * i)
                act(kind == 2, mine[task + 1], mine[task + 3], 2 * i + 1)

    def start_loads(step, buffer):
        def act(of_trial, source, slot, i):
            fetch(of_trial, source, slot, held.at[buffer, i], sems.at[buffer, i])

        each_load(step, act)

    def wait_loads(step, buffer):
        def act(of_trial, source, slot, i):
            pltpu.make_async_copy(
                boxes_in[0].at[pl.ds(0, BOX)], held.at[buffer, i], sems.at[buffer, i]
            ).wait()

        each_load(step, act)

    def box_rows(i):
        return pl.ds(pl.multiple_of(i * BOX, BOX), BOX)

    def sum_slot(task, which, kind):
        of_set = jnp.where(kind == 0, 0, ORB_DEV)
        return mine[task + which] * SOURCE_SLOTS + of_set + mine[task + 2 + which]

    places = []
    for i, (source, low, size) in enumerate(GIVEN[part]):
        for k in range(size):
            places.append((source * SOURCE_SLOTS + low + k, i, pl.ds(k * BOX, BOX)))

    def keep(slot, i, some):
        return pltpu.make_async_copy(nothing, outs[i].at[some], out_sems.at[slot])

    def send(slot, i, some):
        return pltpu.make_async_copy(stage.at[box_rows(slot)], outs[i].at[some], out_sems.at[slot])

    @pl.when(begin < end)
    def _():
        start_loads(begin, begin & 1)
        for copy in table_copies():
            copy.start()

    for i in range(SOURCES * SOURCE_SLOTS):
        touched[i] = 0

    def mark(i, carry):
        task = (i + 1) * TASK_WIDTH
        kind = mine[task + 7]

        @pl.when(kind != 2)
        def _():
            touched[sum_slot(task, 0, kind)] = 1

        @pl.when(kind != 1)
        def _():
            touched[sum_slot(task, 1, kind)] = 1

        return carry

    lax.fori_loop(0, count, mark, 0)
    nothing[...] = jnp.zeros(nothing.shape, BF16)
    for place in places:

        @pl.when(touched[place[0]] == 0)
        def _(place=place):
            keep(*place).start()

    padded[...] = jnp.zeros(padded.shape, F32)

    def clear(i, carry):
        @pl.when(touched[i] == 1)
        def _():
            acc[box_rows(i), :] = jnp.zeros((BOX, PLANE), F32)

        return carry

    lax.fori_loop(0, SOURCES * SOURCE_SLOTS, clear, 0)

    def add(slot, lanes, value):
        at = box_rows(slot)
        acc[at, lanes] = acc[at, lanes] + value

    def one_step(step, carry):
        buffer = step & 1

        @pl.when(step + 1 < end)
        def _():
            start_loads(step + 1, 1 - buffer)

        wait_loads(step, buffer)
        for i in range(2):
            task = (step * 2 + i + 1) * TASK_WIDTH

            @pl.when(step * 2 + i < count)
            def _(i=i, task=task):
                def value(lanes):
                    return held[buffer, 2 * i + 1, :, lanes].astype(F32)

                def put(lanes, block):
                    theirs[i, :, lanes] = block

                shift_box(padded, value, put, mine[task + 4], mine[task + 5], mine[task + 6])

        @pl.when(step == begin)
        def _():
            for copy in table_copies():
                copy.wait()

        def density(b, some, r, c):
            lanes = pl.ds((r * BLOCKS_Z + c) * 128, 128)
            return held[buffer, 2 * b, some, lanes].astype(F32) * theirs[b, some, lanes]

        solve(density, both, work, *tables, 2)
        for i in range(2):
            task = (step * 2 + i + 1) * TASK_WIDTH
            there = step * 2 + i < count
            kind = mine[task + 7]

            @pl.when(there & (kind != 2))
            def _(i=i, task=task, kind=kind):
                near = rounded(work[pl.ds(i * BOX, BOX), :] * theirs[i])
                add(sum_slot(task, 0, kind), pl.ds(0, PLANE), near)

            @pl.when(there & (kind != 1))
            def _(i=i, task=task, kind=kind):
                slot = sum_slot(task, 1, kind)

                def value(lanes):
                    mine_box = held[buffer, 2 * i, :, lanes].astype(F32)
                    return rounded(work[pl.ds(i * BOX, BOX), lanes] * mine_box)

                def put(lanes, block):
                    add(slot, lanes, block)

                shift_box(padded, value, put, -mine[task + 4], -mine[task + 5], -mine[task + 6])

        return carry

    lax.fori_loop(begin, end, one_step, 0)

    def put(i, carry):
        @pl.when(touched[i] == 1)
        def _():
            some = box_rows(i)
            stage[some, :] = acc[some, :].astype(BF16)

        return carry

    lax.fori_loop(0, SOURCES * SOURCE_SLOTS, put, 0)
    for place in places:

        @pl.when(touched[place[0]] == 1)
        def _(place=place):
            send(*place).start()

    for place in places:
        send(*place).wait()


def exchange(part, listing, boxes, tables):
    any_space = pl.BlockSpec(memory_space=pl.ANY)
    smem = pl.BlockSpec(memory_space=pltpu.SMEM)
    outs = [
        jax.ShapeDtypeStruct((size * BOX, PLANE), BF16) for _, _, size in GIVEN[part]
    ]
    slots = SOURCES * SOURCE_SLOTS

    def kernel(*refs):
        exchange_kernel(part, *refs)

    return pl.pallas_call(
        kernel,
        out_shape=outs,
        in_specs=[smem] + [any_space] * (len(boxes) + len(tables)),
        out_specs=[any_space] * len(outs),
        scratch_shapes=[
            *[pltpu.VMEM(t.shape, t.dtype) for t in tables],
            pltpu.VMEM((slots * BOX, PLANE), F32),
            pltpu.VMEM((slots * BOX, PLANE), BF16),
            pltpu.VMEM((BOX, PLANE), BF16),
            pltpu.VMEM((2, 4, BOX, PLANE), BF16),
            pltpu.VMEM((2, BOX, PLANE), F32),
            pltpu.VMEM((4 * BOX, PLANE), BF16),
            pltpu.VMEM((2 * BOX, PLANE), F32),
            pltpu.VMEM((WIDE_Y * WIDE_Z * ROWS_PADDED, 128), F32),
            pltpu.SMEM(((MAX_TASKS + 3) * TASK_WIDTH,), jnp.int32),
            pltpu.SMEM((slots,), jnp.int32),
            pltpu.SemaphoreType.DMA((2, 4)),
            pltpu.SemaphoreType.DMA((N_TABLES,)),
            pltpu.SemaphoreType.DMA((slots,)),
        ],
        compiler_params=pltpu.CompilerParams(vmem_limit_bytes=56 * 1024 * 1024),
        cost_estimate=pl.CostEstimate(
            flops=15_000_000_000, bytes_accessed=30_000_000, transcendentals=0
        ),
        name=("near_tasks", "far_tasks", "other_tasks")[part],
    )(listing, *boxes, *tables)


def reorder_kernel(with_notes, box, *refs):
    order, out = refs[-2:]
    for r in range(BLOCKS_Y):
        lanes = pl.ds(r * CHUNK, CHUNK)
        moved = jnp.dot(box[:, lanes], order[...], preferred_element_type=F32)
        out[pl.ds(0, SET_ROWS), lanes] = moved.astype(BF16)
    if with_notes:
        out[pl.ds(SET_ROWS, NOTE_ROWS), :] = refs[0][...]


def reorder(boxes, order, notes=()):
    rows = SET_ROWS + NOTE_ROWS * len(notes)

    def kernel(*refs):
        reorder_kernel(bool(notes), *refs)

    return pl.pallas_call(
        kernel,
        out_shape=jax.ShapeDtypeStruct((rows, PLANE), BF16),
        name="reorder",
        compiler_params=pltpu.CompilerParams(vmem_limit_bytes=32 * 1024 * 1024),
    )(boxes, *notes, order)


def total_kernel(*refs):
    *parts, order, out = refs
    for r in range(BLOCKS_Y):
        lanes = pl.ds(r * CHUNK, CHUNK)
        result = parts[0][:, lanes].astype(F32)
        for part in parts[1:]:
            result += part[:, lanes].astype(F32)
        moved = jnp.dot((-result).astype(BF16), order[...], preferred_element_type=F32)
        out[:, lanes] = moved.astype(BF16)


def total(abroad, which, parts, order):
    half = SET_ROWS // 2
    whole = pl.BlockSpec((CHUNK, CHUNK), lambda i: (0, 0))
    some = pl.BlockSpec((half, PLANE), lambda i: (i, 0))
    first = pl.BlockSpec((half, PLANE), lambda i: (i + 2 * which, 0))
    return pl.pallas_call(
        total_kernel,
        grid=(2,),
        out_shape=jax.ShapeDtypeStruct((SET_ROWS, PLANE), BF16),
        in_specs=[first] + [some] * len(parts) + [whole],
        out_specs=some,
        name="total",
        compiler_params=pltpu.CompilerParams(vmem_limit_bytes=32 * 1024 * 1024),
    )(abroad, *parts, order)


def moves(n_region):
    def step(dx, dz):
        pairs = []
        for region in range(n_region):
            sign = 1 - 2 * (region % 2)
            for x in range(GRID):
                for z in range(GRID):
                    to = (x + sign * dx) % GRID * GRID + (z + sign * dz) % GRID
                    pairs.append((region * N_SUB + x * GRID + z, region * N_SUB + to))

        def move(block):
            return lax.ppermute(block, ("region", "sub"), pairs)

        return move

    def across(distance):
        pairs = [(i, (i + distance) % n_region) for i in range(n_region)]

        def move(block):
            return lax.ppermute(block, "region", pairs)

        return move

    return step, across


def per_device(orbitals, trial_set, own_slot, partner_route, partner_slot, offsets):
    n_region = lax.axis_size("region")
    region = lax.axis_index("region")
    sub = lax.axis_index("sub")
    step, across = moves(n_region)
    tables = transform_tables()
    tables = [
        jnp.asarray(tables[k])
        for k in TABLES
    ]
    order, order_back = jnp.asarray(order_table()), jnp.asarray(order_table().T.copy())
    table, most = meeting_table()
    meta = jnp.concatenate([own_slot, partner_route[:, 0], partner_slot])
    where = jnp.stack([region, sub, jnp.int32(n_region)]).astype(jnp.int32)
    smem = pl.BlockSpec(memory_space=pltpu.SMEM)

    def planner(*refs):
        plan_kernel(most, *refs)

    chosen = pl.pallas_call(
        planner,
        out_shape=jax.ShapeDtypeStruct((LISTED,), jnp.int32),
        in_specs=[smem] * 4,
        out_specs=smem,
        scratch_shapes=[pltpu.SMEM((3 * len(PLACES),), jnp.int32)],
        name="plan",
    )(where, meta, offsets.reshape(-1), jnp.asarray(table))

    ordered = lax.optimization_barrier
    notes = jnp.pad(chosen.astype(BF16)[None], ((0, NOTE_ROWS - 1), (0, PLANE - LISTED)))
    o00 = reorder(orbitals.reshape(SET_ROWS, PLANE), order, (notes,))
    o01, o10, o_abroad = step(0, 1)(o00), step(1, 0)(o00), across(-1)(o00)
    t00 = reorder(trial_set.reshape(SET_ROWS, PLANE), order)
    t01, t10, t_abroad = step(0, 1)(t00), step(1, 0)(t00), across(-1)(t00)
    o13, o31, o11 = step(0, -1)(o10), step(-1, 0)(o01), step(1, 0)(o01)
    t13, t31, t11 = step(0, -1)(t10), step(-1, 0)(t01), step(0, 1)(t10)

    def list_of(arrays):
        return jnp.concatenate([n[-NOTE_ROWS, :LISTED] for n in arrays]).astype(jnp.int32)

    near_boxes = [o00, t00, o01, t01, o10, t10]
    abroad = [o_abroad, t_abroad]
    near = exchange(0, list_of([o00, o01, o10]), near_boxes + abroad, tables)
    far_boxes = [o11, t11, o13, t13, o31, t31]
    near, far_boxes = ordered((near, far_boxes))
    listing = list_of([o00, o01, o10, far_boxes[0], far_boxes[2], far_boxes[4]])
    all_boxes = near_boxes + far_boxes + abroad
    far = exchange(1, listing, all_boxes, tables)
    far, listing, to_next = ordered((far, listing, near[6]))

    def one(a):
        return step(0, 1)(far[8 + a]), step(1, 0)(far[10 + a])

    r11 = [step(-1, 0)(far[6]), step(0, -1)(far[7])]
    r13, r31 = zip(one(0), one(1))
    r_abroad = across(1)(to_next)
    other = exchange(2, listing, all_boxes, tables)
    other, r11, r13, r31 = ordered((other, r11, r13, r31))

    def add_up(arrays):
        return sum(a.astype(F32) for a in arrays).astype(BF16)

    results = []
    for a in range(SETS):
        to_01 = [near[2 + a], far[2 + a], other[2 + a], r31[a]] + ([] if a else [r11[0]])
        to_10 = [near[4 + a], far[4 + a], other[4 + a], r13[a]] + ([r11[1]] if a else [])
        f01, f10 = step(0, -1)(add_up(to_01)), step(-1, 0)(add_up(to_10))
        result = total(r_abroad, a, [near[a], far[a], other[a], f01, f10], order_back)
        results.append(result.reshape(ORB_DEV, BOX, PLANE))
    return tuple(results)


def solution(mesh):
    in_specs = (
        P(("region", "sub"), None, None),
        P(("region", "sub"), None, None),
        P(("region", "sub")),
        P(("region", "sub"), None),
        P(("region", "sub")),
        P(),
    )
    out_specs = (P(("region", "sub"), None, None), P(("region", "sub"), None, None))
    return jax.shard_map(
        per_device, mesh=mesh, in_specs=in_specs, out_specs=out_specs, check_vma=False
    )
```

```python
import math

import jax
import jax.numpy as jnp
import ml_dtypes
import numpy as np
from jax import lax
from jax.experimental import pallas as pl
from jax.experimental.pallas import tpu as pltpu
from jax.sharding import PartitionSpec as P

BOX = 48
PLANE = BOX * BOX
CHUNK = PLANE // 6
SCREEN = 0.5
GRID = 4
N_SUB = GRID * GRID
ORB_DEV = 4
PAIRS_DEV = 4
N_PAIRS = N_SUB * PAIRS_DEV

PLACES = ((0, 0), (0, 1), (1, 0), (1, 1), (1, 3), (3, 1))
REGION_SOURCE = len(PLACES)
SOURCES = len(PLACES) + 1
LIST_WIDTH = 16
TASK_WIDTH = 8
LISTED = PAIRS_DEV * LIST_WIDTH
NOTE_ROWS = 16
SETS = 2
SET_ROWS = ORB_DEV * BOX
SOURCE_SLOTS = SETS * ORB_DEV
FAR_PLACES = (3, 4, 5)
GIVEN = (
    tuple((source, low, 4) for source in range(6) for low in (0, 4)),
    ((0, 0, 4), (0, 4, 4), (1, 0, 4), (1, 4, 4), (2, 0, 4), (2, 4, 4), (6, 0, 8)),
)
N_TABLES = 4
BLOCKS_Y = 6
BLOCKS_Z = 3
MARGIN = 24
ROWS_PADDED = BOX + 2 * MARGIN
SIDE_Y = 3
SIDE_Z = 2
WIDE_Y = BLOCKS_Y + 2 * SIDE_Y
WIDE_Z = BLOCKS_Z + 2 * SIDE_Z
MAX_TASKS = 3 * len(PLACES) * PAIRS_DEV
HALF_ROOT3 = math.sqrt(3.0) / 2.0
F32 = jnp.float32
BF16 = jnp.bfloat16


def meeting_table():
    found = [[] for _ in range(N_SUB)]
    for i, (ax, az) in enumerate(PLACES):
        for j, (bx, bz) in enumerate(PLACES):
            delta = (ax - bx) % GRID * GRID + (az - bz) % GRID
            found[delta].append(i + 8 * j)
    most = max(len(f) for f in found)
    codes = np.array([f + [f[-1]] * (most - len(f)) for f in found], np.int32)
    counts = np.array([len(f) for f in found], np.int32)
    return np.concatenate([counts, codes.reshape(-1)]), most


def high_low(matrix):
    high = matrix.astype(ml_dtypes.bfloat16)
    low = (matrix - high.astype(np.float64)).astype(ml_dtypes.bfloat16)
    return np.stack([high, low])


def cas(angles):
    return np.cos(angles) + np.sin(angles)


def transform_tables():
    turn = 2.0 * math.pi / BOX
    n = np.arange(BOX)
    line = cas(turn * (n[:, None] * n[None, :] % BOX))
    q, w = np.arange(8), np.arange(16)

    def angle_y(j):
        return turn * (q[:, None] * (6 * q[None, :] + j) % BOX)

    def angle_z(j):
        return turn * (w[:, None] * (3 * w[None, :] + j) % BOX)

    def both_parts(angle):
        c, s = np.cos(angle), np.sin(angle)
        return np.block([[c, -s], [s, c]])

    def planes(y, z, sign):
        whole = angle_y(y)[:, None, :, None] + sign * angle_z(z)[None, :, None, :]
        return both_parts(whole.reshape(128, 128))

    def real_complex(y):
        z = both_parts(angle_z(1)).reshape(2, 16, 2, 16)
        return np.einsum("qm,awbn->aqwbmn", cas(angle_y(y)), z).reshape(256, 256)

    def complex_real(y):
        return np.kron(both_parts(angle_y(y)), cas(angle_z(0)))

    zero = np.zeros((128, 128))
    real = [np.kron(cas(angle_y(y)), cas(angle_z(0))) for y in (0, 3)]
    waves = [np.block([[real[0], zero], [zero, real[1]]]), real_complex(0), real_complex(3)]
    waves += [complex_real(1), complex_real(2)]
    for y in (1, 2):
        waves += [planes(y, 1, 1), planes(y, 1, -1)]
    waves = np.stack(waves)
    lam = 4.0 * np.sin(math.pi * n / BOX) ** 2

    def spectrum(y, z, weight):
        ky, kz = 6 * q + y, 3 * w + z
        total = lam[:, None, None] + lam[ky][None, :, None] + lam[kz][None, None, :] + SCREEN
        return (weight * 4.0 * math.pi / total / float(BOX**3)).reshape(BOX, 128)

    order = [(0, 0, 1.0), (3, 0, 1.0)]
    for y, z in ((0, 1), (3, 1), (1, 0), (2, 0), (1, 1), (1, 1), (2, 1), (2, 1)):
        order += [(y, z, 2.0)] * 2
    green = np.concatenate([spectrum(*o) for o in order], axis=1)
    rows = high_low(line)
    rows = np.concatenate([rows[0], rows[1], rows[0]], axis=1)
    return dict(
        waves=high_low(waves),
        waves_back=high_low(waves.transpose(0, 2, 1)),
        green=green.astype(np.float32),
        rows=rows,
    )


TABLES = ("waves", "waves_back", "green", "rows")


def order_table():
    lane = np.arange(8 * BOX)
    q, c, w = lane // BOX, lane % BOX // 16, lane % 16
    table = np.zeros((8 * BOX, 8 * BOX), np.float32)
    table[lane, c * 128 + q * 16 + w] = 1.0
    return table.astype(ml_dtypes.bfloat16)


def plan_kernel(most, where, meta, offsets, table, chosen, used):
    region, sub, n_region = where[0], where[1], where[2]
    sign = 1 - 2 * (region & 1)
    next_region = jnp.where(region + 1 == n_region, 0, region + 1)
    for i in range(3 * len(PLACES)):
        used[i] = 0

    def place(pair, turn):
        own_slot = meta[pair]
        route = meta[PAIRS_DEV + pair]
        partner_slot = meta[2 * PAIRS_DEV + pair]
        abroad = route == N_SUB
        other = jnp.where(abroad, sub, route)
        dx = (sign * ((other >> 2) - (sub >> 2))) & 3
        dz = (sign * ((other & 3) - (sub & 3))) & 3
        delta = dx * GRID + dz
        count = jnp.where(abroad, 1, table[delta])

        @pl.when(jnp.where(count == 1, 0, 1) == turn)
        def _():
            row = pair * LIST_WIDTH
            for kind in range(3):
                best_load = jnp.int32(1 << 20)
                best_code = jnp.int32(0)
                best_count = jnp.int32(0)
                for k in range(most):
                    code = table[N_SUB + delta * most + k]
                    home_near = (code & 7) < FAR_PLACES[0]
                    source_near = ((code >> 3) & 7) < FAR_PLACES[0]
                    gives_near = (home_near & source_near, home_near, source_near)[kind]
                    rank = jnp.where(gives_near, 0, 1)
                    counter = rank * len(PLACES) + (code & 7)
                    load = rank * 64 + used[counter]
                    better = load < best_load
                    best_load = jnp.where(better, load, best_load)
                    best_code = jnp.where(better, code, best_code)
                    best_count = jnp.where(better, counter, best_count)
                at = jnp.where(abroad, 0, best_code & 7)
                counter = jnp.where(abroad, 0, best_count)
                used[counter] = used[counter] + 1
                chosen[row + 2 * kind] = at
                chosen[row + 2 * kind + 1] = jnp.where(
                    abroad, REGION_SOURCE, (best_code >> 3) & 7
                )
            first = (region * N_SUB + sub) * ORB_DEV + own_slot
            second_region = jnp.where(abroad, next_region, region)
            second = (second_region * N_SUB + other) * ORB_DEV + partner_slot
            chosen[row + 6] = own_slot
            chosen[row + 7] = partner_slot
            for c in range(3):
                chosen[row + 8 + c] = offsets[first * 3 + c] - offsets[second * 3 + c]
            for c in range(11, LIST_WIDTH):
                chosen[row + c] = 0

    for turn in range(2):
        for pair in range(PAIRS_DEV):
            place(pair, turn)


def three_dots(high, low, weights, index):
    boxes_high = jnp.concatenate([high, low], axis=0)
    half = high.shape[0]
    wide = jnp.dot(boxes_high, weights[0, index], preferred_element_type=F32)
    rest = jnp.dot(high, weights[1, index], preferred_element_type=F32)
    return wide[:half] + wide[half:] + rest


def split(value):
    high = value.astype(BF16)
    return high, (value - high.astype(F32)).astype(BF16)


def six_points(x):
    u = [x[r] + x[r + 3] for r in range(3)]
    v = [x[r] - x[r + 3] for r in range(3)]
    return (
        u[0] + u[1] + u[2],
        v[0] - v[1] + v[2],
        v[0] + 0.5 * (v[1] - v[2]),
        -HALF_ROOT3 * (v[1] + v[2]),
        u[0] - 0.5 * (u[1] + u[2]),
        -HALF_ROOT3 * (u[1] - u[2]),
    )


def six_points_back(t0, t3, t1r, t1i, t2r, t2i):
    a0 = t0 + t2r
    t2h = t0 - 0.5 * t2r
    t2s = HALF_ROOT3 * t2i
    a1 = t2h - t2s
    a2 = t2h + t2s
    t1s = HALF_ROOT3 * t1i
    b0 = t3 + t1r
    b1 = 0.5 * t1r - t3 - t1s
    b2 = t3 - 0.5 * t1r - t1s
    return a0 + b0, a1 + b1, a2 + b2, a0 - b0, a1 - b1, a2 - b2


def three_points(x):
    total = x[1] + x[2]
    return x[0] + total, x[0] - 0.5 * total, -HALF_ROOT3 * (x[1] - x[2])


def three_points_back(s0, s1r, s1i):
    low = s0 - 0.5 * s1r
    turned = HALF_ROOT3 * s1i
    return s0 + s1r, low - turned, low + turned


def solve(density, both, work, waves, waves_back, green, rows, boxes):
    for b in range(boxes):
        for g in range(BOX // 16):
            some = pl.ds(b * BOX + g * 16, 16)
            low_some = pl.ds((boxes + b) * BOX + g * 16, 16)
            columns = []
            for c in range(BLOCKS_Z):
                x = [density(b, pl.ds(g * 16, 16), r, c) for r in range(BLOCKS_Y)]
                columns.append(six_points(x))
            t = [three_points([columns[c][j] for c in range(BLOCKS_Z)]) for j in range(6)]
            parts = [t[0][0], t[1][0], t[0][1], t[0][2], t[1][1], t[1][2]]
            parts += [t[2][0], t[3][0], t[4][0], t[5][0]]
            for j in (2, 4):
                (_, rr, ri), (_, ir, ii) = t[j], t[j + 1]
                parts += [rr - ii, ri + ir, rr + ii, ir - ri]
            for i, part in enumerate(parts):
                high, low = split(part)
                both[some, pl.ds(i * 128, 128)] = high
                both[low_some, pl.ds(i * 128, 128)] = low

    def row_pass(value):
        high, low = split(value)
        stacked = jnp.concatenate([high, high, low], axis=0)
        return jnp.dot(rows[...], stacked, preferred_element_type=F32)

    def plane_pass(weights):
        for group in range(9):
            lanes = pl.ds(group * 256, 256)
            high = both[pl.ds(0, boxes * BOX), lanes]
            low = both[pl.ds(boxes * BOX, boxes * BOX), lanes]
            work[:, lanes] = three_dots(high, low, weights, group)

    places = [
        (pl.ds(b * BOX, BOX), pl.ds((boxes + b) * BOX, BOX), pl.ds(group * 256, 256))
        for b in range(boxes)
        for group in range(9)
    ]
    plane_pass(waves)
    for some, _, lanes in places:
        work[some, lanes] = row_pass(work[some, lanes]) * green[:, lanes]
    for some, low_some, lanes in places:
        both[some, lanes], both[low_some, lanes] = split(row_pass(work[some, lanes]))
    plane_pass(waves_back)

    for b in range(boxes):
        for g in range(BOX // 16):
            some = pl.ds(b * BOX + g * 16, 16)
            p = [work[some, pl.ds(i * 128, 128)] for i in range(18)]
            t = [[p[0], p[2], p[3]], [p[1], p[4], p[5]]]
            for j in range(2):
                pr, pi, mr, mi = p[10 + 4 * j : 14 + 4 * j]
                t.append([p[6 + 2 * j], pr + mr, pi - mi])
                t.append([p[7 + 2 * j], pi + mi, mr - pr])
            t = [three_points_back(*parts) for parts in t]
            for c in range(BLOCKS_Z):
                values = six_points_back(*[t[j][c] for j in range(6)])
                for r, value in enumerate(values):
                    work[some, pl.ds((r * BLOCKS_Z + c) * 128, 128)] = value


def rounded(value):
    return value.astype(BF16).astype(F32)


def shift_box(padded, value, put, dx, dy, dz):
    for r in range(BLOCKS_Y):
        for c in range(BLOCKS_Z):
            at = ((r + SIDE_Y) * WIDE_Z + c + SIDE_Z) * ROWS_PADDED + MARGIN
            padded[pl.ds(at, BOX), :] = value(pl.ds((r * BLOCKS_Z + c) * 128, 128))
    fine_y, fine_z = dy & 7, dz & 15
    start = ((dy >> 3) + SIDE_Y) * WIDE_Z + (dz >> 4) + SIDE_Z
    base = start * ROWS_PADDED + MARGIN + dx
    lane = lax.broadcasted_iota(jnp.int32, (1, 128), 1)
    next_y = (lane >> 4) < fine_y
    next_z = (lane & 15) < fine_z
    carried = (lane & 15) + fine_z >= 16
    ahead = fine_y * 16 + fine_z
    turn = (128 - ahead) & 127
    turn_carried = (128 + 16 - ahead) & 127

    def block(r, c):
        return padded[pl.ds(base + (r * WIDE_Z + c) * ROWS_PADDED, BOX), :]

    for r in range(BLOCKS_Y):
        mixed = [jnp.where(next_y, block(r + 1, c), block(r, c)) for c in range(BLOCKS_Z + 1)]
        for c in range(BLOCKS_Z):
            source = jnp.where(next_z, mixed[c + 1], mixed[c])
            out = jnp.where(
                carried, pltpu.roll(source, turn_carried, 1), pltpu.roll(source, turn, 1)
            )
            put(pl.ds((r * BLOCKS_Z + c) * 128, 128), out)


def exchange_kernel(part, *refs):
    n_in = SETS * SOURCES
    n_out = len(GIVEN[part])
    listing, *refs = refs
    boxes_in, refs = refs[:n_in], refs[n_in:]
    tables_in, refs = refs[:N_TABLES], refs[N_TABLES:]
    outs, refs = refs[:n_out], refs[n_out:]
    tables, refs = refs[:N_TABLES], refs[N_TABLES:]
    acc, stage, nothing, held, theirs, both, work, padded, *refs = refs
    mine, touched, sems, table_sems, out_sems = refs

    def is_far(source):
        return (source >= FAR_PLACES[0]) & (source <= FAR_PLACES[-1])

    mine[0] = 0
    for home in range(len(PLACES)):
        def check(pair, carry, home=home):
            row = (home * PAIRS_DEV + pair) * LIST_WIDTH
            for kind in range(3):
                source = listing[row + 2 * kind + 1]
                far = is_far(source)
                gives_far = far if kind != 1 else jnp.bool_(False)
                if home in FAR_PLACES and kind != 2:
                    gives_far = jnp.bool_(True)
                now = gives_far if part == 0 else jnp.logical_not(gives_far)

                @pl.when((listing[row + 2 * kind] == home) & now)
                def _(kind=kind):
                    at = mine[0]
                    mine[0] = at + 1
                    task = (at + 1) * TASK_WIDTH
                    mine[task] = home
                    mine[task + 1] = listing[row + 2 * kind + 1]
                    for c in range(5):
                        mine[task + 2 + c] = listing[row + 6 + c]
                    mine[task + 7] = kind

            return carry

        lax.fori_loop(0, PAIRS_DEV, check, 0)

    count = mine[0]
    begin, end = 0, (count + 1) >> 1

    def table_copies():
        return [
            pltpu.make_async_copy(tables_in[i], tables[i], table_sems.at[i])
            for i in range(N_TABLES)
        ]

    def fetch(of_trial, source, slot, target, sem):
        row = pl.multiple_of(slot * BOX, 16)
        code = source * 2 + jnp.where(of_trial, 1, 0)
        for s in range(SOURCES):
            for k in range(SETS):

                @pl.when(code == 2 * s + k)
                def _(ref=boxes_in[2 * s + k]):
                    pltpu.make_async_copy(ref.at[pl.ds(row, BOX)], target, sem).start()

    def each_load(step, act):
        for i in range(2):
            task = (step * 2 + i + 1) * TASK_WIDTH

            @pl.when(step * 2 + i < count)
            def _(i=i, task=task):
                kind = mine[task + 7]
                act(kind == 1, mine[task], mine[task + 2], 2 * i)
                act(kind == 2, mine[task + 1], mine[task + 3], 2 * i + 1)

    def start_loads(step, buffer):
        def act(of_trial, source, slot, i):
            fetch(of_trial, source, slot, held.at[buffer, i], sems.at[buffer, i])

        each_load(step, act)

    def wait_loads(step, buffer):
        def act(of_trial, source, slot, i):
            pltpu.make_async_copy(
                boxes_in[0].at[pl.ds(0, BOX)], held.at[buffer, i], sems.at[buffer, i]
            ).wait()

        each_load(step, act)

    def box_rows(i):
        return pl.ds(pl.multiple_of(i * BOX, BOX), BOX)

    def sum_slot(task, which, kind):
        of_set = jnp.where(kind == 0, 0, ORB_DEV)
        return mine[task + which] * SOURCE_SLOTS + of_set + mine[task + 2 + which]

    places = []
    for i, (source, low, size) in enumerate(GIVEN[part]):
        for k in range(size):
            places.append((source * SOURCE_SLOTS + low + k, i, pl.ds(k * BOX, BOX)))

    def keep(slot, i, some):
        return pltpu.make_async_copy(nothing, outs[i].at[some], out_sems.at[slot])

    def send(slot, i, some):
        return pltpu.make_async_copy(stage.at[box_rows(slot)], outs[i].at[some], out_sems.at[slot])

    @pl.when(begin < end)
    def _():
        start_loads(begin, begin & 1)
        for copy in table_copies():
            copy.start()

    for i in range(SOURCES * SOURCE_SLOTS):
        touched[i] = 0

    def mark(i, carry):
        task = (i + 1) * TASK_WIDTH
        kind = mine[task + 7]

        @pl.when(kind != 2)
        def _():
            touched[sum_slot(task, 0, kind)] = 1

        @pl.when(kind != 1)
        def _():
            touched[sum_slot(task, 1, kind)] = 1

        return carry

    lax.fori_loop(0, count, mark, 0)
    nothing[...] = jnp.zeros(nothing.shape, BF16)
    for place in places:

        @pl.when(touched[place[0]] == 0)
        def _(place=place):
            keep(*place).start()

    padded[...] = jnp.zeros(padded.shape, F32)

    def clear(i, carry):
        @pl.when(touched[i] == 1)
        def _():
            acc[box_rows(i), :] = jnp.zeros((BOX, PLANE), F32)

        return carry

    lax.fori_loop(0, SOURCES * SOURCE_SLOTS, clear, 0)

    def add(slot, lanes, value):
        at = box_rows(slot)
        acc[at, lanes] = acc[at, lanes] + value

    def one_step(step, carry):
        buffer = step & 1

        @pl.when(step + 1 < end)
        def _():
            start_loads(step + 1, 1 - buffer)

        wait_loads(step, buffer)
        for i in range(2):
            task = (step * 2 + i + 1) * TASK_WIDTH

            @pl.when(step * 2 + i < count)
            def _(i=i, task=task):
                def value(lanes):
                    return held[buffer, 2 * i + 1, :, lanes].astype(F32)

                def put(lanes, block):
                    theirs[i, :, lanes] = block

                shift_box(padded, value, put, mine[task + 4], mine[task + 5], mine[task + 6])

        @pl.when(step == begin)
        def _():
            for copy in table_copies():
                copy.wait()

        def density(b, some, r, c):
            lanes = pl.ds((r * BLOCKS_Z + c) * 128, 128)
            return held[buffer, 2 * b, some, lanes].astype(F32) * theirs[b, some, lanes]

        solve(density, both, work, *tables, 2)
        for i in range(2):
            task = (step * 2 + i + 1) * TASK_WIDTH
            there = step * 2 + i < count
            kind = mine[task + 7]

            @pl.when(there & (kind != 2))
            def _(i=i, task=task, kind=kind):
                near = rounded(work[pl.ds(i * BOX, BOX), :] * theirs[i])
                add(sum_slot(task, 0, kind), pl.ds(0, PLANE), near)

            @pl.when(there & (kind != 1))
            def _(i=i, task=task, kind=kind):
                slot = sum_slot(task, 1, kind)

                def value(lanes):
                    mine_box = held[buffer, 2 * i, :, lanes].astype(F32)
                    return rounded(work[pl.ds(i * BOX, BOX), lanes] * mine_box)

                def put(lanes, block):
                    add(slot, lanes, block)

                shift_box(padded, value, put, -mine[task + 4], -mine[task + 5], -mine[task + 6])

        return carry

    lax.fori_loop(begin, end, one_step, 0)

    def put(i, carry):
        @pl.when(touched[i] == 1)
        def _():
            some = box_rows(i)
            stage[some, :] = acc[some, :].astype(BF16)

        return carry

    lax.fori_loop(0, SOURCES * SOURCE_SLOTS, put, 0)
    for place in places:

        @pl.when(touched[place[0]] == 1)
        def _(place=place):
            send(*place).start()

    for place in places:
        send(*place).wait()


def exchange(part, listing, boxes, tables):
    any_space = pl.BlockSpec(memory_space=pl.ANY)
    smem = pl.BlockSpec(memory_space=pltpu.SMEM)
    outs = [
        jax.ShapeDtypeStruct((size * BOX, PLANE), BF16) for _, _, size in GIVEN[part]
    ]
    slots = SOURCES * SOURCE_SLOTS

    def kernel(*refs):
        exchange_kernel(part, *refs)

    return pl.pallas_call(
        kernel,
        out_shape=outs,
        in_specs=[smem] + [any_space] * (len(boxes) + len(tables)),
        out_specs=[any_space] * len(outs),
        scratch_shapes=[
            *[pltpu.VMEM(t.shape, t.dtype) for t in tables],
            pltpu.VMEM((slots * BOX, PLANE), F32),
            pltpu.VMEM((slots * BOX, PLANE), BF16),
            pltpu.VMEM((BOX, PLANE), BF16),
            pltpu.VMEM((2, 4, BOX, PLANE), BF16),
            pltpu.VMEM((2, BOX, PLANE), F32),
            pltpu.VMEM((4 * BOX, PLANE), BF16),
            pltpu.VMEM((2 * BOX, PLANE), F32),
            pltpu.VMEM((WIDE_Y * WIDE_Z * ROWS_PADDED, 128), F32),
            pltpu.SMEM(((MAX_TASKS + 3) * TASK_WIDTH,), jnp.int32),
            pltpu.SMEM((slots,), jnp.int32),
            pltpu.SemaphoreType.DMA((2, 4)),
            pltpu.SemaphoreType.DMA((N_TABLES,)),
            pltpu.SemaphoreType.DMA((slots,)),
        ],
        compiler_params=pltpu.CompilerParams(vmem_limit_bytes=56 * 1024 * 1024),
        cost_estimate=pl.CostEstimate(
            flops=15_000_000_000, bytes_accessed=30_000_000, transcendentals=0
        ),
        name=("far_tasks", "other_tasks")[part],
    )(listing, *boxes, *tables)


def reorder_kernel(with_notes, box, *refs):
    order, out = refs[-2:]
    for r in range(BLOCKS_Y):
        lanes = pl.ds(r * CHUNK, CHUNK)
        moved = jnp.dot(box[:, lanes], order[...], preferred_element_type=F32)
        out[pl.ds(0, SET_ROWS), lanes] = moved.astype(BF16)
    if with_notes:
        out[pl.ds(SET_ROWS, NOTE_ROWS), :] = refs[0][...]


def reorder(boxes, order, notes=()):
    rows = SET_ROWS + NOTE_ROWS * len(notes)

    def kernel(*refs):
        reorder_kernel(bool(notes), *refs)

    return pl.pallas_call(
        kernel,
        out_shape=jax.ShapeDtypeStruct((rows, PLANE), BF16),
        name="reorder",
        compiler_params=pltpu.CompilerParams(vmem_limit_bytes=32 * 1024 * 1024),
    )(boxes, *notes, order)


def total_kernel(*refs):
    *parts, order, out = refs
    for r in range(BLOCKS_Y):
        lanes = pl.ds(r * CHUNK, CHUNK)
        result = parts[0][:, lanes].astype(F32)
        for part in parts[1:]:
            result += part[:, lanes].astype(F32)
        moved = jnp.dot((-result).astype(BF16), order[...], preferred_element_type=F32)
        out[:, lanes] = moved.astype(BF16)


def total(abroad, which, parts, order):
    half = SET_ROWS // 2
    whole = pl.BlockSpec((CHUNK, CHUNK), lambda i: (0, 0))
    some = pl.BlockSpec((half, PLANE), lambda i: (i, 0))
    first = pl.BlockSpec((half, PLANE), lambda i: (i + 2 * which, 0))
    return pl.pallas_call(
        total_kernel,
        grid=(2,),
        out_shape=jax.ShapeDtypeStruct((SET_ROWS, PLANE), BF16),
        in_specs=[first] + [some] * len(parts) + [whole],
        out_specs=some,
        name="total",
        compiler_params=pltpu.CompilerParams(vmem_limit_bytes=32 * 1024 * 1024),
    )(abroad, *parts, order)


def moves(n_region):
    def step(dx, dz):
        pairs = []
        for region in range(n_region):
            sign = 1 - 2 * (region % 2)
            for x in range(GRID):
                for z in range(GRID):
                    to = (x + sign * dx) % GRID * GRID + (z + sign * dz) % GRID
                    pairs.append((region * N_SUB + x * GRID + z, region * N_SUB + to))

        def move(block):
            return lax.ppermute(block, ("region", "sub"), pairs)

        return move

    def across(distance):
        pairs = [(i, (i + distance) % n_region) for i in range(n_region)]

        def move(block):
            return lax.ppermute(block, "region", pairs)

        return move

    return step, across


def per_device(orbitals, trial_set, own_slot, partner_route, partner_slot, offsets):
    n_region = lax.axis_size("region")
    region = lax.axis_index("region")
    sub = lax.axis_index("sub")
    step, across = moves(n_region)
    tables = transform_tables()
    tables = [
        jnp.asarray(tables[k])
        for k in TABLES
    ]
    order, order_back = jnp.asarray(order_table()), jnp.asarray(order_table().T.copy())
    table, most = meeting_table()
    meta = jnp.concatenate([own_slot, partner_route[:, 0], partner_slot])
    where = jnp.stack([region, sub, jnp.int32(n_region)]).astype(jnp.int32)
    smem = pl.BlockSpec(memory_space=pltpu.SMEM)

    def planner(*refs):
        plan_kernel(most, *refs)

    chosen = pl.pallas_call(
        planner,
        out_shape=jax.ShapeDtypeStruct((LISTED,), jnp.int32),
        in_specs=[smem] * 4,
        out_specs=smem,
        scratch_shapes=[pltpu.SMEM((3 * len(PLACES),), jnp.int32)],
        name="plan",
    )(where, meta, offsets.reshape(-1), jnp.asarray(table))

    ordered = lax.optimization_barrier
    notes = jnp.pad(chosen.astype(BF16)[None], ((0, NOTE_ROWS - 1), (0, PLANE - LISTED)))
    o00 = reorder(orbitals.reshape(SET_ROWS, PLANE), order, (notes,))
    o01, o10, o_abroad = step(0, 1)(o00), step(1, 0)(o00), across(-1)(o00)
    t00 = reorder(trial_set.reshape(SET_ROWS, PLANE), order)
    t01, t10, t_abroad = step(0, 1)(t00), step(1, 0)(t00), across(-1)(t00)
    o13, o31, o11 = step(0, -1)(o10), step(-1, 0)(o01), step(1, 0)(o01)
    t13, t31, t11 = step(0, -1)(t10), step(-1, 0)(t01), step(0, 1)(t10)

    def list_of(arrays):
        return jnp.concatenate([n[-NOTE_ROWS, :LISTED] for n in arrays]).astype(jnp.int32)

    listing = list_of([o00, o01, o10, o11, o13, o31])
    all_boxes = [o00, t00, o01, t01, o10, t10, o11, t11, o13, t13, o31, t31, o_abroad, t_abroad]
    far = exchange(0, listing, all_boxes, tables)
    far, listing = ordered((far, listing))

    def one(a):
        return step(0, 1)(far[8 + a]), step(1, 0)(far[10 + a])

    r11 = [step(-1, 0)(far[6]), step(0, -1)(far[7])]
    r13, r31 = zip(one(0), one(1))
    other = exchange(1, listing, all_boxes, tables)
    other, r11, r13, r31 = ordered((other, r11, r13, r31))
    r_abroad = across(1)(other[6])

    def add_up(arrays):
        return sum(a.astype(F32) for a in arrays).astype(BF16)

    results = []
    for a in range(SETS):
        to_01 = [far[2 + a], other[2 + a], r31[a]] + ([] if a else [r11[0]])
        to_10 = [far[4 + a], other[4 + a], r13[a]] + ([r11[1]] if a else [])
        f01, f10 = step(0, -1)(add_up(to_01)), step(-1, 0)(add_up(to_10))
        result = total(r_abroad, a, [far[a], other[a], f01, f10], order_back)
        results.append(result.reshape(ORB_DEV, BOX, PLANE))
    return tuple(results)


def solution(mesh):
    in_specs = (
        P(("region", "sub"), None, None),
        P(("region", "sub"), None, None),
        P(("region", "sub")),
        P(("region", "sub"), None),
        P(("region", "sub")),
        P(),
    )
    out_specs = (P(("region", "sub"), None, None), P(("region", "sub"), None, None))
    return jax.shard_map(
        per_device, mesh=mesh, in_specs=in_specs, out_specs=out_specs, check_vma=False
    )
```

```python
import math

import jax
import jax.numpy as jnp
import ml_dtypes
import numpy as np
from jax import lax
from jax.experimental import pallas as pl
from jax.experimental.pallas import tpu as pltpu
from jax.sharding import PartitionSpec as P

BOX = 48
PLANE = BOX * BOX
CHUNK = PLANE // 6
SCREEN = 0.5
GRID = 4
N_SUB = GRID * GRID
ORB_DEV = 4
PAIRS_DEV = 4
N_PAIRS = N_SUB * PAIRS_DEV

PLACES = ((0, 0), (0, 1), (1, 0), (1, 1), (1, 3), (3, 1))
REGION_SOURCE = len(PLACES)
SOURCES = len(PLACES) + 1
LIST_WIDTH = 16
TASK_WIDTH = 8
LISTED = PAIRS_DEV * LIST_WIDTH
NOTE_ROWS = 16
SETS = 2
SET_ROWS = ORB_DEV * BOX
SOURCE_SLOTS = SETS * ORB_DEV
FAR_PLACES = (3, 4, 5)
GIVEN = (
    tuple((source, low, 4) for source in range(6) for low in (0, 4)) + ((6, 0, 8),),
    tuple((source, low, 4) for source in range(3) for low in (0, 4)),
)
N_TABLES = 4
BLOCKS_Y = 6
BLOCKS_Z = 3
MARGIN = 24
ROWS_PADDED = BOX + 2 * MARGIN
SIDE_Y = 3
SIDE_Z = 2
WIDE_Y = BLOCKS_Y + 2 * SIDE_Y
WIDE_Z = BLOCKS_Z + 2 * SIDE_Z
MAX_TASKS = 3 * len(PLACES) * PAIRS_DEV
HALF_ROOT3 = math.sqrt(3.0) / 2.0
F32 = jnp.float32
BF16 = jnp.bfloat16


def meeting_table():
    found = [[] for _ in range(N_SUB)]
    for i, (ax, az) in enumerate(PLACES):
        for j, (bx, bz) in enumerate(PLACES):
            delta = (ax - bx) % GRID * GRID + (az - bz) % GRID
            found[delta].append(i + 8 * j)
    most = max(len(f) for f in found)
    codes = np.array([f + [f[-1]] * (most - len(f)) for f in found], np.int32)
    counts = np.array([len(f) for f in found], np.int32)
    return np.concatenate([counts, codes.reshape(-1)]), most


def high_low(matrix):
    high = matrix.astype(ml_dtypes.bfloat16)
    low = (matrix - high.astype(np.float64)).astype(ml_dtypes.bfloat16)
    return np.stack([high, low])


def cas(angles):
    return np.cos(angles) + np.sin(angles)


def transform_tables():
    turn = 2.0 * math.pi / BOX
    n = np.arange(BOX)
    line = cas(turn * (n[:, None] * n[None, :] % BOX))
    q, w = np.arange(8), np.arange(16)

    def angle_y(j):
        return turn * (q[:, None] * (6 * q[None, :] + j) % BOX)

    def angle_z(j):
        return turn * (w[:, None] * (3 * w[None, :] + j) % BOX)

    def both_parts(angle):
        c, s = np.cos(angle), np.sin(angle)
        return np.block([[c, -s], [s, c]])

    def planes(y, z, sign):
        whole = angle_y(y)[:, None, :, None] + sign * angle_z(z)[None, :, None, :]
        return both_parts(whole.reshape(128, 128))

    def real_complex(y):
        z = both_parts(angle_z(1)).reshape(2, 16, 2, 16)
        return np.einsum("qm,awbn->aqwbmn", cas(angle_y(y)), z).reshape(256, 256)

    def complex_real(y):
        return np.kron(both_parts(angle_y(y)), cas(angle_z(0)))

    zero = np.zeros((128, 128))
    real = [np.kron(cas(angle_y(y)), cas(angle_z(0))) for y in (0, 3)]
    waves = [np.block([[real[0], zero], [zero, real[1]]]), real_complex(0), real_complex(3)]
    waves += [complex_real(1), complex_real(2)]
    for y in (1, 2):
        waves += [planes(y, 1, 1), planes(y, 1, -1)]
    waves = np.stack(waves)
    lam = 4.0 * np.sin(math.pi * n / BOX) ** 2

    def spectrum(y, z, weight):
        ky, kz = 6 * q + y, 3 * w + z
        total = lam[:, None, None] + lam[ky][None, :, None] + lam[kz][None, None, :] + SCREEN
        return (weight * 4.0 * math.pi / total / float(BOX**3)).reshape(BOX, 128)

    order = [(0, 0, 1.0), (3, 0, 1.0)]
    for y, z in ((0, 1), (3, 1), (1, 0), (2, 0), (1, 1), (1, 1), (2, 1), (2, 1)):
        order += [(y, z, 2.0)] * 2
    green = np.concatenate([spectrum(*o) for o in order], axis=1)
    rows = high_low(line)
    rows = np.block([[rows[0], rows[0]], [rows[1], np.zeros_like(rows[1])]])
    return dict(
        waves=high_low(waves),
        waves_back=high_low(waves.transpose(0, 2, 1)),
        green=green.astype(np.float32),
        rows=rows,
    )


TABLES = ("waves", "waves_back", "green", "rows")


def order_table():
    lane = np.arange(8 * BOX)
    q, c, w = lane // BOX, lane % BOX // 16, lane % 16
    table = np.zeros((8 * BOX, 8 * BOX), np.float32)
    table[lane, c * 128 + q * 16 + w] = 1.0
    return table.astype(ml_dtypes.bfloat16)


def plan_kernel(most, where, meta, offsets, table, chosen, used):
    region, sub, n_region = where[0], where[1], where[2]
    sign = 1 - 2 * (region & 1)
    next_region = jnp.where(region + 1 == n_region, 0, region + 1)
    for i in range(3 * len(PLACES)):
        used[i] = 0

    def place(pair, turn):
        own_slot = meta[pair]
        route = meta[PAIRS_DEV + pair]
        partner_slot = meta[2 * PAIRS_DEV + pair]
        abroad = route == N_SUB
        other = jnp.where(abroad, sub, route)
        dx = (sign * ((other >> 2) - (sub >> 2))) & 3
        dz = (sign * ((other & 3) - (sub & 3))) & 3
        delta = dx * GRID + dz
        count = jnp.where(abroad, 1, table[delta])

        @pl.when(jnp.where(count == 1, 0, 1) == turn)
        def _():
            row = pair * LIST_WIDTH
            for kind in range(3):
                best_load = jnp.int32(1 << 20)
                best_code = jnp.int32(0)
                best_count = jnp.int32(0)
                for k in range(most):
                    code = table[N_SUB + delta * most + k]
                    home_near = (code & 7) < FAR_PLACES[0]
                    source_near = ((code >> 3) & 7) < FAR_PLACES[0]
                    gives_near = (home_near & source_near, home_near, source_near)[kind]
                    rank = jnp.where(gives_near, 0, 1)
                    counter = rank * len(PLACES) + (code & 7)
                    load = rank * 64 + used[counter]
                    better = load < best_load
                    best_load = jnp.where(better, load, best_load)
                    best_code = jnp.where(better, code, best_code)
                    best_count = jnp.where(better, counter, best_count)
                at = jnp.where(abroad, 0, best_code & 7)
                counter = jnp.where(abroad, 0, best_count)
                used[counter] = used[counter] + 1
                chosen[row + 2 * kind] = at
                chosen[row + 2 * kind + 1] = jnp.where(
                    abroad, REGION_SOURCE, (best_code >> 3) & 7
                )
            first = (region * N_SUB + sub) * ORB_DEV + own_slot
            second_region = jnp.where(abroad, next_region, region)
            second = (second_region * N_SUB + other) * ORB_DEV + partner_slot
            chosen[row + 6] = own_slot
            chosen[row + 7] = partner_slot
            for c in range(3):
                chosen[row + 8 + c] = offsets[first * 3 + c] - offsets[second * 3 + c]
            for c in range(11, LIST_WIDTH):
                chosen[row + c] = 0

    for turn in range(2):
        for pair in range(PAIRS_DEV):
            place(pair, turn)


def three_dots(high, low, weights, index):
    boxes_high = jnp.concatenate([high, low], axis=0)
    half = high.shape[0]
    wide = jnp.dot(boxes_high, weights[0, index], preferred_element_type=F32)
    rest = jnp.dot(high, weights[1, index], preferred_element_type=F32)
    return wide[:half] + wide[half:] + rest


def split(value):
    high = value.astype(BF16)
    return high, (value - high.astype(F32)).astype(BF16)


def six_points(x):
    u = [x[r] + x[r + 3] for r in range(3)]
    v = [x[r] - x[r + 3] for r in range(3)]
    return (
        u[0] + u[1] + u[2],
        v[0] - v[1] + v[2],
        v[0] + 0.5 * (v[1] - v[2]),
        -HALF_ROOT3 * (v[1] + v[2]),
        u[0] - 0.5 * (u[1] + u[2]),
        -HALF_ROOT3 * (u[1] - u[2]),
    )


def six_points_back(t0, t3, t1r, t1i, t2r, t2i):
    a0 = t0 + t2r
    t2h = t0 - 0.5 * t2r
    t2s = HALF_ROOT3 * t2i
    a1 = t2h - t2s
    a2 = t2h + t2s
    t1s = HALF_ROOT3 * t1i
    b0 = t3 + t1r
    b1 = 0.5 * t1r - t3 - t1s
    b2 = t3 - 0.5 * t1r - t1s
    return a0 + b0, a1 + b1, a2 + b2, a0 - b0, a1 - b1, a2 - b2


def three_points(x):
    total = x[1] + x[2]
    return x[0] + total, x[0] - 0.5 * total, -HALF_ROOT3 * (x[1] - x[2])


def three_points_back(s0, s1r, s1i):
    low = s0 - 0.5 * s1r
    turned = HALF_ROOT3 * s1i
    return s0 + s1r, low - turned, low + turned


def solve(density, both, work, waves, waves_back, green, rows, boxes):
    for b in range(boxes):
        for g in range(BOX // 16):
            some = pl.ds(b * BOX + g * 16, 16)
            low_some = pl.ds((boxes + b) * BOX + g * 16, 16)
            columns = []
            for c in range(BLOCKS_Z):
                x = [density(b, pl.ds(g * 16, 16), r, c) for r in range(BLOCKS_Y)]
                columns.append(six_points(x))
            t = [three_points([columns[c][j] for c in range(BLOCKS_Z)]) for j in range(6)]
            parts = [t[0][0], t[1][0], t[0][1], t[0][2], t[1][1], t[1][2]]
            parts += [t[2][0], t[3][0], t[4][0], t[5][0]]
            for j in (2, 4):
                (_, rr, ri), (_, ir, ii) = t[j], t[j + 1]
                parts += [rr - ii, ri + ir, rr + ii, ir - ri]
            for i, part in enumerate(parts):
                high, low = split(part)
                both[some, pl.ds(i * 128, 128)] = high
                both[low_some, pl.ds(i * 128, 128)] = low

    def row_pass(value):
        stacked = jnp.concatenate(split(value), axis=0)
        result = jnp.dot(rows[...], stacked, preferred_element_type=F32)
        return result[:BOX] + result[BOX:]

    def plane_pass(weights):
        for group in range(9):
            lanes = pl.ds(group * 256, 256)
            high = both[pl.ds(0, boxes * BOX), lanes]
            low = both[pl.ds(boxes * BOX, boxes * BOX), lanes]
            work[:, lanes] = three_dots(high, low, weights, group)

    places = [
        (pl.ds(b * BOX, BOX), pl.ds((boxes + b) * BOX, BOX), pl.ds(group * 256, 256))
        for b in range(boxes)
        for group in range(9)
    ]
    plane_pass(waves)
    for some, _, lanes in places:
        work[some, lanes] = row_pass(work[some, lanes]) * green[:, lanes]
    for some, low_some, lanes in places:
        both[some, lanes], both[low_some, lanes] = split(row_pass(work[some, lanes]))
    plane_pass(waves_back)

    for b in range(boxes):
        for g in range(BOX // 16):
            some = pl.ds(b * BOX + g * 16, 16)
            p = [work[some, pl.ds(i * 128, 128)] for i in range(18)]
            t = [[p[0], p[2], p[3]], [p[1], p[4], p[5]]]
            for j in range(2):
                pr, pi, mr, mi = p[10 + 4 * j : 14 + 4 * j]
                t.append([p[6 + 2 * j], pr + mr, pi - mi])
                t.append([p[7 + 2 * j], pi + mi, mr - pr])
            t = [three_points_back(*parts) for parts in t]
            for c in range(BLOCKS_Z):
                values = six_points_back(*[t[j][c] for j in range(6)])
                for r, value in enumerate(values):
                    work[some, pl.ds((r * BLOCKS_Z + c) * 128, 128)] = value


def rounded(value):
    return value.astype(BF16).astype(F32)


def shift_box(padded, value, put, dx, dy, dz):
    for r in range(BLOCKS_Y):
        for c in range(BLOCKS_Z):
            at = ((r + SIDE_Y) * WIDE_Z + c + SIDE_Z) * ROWS_PADDED + MARGIN
            padded[pl.ds(at, BOX), :] = value(pl.ds((r * BLOCKS_Z + c) * 128, 128))
    fine_y, fine_z = dy & 7, dz & 15
    start = ((dy >> 3) + SIDE_Y) * WIDE_Z + (dz >> 4) + SIDE_Z
    base = start * ROWS_PADDED + MARGIN + dx
    lane = lax.broadcasted_iota(jnp.int32, (1, 128), 1)
    next_y = (lane >> 4) < fine_y
    next_z = (lane & 15) < fine_z
    carried = (lane & 15) + fine_z >= 16
    ahead = fine_y * 16 + fine_z
    turn = (128 - ahead) & 127
    turn_carried = (128 + 16 - ahead) & 127

    def block(r, c):
        return padded[pl.ds(base + (r * WIDE_Z + c) * ROWS_PADDED, BOX), :]

    for r in range(BLOCKS_Y):
        mixed = [jnp.where(next_y, block(r + 1, c), block(r, c)) for c in range(BLOCKS_Z + 1)]
        for c in range(BLOCKS_Z):
            source = jnp.where(next_z, mixed[c + 1], mixed[c])
            out = jnp.where(
                carried, pltpu.roll(source, turn_carried, 1), pltpu.roll(source, turn, 1)
            )
            put(pl.ds((r * BLOCKS_Z + c) * 128, 128), out)


def exchange_kernel(part, *refs):
    n_in = SETS * SOURCES
    n_out = len(GIVEN[part])
    listing, *refs = refs
    boxes_in, refs = refs[:n_in], refs[n_in:]
    tables_in, refs = refs[:N_TABLES], refs[N_TABLES:]
    outs, refs = refs[:n_out], refs[n_out:]
    tables, refs = refs[:N_TABLES], refs[N_TABLES:]
    acc, stage, nothing, held, theirs, both, work, padded, *refs = refs
    mine, touched, sems, table_sems, out_sems = refs

    mine[0] = 0
    for home in range(len(PLACES)):
        def check(pair, carry, home=home):
            row = (home * PAIRS_DEV + pair) * LIST_WIDTH
            for kind in range(3):
                source = listing[row + 2 * kind + 1]
                gives_far = source >= FAR_PLACES[0] if kind != 1 else jnp.bool_(False)
                if home in FAR_PLACES and kind != 2:
                    gives_far = jnp.bool_(True)
                now = gives_far if part == 0 else jnp.logical_not(gives_far)

                @pl.when((listing[row + 2 * kind] == home) & now)
                def _(kind=kind):
                    at = mine[0]
                    mine[0] = at + 1
                    task = (at + 1) * TASK_WIDTH
                    mine[task] = home
                    mine[task + 1] = listing[row + 2 * kind + 1]
                    for c in range(5):
                        mine[task + 2 + c] = listing[row + 6 + c]
                    mine[task + 7] = kind

            return carry

        lax.fori_loop(0, PAIRS_DEV, check, 0)

    count = mine[0]
    begin, end = 0, (count + 1) >> 1

    def table_copies():
        return [
            pltpu.make_async_copy(tables_in[i], tables[i], table_sems.at[i])
            for i in range(N_TABLES)
        ]

    def fetch(of_trial, source, slot, target, sem):
        row = pl.multiple_of(slot * BOX, 16)
        code = source * 2 + jnp.where(of_trial, 1, 0)
        for s in range(SOURCES):
            for k in range(SETS):

                @pl.when(code == 2 * s + k)
                def _(ref=boxes_in[2 * s + k]):
                    pltpu.make_async_copy(ref.at[pl.ds(row, BOX)], target, sem).start()

    def each_load(step, act):
        for i in range(2):
            task = (step * 2 + i + 1) * TASK_WIDTH

            @pl.when(step * 2 + i < count)
            def _(i=i, task=task):
                kind = mine[task + 7]
                act(kind == 1, mine[task], mine[task + 2], 2 * i)
                act(kind == 2, mine[task + 1], mine[task + 3], 2 * i + 1)

    def start_loads(step, buffer):
        def act(of_trial, source, slot, i):
            fetch(of_trial, source, slot, held.at[buffer, i], sems.at[buffer, i])

        each_load(step, act)

    def wait_loads(step, buffer):
        def act(of_trial, source, slot, i):
            pltpu.make_async_copy(
                boxes_in[0].at[pl.ds(0, BOX)], held.at[buffer, i], sems.at[buffer, i]
            ).wait()

        each_load(step, act)

    def box_rows(i):
        return pl.ds(pl.multiple_of(i * BOX, BOX), BOX)

    def sum_slot(task, which, kind):
        of_set = jnp.where(kind == 0, 0, ORB_DEV)
        return mine[task + which] * SOURCE_SLOTS + of_set + mine[task + 2 + which]

    places = []
    for i, (source, low, size) in enumerate(GIVEN[part]):
        for k in range(size):
            places.append((source * SOURCE_SLOTS + low + k, i, pl.ds(k * BOX, BOX)))

    def keep(slot, i, some):
        return pltpu.make_async_copy(nothing, outs[i].at[some], out_sems.at[slot])

    def send(slot, i, some):
        return pltpu.make_async_copy(stage.at[box_rows(slot)], outs[i].at[some], out_sems.at[slot])

    @pl.when(begin < end)
    def _():
        start_loads(begin, begin & 1)
        for copy in table_copies():
            copy.start()

    for i in range(SOURCES * SOURCE_SLOTS):
        touched[i] = 0

    def mark(i, carry):
        task = (i + 1) * TASK_WIDTH
        kind = mine[task + 7]

        @pl.when(kind != 2)
        def _():
            touched[sum_slot(task, 0, kind)] = 1

        @pl.when(kind != 1)
        def _():
            touched[sum_slot(task, 1, kind)] = 1

        return carry

    lax.fori_loop(0, count, mark, 0)
    nothing[...] = jnp.zeros(nothing.shape, BF16)
    for place in places:

        @pl.when(touched[place[0]] == 0)
        def _(place=place):
            keep(*place).start()

    padded[...] = jnp.zeros(padded.shape, F32)

    def clear(i, carry):
        @pl.when(touched[i] == 1)
        def _():
            acc[box_rows(i), :] = jnp.zeros((BOX, PLANE), F32)

        return carry

    lax.fori_loop(0, SOURCES * SOURCE_SLOTS, clear, 0)

    def add(slot, lanes, value):
        at = box_rows(slot)
        acc[at, lanes] = acc[at, lanes] + value

    def one_step(step, carry):
        buffer = step & 1

        @pl.when(step + 1 < end)
        def _():
            start_loads(step + 1, 1 - buffer)

        wait_loads(step, buffer)
        for i in range(2):
            task = (step * 2 + i + 1) * TASK_WIDTH

            @pl.when(step * 2 + i < count)
            def _(i=i, task=task):
                def value(lanes):
                    return held[buffer, 2 * i + 1, :, lanes].astype(F32)

                def put(lanes, block):
                    theirs[i, :, lanes] = block

                shift_box(padded, value, put, mine[task + 4], mine[task + 5], mine[task + 6])

        @pl.when(step == begin)
        def _():
            for copy in table_copies():
                copy.wait()

        def density(b, some, r, c):
            lanes = pl.ds((r * BLOCKS_Z + c) * 128, 128)
            return held[buffer, 2 * b, some, lanes].astype(F32) * theirs[b, some, lanes]

        solve(density, both, work, *tables, 2)
        for i in range(2):
            task = (step * 2 + i + 1) * TASK_WIDTH
            there = step * 2 + i < count
            kind = mine[task + 7]

            @pl.when(there & (kind != 2))
            def _(i=i, task=task, kind=kind):
                near = rounded(work[pl.ds(i * BOX, BOX), :] * theirs[i])
                add(sum_slot(task, 0, kind), pl.ds(0, PLANE), near)

            @pl.when(there & (kind != 1))
            def _(i=i, task=task, kind=kind):
                slot = sum_slot(task, 1, kind)

                def value(lanes):
                    mine_box = held[buffer, 2 * i, :, lanes].astype(F32)
                    return rounded(work[pl.ds(i * BOX, BOX), lanes] * mine_box)

                def put(lanes, block):
                    add(slot, lanes, block)

                shift_box(padded, value, put, -mine[task + 4], -mine[task + 5], -mine[task + 6])

        return carry

    lax.fori_loop(begin, end, one_step, 0)

    def put(i, carry):
        @pl.when(touched[i] == 1)
        def _():
            some = box_rows(i)
            stage[some, :] = acc[some, :].astype(BF16)

        return carry

    lax.fori_loop(0, SOURCES * SOURCE_SLOTS, put, 0)
    for place in places:

        @pl.when(touched[place[0]] == 1)
        def _(place=place):
            send(*place).start()

    for place in places:
        send(*place).wait()


def exchange(part, listing, boxes, tables):
    any_space = pl.BlockSpec(memory_space=pl.ANY)
    smem = pl.BlockSpec(memory_space=pltpu.SMEM)
    outs = [
        jax.ShapeDtypeStruct((size * BOX, PLANE), BF16) for _, _, size in GIVEN[part]
    ]
    slots = SOURCES * SOURCE_SLOTS

    def kernel(*refs):
        exchange_kernel(part, *refs)

    return pl.pallas_call(
        kernel,
        out_shape=outs,
        in_specs=[smem] + [any_space] * (len(boxes) + len(tables)),
        out_specs=[any_space] * len(outs),
        scratch_shapes=[
            *[pltpu.VMEM(t.shape, t.dtype) for t in tables],
            pltpu.VMEM((slots * BOX, PLANE), F32),
            pltpu.VMEM((slots * BOX, PLANE), BF16),
            pltpu.VMEM((BOX, PLANE), BF16),
            pltpu.VMEM((2, 4, BOX, PLANE), BF16),
            pltpu.VMEM((2, BOX, PLANE), F32),
            pltpu.VMEM((4 * BOX, PLANE), BF16),
            pltpu.VMEM((2 * BOX, PLANE), F32),
            pltpu.VMEM((WIDE_Y * WIDE_Z * ROWS_PADDED, 128), F32),
            pltpu.SMEM(((MAX_TASKS + 3) * TASK_WIDTH,), jnp.int32),
            pltpu.SMEM((slots,), jnp.int32),
            pltpu.SemaphoreType.DMA((2, 4)),
            pltpu.SemaphoreType.DMA((N_TABLES,)),
            pltpu.SemaphoreType.DMA((slots,)),
        ],
        compiler_params=pltpu.CompilerParams(vmem_limit_bytes=56 * 1024 * 1024),
        cost_estimate=pl.CostEstimate(
            flops=15_000_000_000, bytes_accessed=30_000_000, transcendentals=0
        ),
        name=("far_tasks", "other_tasks")[part],
    )(listing, *boxes, *tables)


def reorder_kernel(with_notes, box, *refs):
    order, out = refs[-2:]
    for r in range(BLOCKS_Y):
        lanes = pl.ds(r * CHUNK, CHUNK)
        moved = jnp.dot(box[:, lanes], order[...], preferred_element_type=F32)
        out[pl.ds(0, SET_ROWS), lanes] = moved.astype(BF16)
    if with_notes:
        out[pl.ds(SET_ROWS, NOTE_ROWS), :] = refs[0][...]


def reorder(boxes, order, notes=()):
    rows = SET_ROWS + NOTE_ROWS * len(notes)

    def kernel(*refs):
        reorder_kernel(bool(notes), *refs)

    return pl.pallas_call(
        kernel,
        out_shape=jax.ShapeDtypeStruct((rows, PLANE), BF16),
        name="reorder",
        compiler_params=pltpu.CompilerParams(vmem_limit_bytes=32 * 1024 * 1024),
    )(boxes, *notes, order)


def total_kernel(*refs):
    *parts, order, out = refs
    for r in range(BLOCKS_Y):
        lanes = pl.ds(r * CHUNK, CHUNK)
        result = parts[0][:, lanes].astype(F32)
        for part in parts[1:]:
            result += part[:, lanes].astype(F32)
        moved = jnp.dot((-result).astype(BF16), order[...], preferred_element_type=F32)
        out[:, lanes] = moved.astype(BF16)


def total(abroad, which, parts, order):
    half = SET_ROWS // 2
    whole = pl.BlockSpec((CHUNK, CHUNK), lambda i: (0, 0))
    some = pl.BlockSpec((half, PLANE), lambda i: (i, 0))
    first = pl.BlockSpec((half, PLANE), lambda i: (i + 2 * which, 0))
    return pl.pallas_call(
        total_kernel,
        grid=(2,),
        out_shape=jax.ShapeDtypeStruct((SET_ROWS, PLANE), BF16),
        in_specs=[first] + [some] * len(parts) + [whole],
        out_specs=some,
        name="total",
        compiler_params=pltpu.CompilerParams(vmem_limit_bytes=32 * 1024 * 1024),
    )(abroad, *parts, order)


def moves(n_region):
    def step(dx, dz):
        pairs = []
        for region in range(n_region):
            sign = 1 - 2 * (region % 2)
            for x in range(GRID):
                for z in range(GRID):
                    to = (x + sign * dx) % GRID * GRID + (z + sign * dz) % GRID
                    pairs.append((region * N_SUB + x * GRID + z, region * N_SUB + to))

        def move(block):
            return lax.ppermute(block, ("region", "sub"), pairs)

        return move

    def across(distance):
        pairs = [(i, (i + distance) % n_region) for i in range(n_region)]

        def move(block):
            return lax.ppermute(block, "region", pairs)

        return move

    return step, across


def per_device(orbitals, trial_set, own_slot, partner_route, partner_slot, offsets):
    n_region = lax.axis_size("region")
    region = lax.axis_index("region")
    sub = lax.axis_index("sub")
    step, across = moves(n_region)
    tables = transform_tables()
    tables = [
        jnp.asarray(tables[k])
        for k in TABLES
    ]
    order, order_back = jnp.asarray(order_table()), jnp.asarray(order_table().T.copy())
    table, most = meeting_table()
    meta = jnp.concatenate([own_slot, partner_route[:, 0], partner_slot])
    where = jnp.stack([region, sub, jnp.int32(n_region)]).astype(jnp.int32)
    smem = pl.BlockSpec(memory_space=pltpu.SMEM)

    def planner(*refs):
        plan_kernel(most, *refs)

    chosen = pl.pallas_call(
        planner,
        out_shape=jax.ShapeDtypeStruct((LISTED,), jnp.int32),
        in_specs=[smem] * 4,
        out_specs=smem,
        scratch_shapes=[pltpu.SMEM((3 * len(PLACES),), jnp.int32)],
        name="plan",
    )(where, meta, offsets.reshape(-1), jnp.asarray(table))

    ordered = lax.optimization_barrier
    notes = jnp.pad(chosen.astype(BF16)[None], ((0, NOTE_ROWS - 1), (0, PLANE - LISTED)))
    o00 = reorder(orbitals.reshape(SET_ROWS, PLANE), order, (notes,))
    t00 = reorder(trial_set.reshape(SET_ROWS, PLANE), order)
    o00, t00 = ordered((o00, t00))
    o01, o10, o_abroad = step(0, 1)(o00), step(1, 0)(o00), across(-1)(o00)
    t01, t10, t_abroad = step(0, 1)(t00), step(1, 0)(t00), across(-1)(t00)
    o01, o10, o_abroad, t_abroad = ordered((o01, o10, o_abroad, t_abroad))
    o13, o31, o11 = step(0, -1)(o10), step(-1, 0)(o01), step(1, 0)(o01)
    t13, t31, t11 = step(0, -1)(t10), step(-1, 0)(t01), step(0, 1)(t10)

    def list_of(arrays):
        return jnp.concatenate([n[-NOTE_ROWS, :LISTED] for n in arrays]).astype(jnp.int32)

    listing = list_of([o00, o01, o10, o11, o13, o31])
    all_boxes = [o00, t00, o01, t01, o10, t10, o11, t11, o13, t13, o31, t31, o_abroad, t_abroad]
    far = exchange(0, listing, all_boxes, tables)
    far, listing = ordered((far, listing))

    def one(a):
        return step(0, 1)(far[8 + a]), step(1, 0)(far[10 + a])

    r11 = [step(-1, 0)(far[6]), step(0, -1)(far[7])]
    r13, r31 = zip(one(0), one(1))
    r_abroad = across(1)(far[12])
    other = exchange(1, listing, all_boxes, tables)
    other, r11, r13, r31, r_abroad = ordered((other, r11, r13, r31, r_abroad))

    def add_up(arrays):
        return sum(a.astype(F32) for a in arrays).astype(BF16)

    results = []
    for a in range(SETS):
        to_01 = [far[2 + a], other[2 + a], r31[a]] + ([] if a else [r11[0]])
        to_10 = [far[4 + a], other[4 + a], r13[a]] + ([r11[1]] if a else [])
        f01, f10 = step(0, -1)(add_up(to_01)), step(-1, 0)(add_up(to_10))
        result = total(r_abroad, a, [far[a], other[a], f01, f10], order_back)
        results.append(result.reshape(ORB_DEV, BOX, PLANE))
    return tuple(results)


def solution(mesh):
    in_specs = (
        P(("region", "sub"), None, None),
        P(("region", "sub"), None, None),
        P(("region", "sub")),
        P(("region", "sub"), None),
        P(("region", "sub")),
        P(),
    )
    out_specs = (P(("region", "sub"), None, None), P(("region", "sub"), None, None))
    return jax.shard_map(
        per_device, mesh=mesh, in_specs=in_specs, out_specs=out_specs, check_vma=False
    )
```

```python
import math

import jax
import jax.numpy as jnp
import ml_dtypes
import numpy as np
from jax import lax
from jax.experimental import pallas as pl
from jax.experimental.pallas import tpu as pltpu
from jax.sharding import PartitionSpec as P

BOX = 48
PLANE = BOX * BOX
CHUNK = PLANE // 6
SCREEN = 0.5
GRID = 4
N_SUB = GRID * GRID
ORB_DEV = 4
PAIRS_DEV = 4
N_PAIRS = N_SUB * PAIRS_DEV

PLACES = ((0, 0), (0, 1), (1, 0), (1, 1), (1, 3), (3, 1))
REGION_SOURCE = len(PLACES)
SOURCES = len(PLACES) + 1
LIST_WIDTH = 16
TASK_WIDTH = 8
LISTED = PAIRS_DEV * LIST_WIDTH
NOTE_ROWS = 16
SET_ROWS = ORB_DEV * BOX
SIZES = (4, 4, 4, 2, 2, 4, 4, 4)
N_OUT = len(SIZES)
N_TABLES = 4
BLOCKS_Y = 6
BLOCKS_Z = 3
MARGIN = 24
ROWS_PADDED = BOX + 2 * MARGIN
SIDE_Y = 3
SIDE_Z = 2
WIDE_Y = BLOCKS_Y + 2 * SIDE_Y
WIDE_Z = BLOCKS_Z + 2 * SIDE_Z
MAX_TASKS = 2 * len(PLACES) * PAIRS_DEV
HALF_ROOT3 = math.sqrt(3.0) / 2.0
F32 = jnp.float32
BF16 = jnp.bfloat16


def meeting_table():
    found = [[] for _ in range(N_SUB)]
    for i, (ax, az) in enumerate(PLACES):
        for j, (bx, bz) in enumerate(PLACES):
            delta = (ax - bx) % GRID * GRID + (az - bz) % GRID
            found[delta].append(i + 8 * j)
    most = max(len(f) for f in found)
    codes = np.array([f + [f[-1]] * (most - len(f)) for f in found], np.int32)
    counts = np.array([len(f) for f in found], np.int32)
    return np.concatenate([counts, codes.reshape(-1)]), most


def high_low(matrix):
    high = matrix.astype(ml_dtypes.bfloat16)
    low = (matrix - high.astype(np.float64)).astype(ml_dtypes.bfloat16)
    return np.stack([high, low])


def cas(angles):
    return np.cos(angles) + np.sin(angles)


def transform_tables():
    turn = 2.0 * math.pi / BOX
    n = np.arange(BOX)
    line = cas(turn * (n[:, None] * n[None, :] % BOX))
    q, w = np.arange(8), np.arange(16)

    def angle_y(j):
        return turn * (q[:, None] * (6 * q[None, :] + j) % BOX)

    def angle_z(j):
        return turn * (w[:, None] * (3 * w[None, :] + j) % BOX)

    def both_parts(angle):
        c, s = np.cos(angle), np.sin(angle)
        return np.block([[c, -s], [s, c]])

    def planes(y, z, sign):
        whole = angle_y(y)[:, None, :, None] + sign * angle_z(z)[None, :, None, :]
        return both_parts(whole.reshape(128, 128))

    def real_complex(y):
        z = both_parts(angle_z(1)).reshape(2, 16, 2, 16)
        return np.einsum("qm,awbn->aqwbmn", cas(angle_y(y)), z).reshape(256, 256)

    def complex_real(y):
        return np.kron(both_parts(angle_y(y)), cas(angle_z(0)))

    zero = np.zeros((128, 128))
    real = [np.kron(cas(angle_y(y)), cas(angle_z(0))) for y in (0, 3)]
    waves = [np.block([[real[0], zero], [zero, real[1]]]), real_complex(0), real_complex(3)]
    waves += [complex_real(1), complex_real(2)]
    for y in (1, 2):
        waves += [planes(y, 1, 1), planes(y, 1, -1)]
    waves = np.stack(waves)
    lam = 4.0 * np.sin(math.pi * n / BOX) ** 2

    def spectrum(y, z, weight):
        ky, kz = 6 * q + y, 3 * w + z
        total = lam[:, None, None] + lam[ky][None, :, None] + lam[kz][None, None, :] + SCREEN
        return (weight * 4.0 * math.pi / total / float(BOX**3)).reshape(BOX, 128)

    order = [(0, 0, 1.0), (3, 0, 1.0)]
    for y, z in ((0, 1), (3, 1), (1, 0), (2, 0), (1, 1), (1, 1), (2, 1), (2, 1)):
        order += [(y, z, 2.0)] * 2
    green = np.concatenate([spectrum(*o) for o in order], axis=1)
    rows = high_low(line)
    rows = np.block([[rows[0], rows[0]], [rows[1], np.zeros_like(rows[1])]])
    return dict(
        waves=high_low(waves),
        waves_back=high_low(waves.transpose(0, 2, 1)),
        green=green.astype(np.float32),
        rows=rows,
    )


TABLES = ("waves", "waves_back", "green", "rows")


def order_table():
    lane = np.arange(8 * BOX)
    q, c, w = lane // BOX, lane % BOX // 16, lane % 16
    table = np.zeros((8 * BOX, 8 * BOX), np.float32)
    table[lane, c * 128 + q * 16 + w] = 1.0
    return table.astype(ml_dtypes.bfloat16)


def plan_kernel(most, where, meta, offsets, table, chosen, used):
    region, sub, n_region = where[0], where[1], where[2]
    sign = 1 - 2 * (region & 1)
    next_region = jnp.where(region + 1 == n_region, 0, region + 1)
    for i in range(2 * len(PLACES)):
        used[i] = 0

    def place(pair, turn):
        own_slot = meta[pair]
        route = meta[PAIRS_DEV + pair]
        partner_slot = meta[2 * PAIRS_DEV + pair]
        abroad = route == N_SUB
        other = jnp.where(abroad, sub, route)
        dx = (sign * ((other >> 2) - (sub >> 2))) & 3
        dz = (sign * ((other & 3) - (sub & 3))) & 3
        delta = dx * GRID + dz
        count = jnp.where(abroad, 1, table[delta])

        @pl.when(jnp.where(count == 1, 0, 1) == turn)
        def _():
            row = pair * LIST_WIDTH
            for kind in range(3):
                load_of = len(PLACES) * min(kind, 1)
                best_load = jnp.int32(1 << 20)
                best_code = jnp.int32(0)
                for k in range(most):
                    code = table[N_SUB + delta * most + k]
                    load = used[load_of + (code & 7)]
                    better = load < best_load
                    best_load = jnp.where(better, load, best_load)
                    best_code = jnp.where(better, code, best_code)
                at = jnp.where(abroad, 0, best_code & 7)
                used[load_of + at] = used[load_of + at] + 1
                chosen[row + 2 * kind] = at
                chosen[row + 2 * kind + 1] = jnp.where(
                    abroad, REGION_SOURCE, (best_code >> 3) & 7
                )
            first = (region * N_SUB + sub) * ORB_DEV + own_slot
            second_region = jnp.where(abroad, next_region, region)
            second = (second_region * N_SUB + other) * ORB_DEV + partner_slot
            chosen[row + 6] = own_slot
            chosen[row + 7] = partner_slot
            for c in range(3):
                chosen[row + 8 + c] = offsets[first * 3 + c] - offsets[second * 3 + c]
            for c in range(11, LIST_WIDTH):
                chosen[row + c] = 0

    for turn in range(2):
        for pair in range(PAIRS_DEV):
            place(pair, turn)


def three_dots(high, low, weights, index):
    boxes_high = jnp.concatenate([high, low], axis=0)
    half = high.shape[0]
    wide = jnp.dot(boxes_high, weights[0, index], preferred_element_type=F32)
    rest = jnp.dot(high, weights[1, index], preferred_element_type=F32)
    return wide[:half] + wide[half:] + rest


def split(value):
    high = value.astype(BF16)
    return high, (value - high.astype(F32)).astype(BF16)


def six_points(x):
    u = [x[r] + x[r + 3] for r in range(3)]
    v = [x[r] - x[r + 3] for r in range(3)]
    return (
        u[0] + u[1] + u[2],
        v[0] - v[1] + v[2],
        v[0] + 0.5 * (v[1] - v[2]),
        -HALF_ROOT3 * (v[1] + v[2]),
        u[0] - 0.5 * (u[1] + u[2]),
        -HALF_ROOT3 * (u[1] - u[2]),
    )


def six_points_back(t0, t3, t1r, t1i, t2r, t2i):
    a0 = t0 + t2r
    t2h = t0 - 0.5 * t2r
    t2s = HALF_ROOT3 * t2i
    a1 = t2h - t2s
    a2 = t2h + t2s
    t1s = HALF_ROOT3 * t1i
    b0 = t3 + t1r
    b1 = 0.5 * t1r - t3 - t1s
    b2 = t3 - 0.5 * t1r - t1s
    return a0 + b0, a1 + b1, a2 + b2, a0 - b0, a1 - b1, a2 - b2


def three_points(x):
    total = x[1] + x[2]
    return x[0] + total, x[0] - 0.5 * total, -HALF_ROOT3 * (x[1] - x[2])


def three_points_back(s0, s1r, s1i):
    low = s0 - 0.5 * s1r
    turned = HALF_ROOT3 * s1i
    return s0 + s1r, low - turned, low + turned


def solve(density, both, work, waves, waves_back, green, rows, boxes):
    for b in range(boxes):
        for g in range(BOX // 16):
            some = pl.ds(b * BOX + g * 16, 16)
            low_some = pl.ds((boxes + b) * BOX + g * 16, 16)
            columns = []
            for c in range(BLOCKS_Z):
                x = [density(b, pl.ds(g * 16, 16), r, c) for r in range(BLOCKS_Y)]
                columns.append(six_points(x))
            t = [three_points([columns[c][j] for c in range(BLOCKS_Z)]) for j in range(6)]
            parts = [t[0][0], t[1][0], t[0][1], t[0][2], t[1][1], t[1][2]]
            parts += [t[2][0], t[3][0], t[4][0], t[5][0]]
            for j in (2, 4):
                (_, rr, ri), (_, ir, ii) = t[j], t[j + 1]
                parts += [rr - ii, ri + ir, rr + ii, ir - ri]
            for i, part in enumerate(parts):
                high, low = split(part)
                both[some, pl.ds(i * 128, 128)] = high
                both[low_some, pl.ds(i * 128, 128)] = low

    def row_pass(value):
        stacked = jnp.concatenate(split(value), axis=0)
        result = jnp.dot(rows[...], stacked, preferred_element_type=F32)
        return result[:BOX] + result[BOX:]

    def plane_pass(weights):
        for group in range(9):
            lanes = pl.ds(group * 256, 256)
            high = both[pl.ds(0, boxes * BOX), lanes]
            low = both[pl.ds(boxes * BOX, boxes * BOX), lanes]
            work[:, lanes] = three_dots(high, low, weights, group)

    places = [
        (pl.ds(b * BOX, BOX), pl.ds((boxes + b) * BOX, BOX), pl.ds(group * 256, 256))
        for b in range(boxes)
        for group in range(9)
    ]
    plane_pass(waves)
    for some, _, lanes in places:
        work[some, lanes] = row_pass(work[some, lanes]) * green[:, lanes]
    for some, low_some, lanes in places:
        both[some, lanes], both[low_some, lanes] = split(row_pass(work[some, lanes]))
    plane_pass(waves_back)

    for b in range(boxes):
        for g in range(BOX // 16):
            some = pl.ds(b * BOX + g * 16, 16)
            p = [work[some, pl.ds(i * 128, 128)] for i in range(18)]
            t = [[p[0], p[2], p[3]], [p[1], p[4], p[5]]]
            for j in range(2):
                pr, pi, mr, mi = p[10 + 4 * j : 14 + 4 * j]
                t.append([p[6 + 2 * j], pr + mr, pi - mi])
                t.append([p[7 + 2 * j], pi + mi, mr - pr])
            t = [three_points_back(*parts) for parts in t]
            for c in range(BLOCKS_Z):
                values = six_points_back(*[t[j][c] for j in range(6)])
                for r, value in enumerate(values):
                    work[some, pl.ds((r * BLOCKS_Z + c) * 128, 128)] = value


def rounded(value):
    return value.astype(BF16).astype(F32)


def shift_box(padded, value, put, dx, dy, dz):
    for r in range(BLOCKS_Y):
        for c in range(BLOCKS_Z):
            at = ((r + SIDE_Y) * WIDE_Z + c + SIDE_Z) * ROWS_PADDED + MARGIN
            padded[pl.ds(at, BOX), :] = value(pl.ds((r * BLOCKS_Z + c) * 128, 128))
    fine_y, fine_z = dy & 7, dz & 15
    start = ((dy >> 3) + SIDE_Y) * WIDE_Z + (dz >> 4) + SIDE_Z
    base = start * ROWS_PADDED + MARGIN + dx
    lane = lax.broadcasted_iota(jnp.int32, (1, 128), 1)
    next_y = (lane >> 4) < fine_y
    next_z = (lane & 15) < fine_z
    carried = (lane & 15) + fine_z >= 16
    ahead = fine_y * 16 + fine_z
    turn = (128 - ahead) & 127
    turn_carried = (128 + 16 - ahead) & 127

    def block(r, c):
        return padded[pl.ds(base + (r * WIDE_Z + c) * ROWS_PADDED, BOX), :]

    for r in range(BLOCKS_Y):
        mixed = [jnp.where(next_y, block(r + 1, c), block(r, c)) for c in range(BLOCKS_Z + 1)]
        for c in range(BLOCKS_Z):
            source = jnp.where(next_z, mixed[c + 1], mixed[c])
            out = jnp.where(
                carried, pltpu.roll(source, turn_carried, 1), pltpu.roll(source, turn, 1)
            )
            put(pl.ds((r * BLOCKS_Z + c) * 128, 128), out)


def exchange_kernel(part, *refs):
    second = part > 0
    sets = 2 if second else 1
    carried = N_OUT if part == 2 else 0
    n_in = sets * (SOURCES + 1)
    listing, *refs = refs
    boxes_in, refs = refs[:n_in], refs[n_in:]
    tables_in, refs = refs[:N_TABLES], refs[N_TABLES:]
    sums_in, refs = refs[:carried], refs[carried:]
    outs, refs = refs[:N_OUT], refs[N_OUT:]
    tables, refs = refs[:N_TABLES], refs[N_TABLES:]
    acc, stage, held, theirs, both, work, padded, mine, sems, table_sems, out_sems = refs

    mine[0] = 0
    for home in range(len(PLACES)):

        def check(pair, carry, home=home):
            row = (home * PAIRS_DEV + pair) * LIST_WIDTH
            for kind in (1, 2) if second else (0,):

                @pl.when(listing[row + 2 * kind] == home)
                def _(kind=kind):
                    at = mine[0]
                    mine[0] = at + 1
                    task = (at + 1) * TASK_WIDTH
                    mine[task] = home
                    mine[task + 1] = listing[row + 2 * kind + 1]
                    for c in range(5):
                        mine[task + 2 + c] = listing[row + 6 + c]
                    mine[task + 7] = kind

            return carry

        lax.fori_loop(0, PAIRS_DEV, check, 0)

    count = mine[0]
    steps = (count + 1) >> 1
    half = (steps + 1) >> 1
    begin = half if part == 2 else 0
    end = half if part == 1 else steps

    def table_copies():
        return [
            pltpu.make_async_copy(tables_in[i], tables[i], table_sems.at[i])
            for i in range(N_TABLES)
        ]

    def fetch(group, source, slot, target, sem):
        refs_of = boxes_in[group * (SOURCES + 1) : (group + 1) * (SOURCES + 1)]

        def start(ref, row):
            row = pl.multiple_of(row, 16)
            pltpu.make_async_copy(ref.at[pl.ds(row, BOX)], target, sem).start()

        for s in range(SOURCES):
            if s == 3:
                for part_of in range(2):

                    @pl.when((source == s) & ((slot >> 1) == part_of))
                    def _(part_of=part_of):
                        start(refs_of[3 + part_of], (slot & 1) * BOX)
            else:
                at = s if s < 3 else s + 1

                @pl.when(source == s)
                def _(at=at):
                    start(refs_of[at], slot * BOX)

    def each_load(step, act):
        for i in range(2):
            task = (step * 2 + i + 1) * TASK_WIDTH

            @pl.when(step * 2 + i < count)
            def _(i=i, task=task):
                kind = mine[task + 7]
                act(kind == 1, mine[task], mine[task + 2], 2 * i)
                act(kind == 2, mine[task + 1], mine[task + 3], 2 * i + 1)

    def start_loads(step, buffer):
        def act(of_trial, source, slot, i):
            if second:

                @pl.when(of_trial)
                def _():
                    fetch(1, source, slot, held.at[buffer, i], sems.at[buffer, i])

                @pl.when(jnp.logical_not(of_trial))
                def _():
                    fetch(0, source, slot, held.at[buffer, i], sems.at[buffer, i])
            else:
                fetch(0, source, slot, held.at[buffer, i], sems.at[buffer, i])

        each_load(step, act)

    def wait_loads(step, buffer):
        def act(of_trial, source, slot, i):
            pltpu.make_async_copy(
                boxes_in[0].at[pl.ds(0, BOX)], held.at[buffer, i], sems.at[buffer, i]
            ).wait()

        each_load(step, act)

    def sum_copies(into):
        copies = []
        for i, size in enumerate(SIZES):
            low = sum(SIZES[:i]) * BOX
            vmem = stage.at[pl.ds(low, size * BOX)]
            if into:
                copies.append(pltpu.make_async_copy(sums_in[i], vmem, out_sems.at[i]))
            else:
                copies.append(pltpu.make_async_copy(vmem, outs[i], out_sems.at[i]))
        return copies

    @pl.when(begin < end)
    def _():
        start_loads(begin, begin & 1)
        for copy in table_copies():
            copy.start()

    if carried:
        for copy in sum_copies(True):
            copy.start()
    padded[...] = jnp.zeros(padded.shape, F32)

    def box_rows(i):
        return pl.ds(pl.multiple_of(i * BOX, BOX), BOX)

    if carried:
        for copy in sum_copies(True):
            copy.wait()

    def prepare(i, carry):
        if carried:
            acc[box_rows(i), :] = stage[box_rows(i), :].astype(F32)
        else:
            acc[box_rows(i), :] = jnp.zeros((BOX, PLANE), F32)
        return carry

    lax.fori_loop(0, SOURCES * ORB_DEV, prepare, 0)

    def add(source, slot, lanes, value):
        at = box_rows(source * ORB_DEV + slot)
        acc[at, lanes] = acc[at, lanes] + value

    def one_step(step, carry):
        buffer = step & 1

        @pl.when(step + 1 < end)
        def _():
            start_loads(step + 1, 1 - buffer)

        wait_loads(step, buffer)
        for i in range(2):
            task = (step * 2 + i + 1) * TASK_WIDTH

            @pl.when(step * 2 + i < count)
            def _(i=i, task=task):
                def value(lanes):
                    return held[buffer, 2 * i + 1, :, lanes].astype(F32)

                def put(lanes, block):
                    theirs[i, :, lanes] = block

                shift_box(padded, value, put, mine[task + 4], mine[task + 5], mine[task + 6])

        @pl.when(step == begin)
        def _():
            for copy in table_copies():
                copy.wait()

        def density(b, some, r, c):
            lanes = pl.ds((r * BLOCKS_Z + c) * 128, 128)
            return held[buffer, 2 * b, some, lanes].astype(F32) * theirs[b, some, lanes]

        solve(density, both, work, *tables, 2)
        for i in range(2):
            task = (step * 2 + i + 1) * TASK_WIDTH
            there = step * 2 + i < count
            kind = mine[task + 7]

            @pl.when(there & (kind != 2))
            def _(i=i, task=task):
                near = rounded(work[pl.ds(i * BOX, BOX), :] * theirs[i])
                add(mine[task], mine[task + 2], pl.ds(0, PLANE), near)

            @pl.when(there & (kind != 1))
            def _(i=i, task=task):
                def value(lanes):
                    mine_box = held[buffer, 2 * i, :, lanes].astype(F32)
                    return rounded(work[pl.ds(i * BOX, BOX), lanes] * mine_box)

                def put(lanes, block):
                    add(mine[task + 1], mine[task + 3], lanes, block)

                shift_box(padded, value, put, -mine[task + 4], -mine[task + 5], -mine[task + 6])

        return carry

    lax.fori_loop(begin, end, one_step, 0)

    copies = sum_copies(False)
    at = 0
    for copy, size in zip(copies, SIZES):

        def put(i, carry):
            stage[box_rows(i), :] = acc[box_rows(i), :].astype(BF16)
            return carry

        lax.fori_loop(at, at + size, put, 0)
        copy.start()
        at += size
    for copy in copies:
        copy.wait()


def exchange(part, listing, boxes, tables, sums=()):
    any_space = pl.BlockSpec(memory_space=pl.ANY)
    smem = pl.BlockSpec(memory_space=pltpu.SMEM)
    outs = [
        jax.ShapeDtypeStruct((size * BOX, PLANE), BF16) for size in SIZES
    ]

    def kernel(*refs):
        exchange_kernel(part, *refs)

    return pl.pallas_call(
        kernel,
        out_shape=outs,
        in_specs=[smem] + [any_space] * (len(boxes) + len(tables) + len(sums)),
        out_specs=[any_space] * len(outs),
        scratch_shapes=[
            *[pltpu.VMEM(t.shape, t.dtype) for t in tables],
            pltpu.VMEM((SOURCES * ORB_DEV * BOX, PLANE), F32),
            pltpu.VMEM((SOURCES * ORB_DEV * BOX, PLANE), BF16),
            pltpu.VMEM((2, 4, BOX, PLANE), BF16),
            pltpu.VMEM((2, BOX, PLANE), F32),
            pltpu.VMEM((4 * BOX, PLANE), BF16),
            pltpu.VMEM((2 * BOX, PLANE), F32),
            pltpu.VMEM((WIDE_Y * WIDE_Z * ROWS_PADDED, 128), F32),
            pltpu.SMEM(((MAX_TASKS + 3) * TASK_WIDTH,), jnp.int32),
            pltpu.SemaphoreType.DMA((2, 4)),
            pltpu.SemaphoreType.DMA((N_TABLES,)),
            pltpu.SemaphoreType.DMA((N_OUT,)),
        ],
        compiler_params=pltpu.CompilerParams(vmem_limit_bytes=56 * 1024 * 1024),
        cost_estimate=pl.CostEstimate(
            flops=10_000_000_000, bytes_accessed=30_000_000, transcendentals=0
        ),
        name=("first_application", "second_early", "second_late")[part],
    )(listing, *boxes, *tables, *sums)


def reorder_kernel(with_notes, box, *refs):
    order, out = refs[-2:]
    for r in range(BLOCKS_Y):
        lanes = pl.ds(r * CHUNK, CHUNK)
        moved = jnp.dot(box[:, lanes], order[...], preferred_element_type=F32)
        out[pl.ds(0, SET_ROWS), lanes] = moved.astype(BF16)
    if with_notes:
        out[pl.ds(SET_ROWS, NOTE_ROWS), :] = refs[0][...]


def reorder(boxes, order, notes=()):
    rows = SET_ROWS + NOTE_ROWS * len(notes)

    def kernel(*refs):
        reorder_kernel(bool(notes), *refs)

    return pl.pallas_call(
        kernel,
        out_shape=jax.ShapeDtypeStruct((rows, PLANE), BF16),
        name="reorder",
        compiler_params=pltpu.CompilerParams(vmem_limit_bytes=32 * 1024 * 1024),
    )(boxes, *notes, order)


def total_kernel(*refs):
    *parts, order, out = refs
    for r in range(BLOCKS_Y):
        lanes = pl.ds(r * CHUNK, CHUNK)
        result = parts[0][:, lanes].astype(F32)
        for part in parts[1:]:
            result += part[:, lanes].astype(F32)
        moved = jnp.dot((-result).astype(BF16), order[...], preferred_element_type=F32)
        out[:, lanes] = moved.astype(BF16)


def total(parts, order):
    half = SET_ROWS // 2
    whole = pl.BlockSpec((CHUNK, CHUNK), lambda i: (0, 0))
    some = pl.BlockSpec((half, PLANE), lambda i: (i, 0))
    return pl.pallas_call(
        total_kernel,
        grid=(2,),
        out_shape=jax.ShapeDtypeStruct((SET_ROWS, PLANE), BF16),
        in_specs=[some] * len(parts) + [whole],
        out_specs=some,
        name="total",
        compiler_params=pltpu.CompilerParams(vmem_limit_bytes=32 * 1024 * 1024),
    )(*parts, order)


def moves(n_region):
    def step(dx, dz):
        pairs = []
        for region in range(n_region):
            sign = 1 - 2 * (region % 2)
            for x in range(GRID):
                for z in range(GRID):
                    to = (x + sign * dx) % GRID * GRID + (z + sign * dz) % GRID
                    pairs.append((region * N_SUB + x * GRID + z, region * N_SUB + to))

        def move(block):
            return lax.ppermute(block, ("region", "sub"), pairs)

        return move

    def across(distance):
        pairs = [(i, (i + distance) % n_region) for i in range(n_region)]

        def move(block):
            return lax.ppermute(block, "region", pairs)

        return move

    return step, across


def per_device(orbitals, trial_set, own_slot, partner_route, partner_slot, offsets):
    n_region = lax.axis_size("region")
    region = lax.axis_index("region")
    sub = lax.axis_index("sub")
    step, across = moves(n_region)
    tables = transform_tables()
    tables = [
        jnp.asarray(tables[k])
        for k in TABLES
    ]
    order, order_back = jnp.asarray(order_table()), jnp.asarray(order_table().T.copy())
    table, most = meeting_table()
    meta = jnp.concatenate([own_slot, partner_route[:, 0], partner_slot])
    where = jnp.stack([region, sub, jnp.int32(n_region)]).astype(jnp.int32)
    smem = pl.BlockSpec(memory_space=pltpu.SMEM)

    def planner(*refs):
        plan_kernel(most, *refs)

    chosen = pl.pallas_call(
        planner,
        out_shape=jax.ShapeDtypeStruct((LISTED,), jnp.int32),
        in_specs=[smem] * 4,
        out_specs=smem,
        scratch_shapes=[pltpu.SMEM((2 * len(PLACES),), jnp.int32)],
        name="plan",
    )(where, meta, offsets.reshape(-1), jnp.asarray(table))

    def near_places(boxes):
        return step(0, 1)(boxes), step(1, 0)(boxes), across(-1)(boxes)

    def cut(b01, b10):
        return b01[: 2 * BOX], b10[2 * BOX :]

    def far_places(b01, b10, halves):
        low, high = halves
        return step(1, 0)(low), step(0, 1)(high), step(0, -1)(b10), step(-1, 0)(b01)

    def begin_back(parts):
        own, c01, c10, c11_low, c11_high, c13, c31, c_abroad = parts
        return (
            step(0, 1)(c13),
            step(1, 0)(c31),
            step(-1, 0)(c11_low),
            step(0, -1)(c11_high),
            across(1)(c_abroad),
        )

    def merge(parts, arrived):
        r13, r31, r11_low, r11_high, _ = arrived
        none = jnp.zeros_like(r11_low)
        low = jnp.concatenate([r11_low, none])
        high = jnp.concatenate([none, r11_high])
        m01 = (parts[1].astype(F32) + r31.astype(F32) + low.astype(F32)).astype(BF16)
        m10 = (parts[2].astype(F32) + r13.astype(F32) + high.astype(F32)).astype(BF16)
        return step(0, -1)(m01), step(-1, 0)(m10)

    def finish(parts, arrived, merged):
        result = total([parts[0], arrived[4], *merged], order_back)
        return result.reshape(ORB_DEV, BOX, PLANE)

    ordered = lax.optimization_barrier
    notes = jnp.pad(chosen.astype(BF16)[None], ((0, NOTE_ROWS - 1), (0, PLANE - LISTED)))
    trials = reorder(trial_set.reshape(SET_ROWS, PLANE), order)
    boxes = reorder(orbitals.reshape(SET_ROWS, PLANE), order, (notes,))
    t01, t10, t_abroad = near_places(trials)
    boxes, t01, t10, t_abroad = ordered((boxes, t01, t10, t_abroad))
    t_cut = cut(t01, t10)
    o01, o10, o_abroad = near_places(boxes)
    o01, o10, o_abroad, t_cut = ordered((o01, o10, o_abroad, t_cut))
    o_far = far_places(o01, o10, cut(o01, o10))
    t01, t10, t_cut, o_far = ordered((t01, t10, t_cut, o_far))
    t_far = far_places(t01, t10, t_cut)
    orbital_boxes = [boxes, o01, o10, *o_far, o_abroad]
    notes = [boxes, o01, o10, o_far[1], o_far[2], o_far[3]]
    listing = jnp.concatenate([n[-NOTE_ROWS, :LISTED] for n in notes]).astype(jnp.int32)
    first = exchange(0, listing, orbital_boxes, tables)
    arrived_first = begin_back(first)
    first, listing, t_far = ordered((first, listing, t_far))
    all_boxes = orbital_boxes + [trials, t01, t10, *t_far, t_abroad]
    early = exchange(1, listing, all_boxes, tables)
    early, first, arrived_first = ordered((early, first, arrived_first))
    merged_first = merge(first, arrived_first)
    late = exchange(2, listing, all_boxes, tables, early)
    late, merged_first = ordered((late, merged_first))
    result_first = finish(first, arrived_first, merged_first)
    arrived_late = begin_back(late)
    result_second = finish(late, arrived_late, merge(late, arrived_late))
    return result_first, result_second


def solution(mesh):
    in_specs = (
        P(("region", "sub"), None, None),
        P(("region", "sub"), None, None),
        P(("region", "sub")),
        P(("region", "sub"), None),
        P(("region", "sub")),
        P(),
    )
    out_specs = (P(("region", "sub"), None, None), P(("region", "sub"), None, None))
    return jax.shard_map(
        per_device, mesh=mesh, in_specs=in_specs, out_specs=out_specs, check_vma=False
    )
```

```python
import math

import jax
import jax.numpy as jnp
import ml_dtypes
import numpy as np
from jax import lax
from jax.experimental import pallas as pl
from jax.experimental.pallas import tpu as pltpu
from jax.sharding import PartitionSpec as P

BOX = 48
PLANE = BOX * BOX
CHUNK = PLANE // 6
SCREEN = 0.5
GRID = 4
N_SUB = GRID * GRID
ORB_DEV = 4
PAIRS_DEV = 4
N_PAIRS = N_SUB * PAIRS_DEV

PLACES = ((0, 0), (0, 1), (1, 0), (1, 1), (1, 3), (3, 1))
REGION_SOURCE = len(PLACES)
SOURCES = len(PLACES) + 1
LIST_WIDTH = 16
TASK_WIDTH = 8
LISTED = PAIRS_DEV * LIST_WIDTH
NOTE_ROWS = 16
SET_ROWS = ORB_DEV * BOX
GIVEN = (tuple(range(SOURCES)), tuple(range(SOURCES)), (0, 1, 2, REGION_SOURCE))
FAR_PLACES = (3, 4, 5)
N_TABLES = 4
BLOCKS_Y = 6
BLOCKS_Z = 3
MARGIN = 24
ROWS_PADDED = BOX + 2 * MARGIN
SIDE_Y = 3
SIDE_Z = 2
WIDE_Y = BLOCKS_Y + 2 * SIDE_Y
WIDE_Z = BLOCKS_Z + 2 * SIDE_Z
MAX_TASKS = 2 * len(PLACES) * PAIRS_DEV
HALF_ROOT3 = math.sqrt(3.0) / 2.0
F32 = jnp.float32
BF16 = jnp.bfloat16


def meeting_table():
    found = [[] for _ in range(N_SUB)]
    for i, (ax, az) in enumerate(PLACES):
        for j, (bx, bz) in enumerate(PLACES):
            delta = (ax - bx) % GRID * GRID + (az - bz) % GRID
            found[delta].append(i + 8 * j)
    most = max(len(f) for f in found)
    codes = np.array([f + [f[-1]] * (most - len(f)) for f in found], np.int32)
    counts = np.array([len(f) for f in found], np.int32)
    return np.concatenate([counts, codes.reshape(-1)]), most


def high_low(matrix):
    high = matrix.astype(ml_dtypes.bfloat16)
    low = (matrix - high.astype(np.float64)).astype(ml_dtypes.bfloat16)
    return np.stack([high, low])


def cas(angles):
    return np.cos(angles) + np.sin(angles)


def transform_tables():
    turn = 2.0 * math.pi / BOX
    n = np.arange(BOX)
    line = cas(turn * (n[:, None] * n[None, :] % BOX))
    q, w = np.arange(8), np.arange(16)

    def angle_y(j):
        return turn * (q[:, None] * (6 * q[None, :] + j) % BOX)

    def angle_z(j):
        return turn * (w[:, None] * (3 * w[None, :] + j) % BOX)

    def both_parts(angle):
        c, s = np.cos(angle), np.sin(angle)
        return np.block([[c, -s], [s, c]])

    def planes(y, z, sign):
        whole = angle_y(y)[:, None, :, None] + sign * angle_z(z)[None, :, None, :]
        return both_parts(whole.reshape(128, 128))

    def real_complex(y):
        z = both_parts(angle_z(1)).reshape(2, 16, 2, 16)
        return np.einsum("qm,awbn->aqwbmn", cas(angle_y(y)), z).reshape(256, 256)

    def complex_real(y):
        return np.kron(both_parts(angle_y(y)), cas(angle_z(0)))

    zero = np.zeros((128, 128))
    real = [np.kron(cas(angle_y(y)), cas(angle_z(0))) for y in (0, 3)]
    waves = [np.block([[real[0], zero], [zero, real[1]]]), real_complex(0), real_complex(3)]
    waves += [complex_real(1), complex_real(2)]
    for y in (1, 2):
        waves += [planes(y, 1, 1), planes(y, 1, -1)]
    waves = np.stack(waves)
    lam = 4.0 * np.sin(math.pi * n / BOX) ** 2

    def spectrum(y, z, weight):
        ky, kz = 6 * q + y, 3 * w + z
        total = lam[:, None, None] + lam[ky][None, :, None] + lam[kz][None, None, :] + SCREEN
        return (weight * 4.0 * math.pi / total / float(BOX**3)).reshape(BOX, 128)

    order = [(0, 0, 1.0), (3, 0, 1.0)]
    for y, z in ((0, 1), (3, 1), (1, 0), (2, 0), (1, 1), (1, 1), (2, 1), (2, 1)):
        order += [(y, z, 2.0)] * 2
    green = np.concatenate([spectrum(*o) for o in order], axis=1)
    rows = high_low(line)
    rows = np.block([[rows[0], rows[0]], [rows[1], np.zeros_like(rows[1])]])
    return dict(
        waves=high_low(waves),
        waves_back=high_low(waves.transpose(0, 2, 1)),
        green=green.astype(np.float32),
        rows=rows,
    )


TABLES = ("waves", "waves_back", "green", "rows")


def order_table():
    lane = np.arange(8 * BOX)
    q, c, w = lane // BOX, lane % BOX // 16, lane % 16
    table = np.zeros((8 * BOX, 8 * BOX), np.float32)
    table[lane, c * 128 + q * 16 + w] = 1.0
    return table.astype(ml_dtypes.bfloat16)


def plan_kernel(most, where, meta, offsets, table, chosen, used):
    region, sub, n_region = where[0], where[1], where[2]
    sign = 1 - 2 * (region & 1)
    next_region = jnp.where(region + 1 == n_region, 0, region + 1)
    for i in range(2 * len(PLACES)):
        used[i] = 0

    def place(pair, turn):
        own_slot = meta[pair]
        route = meta[PAIRS_DEV + pair]
        partner_slot = meta[2 * PAIRS_DEV + pair]
        abroad = route == N_SUB
        other = jnp.where(abroad, sub, route)
        dx = (sign * ((other >> 2) - (sub >> 2))) & 3
        dz = (sign * ((other & 3) - (sub & 3))) & 3
        delta = dx * GRID + dz
        count = jnp.where(abroad, 1, table[delta])

        @pl.when(jnp.where(count == 1, 0, 1) == turn)
        def _():
            row = pair * LIST_WIDTH
            for kind in range(3):
                load_of = len(PLACES) * min(kind, 1)
                best_load = jnp.int32(1 << 20)
                best_code = jnp.int32(0)
                for k in range(most):
                    code = table[N_SUB + delta * most + k]
                    load = used[load_of + (code & 7)]
                    better = load < best_load
                    best_load = jnp.where(better, load, best_load)
                    best_code = jnp.where(better, code, best_code)
                at = jnp.where(abroad, 0, best_code & 7)
                used[load_of + at] = used[load_of + at] + 1
                chosen[row + 2 * kind] = at
                chosen[row + 2 * kind + 1] = jnp.where(
                    abroad, REGION_SOURCE, (best_code >> 3) & 7
                )
            first = (region * N_SUB + sub) * ORB_DEV + own_slot
            second_region = jnp.where(abroad, next_region, region)
            second = (second_region * N_SUB + other) * ORB_DEV + partner_slot
            chosen[row + 6] = own_slot
            chosen[row + 7] = partner_slot
            for c in range(3):
                chosen[row + 8 + c] = offsets[first * 3 + c] - offsets[second * 3 + c]
            for c in range(11, LIST_WIDTH):
                chosen[row + c] = 0

    for turn in range(2):
        for pair in range(PAIRS_DEV):
            place(pair, turn)


def three_dots(high, low, weights, index):
    boxes_high = jnp.concatenate([high, low], axis=0)
    half = high.shape[0]
    wide = jnp.dot(boxes_high, weights[0, index], preferred_element_type=F32)
    rest = jnp.dot(high, weights[1, index], preferred_element_type=F32)
    return wide[:half] + wide[half:] + rest


def split(value):
    high = value.astype(BF16)
    return high, (value - high.astype(F32)).astype(BF16)


def six_points(x):
    u = [x[r] + x[r + 3] for r in range(3)]
    v = [x[r] - x[r + 3] for r in range(3)]
    return (
        u[0] + u[1] + u[2],
        v[0] - v[1] + v[2],
        v[0] + 0.5 * (v[1] - v[2]),
        -HALF_ROOT3 * (v[1] + v[2]),
        u[0] - 0.5 * (u[1] + u[2]),
        -HALF_ROOT3 * (u[1] - u[2]),
    )


def six_points_back(t0, t3, t1r, t1i, t2r, t2i):
    a0 = t0 + t2r
    t2h = t0 - 0.5 * t2r
    t2s = HALF_ROOT3 * t2i
    a1 = t2h - t2s
    a2 = t2h + t2s
    t1s = HALF_ROOT3 * t1i
    b0 = t3 + t1r
    b1 = 0.5 * t1r - t3 - t1s
    b2 = t3 - 0.5 * t1r - t1s
    return a0 + b0, a1 + b1, a2 + b2, a0 - b0, a1 - b1, a2 - b2


def three_points(x):
    total = x[1] + x[2]
    return x[0] + total, x[0] - 0.5 * total, -HALF_ROOT3 * (x[1] - x[2])


def three_points_back(s0, s1r, s1i):
    low = s0 - 0.5 * s1r
    turned = HALF_ROOT3 * s1i
    return s0 + s1r, low - turned, low + turned


def solve(density, both, work, waves, waves_back, green, rows, boxes):
    for b in range(boxes):
        for g in range(BOX // 16):
            some = pl.ds(b * BOX + g * 16, 16)
            low_some = pl.ds((boxes + b) * BOX + g * 16, 16)
            columns = []
            for c in range(BLOCKS_Z):
                x = [density(b, pl.ds(g * 16, 16), r, c) for r in range(BLOCKS_Y)]
                columns.append(six_points(x))
            t = [three_points([columns[c][j] for c in range(BLOCKS_Z)]) for j in range(6)]
            parts = [t[0][0], t[1][0], t[0][1], t[0][2], t[1][1], t[1][2]]
            parts += [t[2][0], t[3][0], t[4][0], t[5][0]]
            for j in (2, 4):
                (_, rr, ri), (_, ir, ii) = t[j], t[j + 1]
                parts += [rr - ii, ri + ir, rr + ii, ir - ri]
            for i, part in enumerate(parts):
                high, low = split(part)
                both[some, pl.ds(i * 128, 128)] = high
                both[low_some, pl.ds(i * 128, 128)] = low

    def row_pass(value):
        stacked = jnp.concatenate(split(value), axis=0)
        result = jnp.dot(rows[...], stacked, preferred_element_type=F32)
        return result[:BOX] + result[BOX:]

    def plane_pass(weights):
        for group in range(9):
            lanes = pl.ds(group * 256, 256)
            high = both[pl.ds(0, boxes * BOX), lanes]
            low = both[pl.ds(boxes * BOX, boxes * BOX), lanes]
            work[:, lanes] = three_dots(high, low, weights, group)

    places = [
        (pl.ds(b * BOX, BOX), pl.ds((boxes + b) * BOX, BOX), pl.ds(group * 256, 256))
        for b in range(boxes)
        for group in range(9)
    ]
    plane_pass(waves)
    for some, _, lanes in places:
        work[some, lanes] = row_pass(work[some, lanes]) * green[:, lanes]
    for some, low_some, lanes in places:
        both[some, lanes], both[low_some, lanes] = split(row_pass(work[some, lanes]))
    plane_pass(waves_back)

    for b in range(boxes):
        for g in range(BOX // 16):
            some = pl.ds(b * BOX + g * 16, 16)
            p = [work[some, pl.ds(i * 128, 128)] for i in range(18)]
            t = [[p[0], p[2], p[3]], [p[1], p[4], p[5]]]
            for j in range(2):
                pr, pi, mr, mi = p[10 + 4 * j : 14 + 4 * j]
                t.append([p[6 + 2 * j], pr + mr, pi - mi])
                t.append([p[7 + 2 * j], pi + mi, mr - pr])
            t = [three_points_back(*parts) for parts in t]
            for c in range(BLOCKS_Z):
                values = six_points_back(*[t[j][c] for j in range(6)])
                for r, value in enumerate(values):
                    work[some, pl.ds((r * BLOCKS_Z + c) * 128, 128)] = value


def rounded(value):
    return value.astype(BF16).astype(F32)


def shift_box(padded, value, put, dx, dy, dz):
    for r in range(BLOCKS_Y):
        for c in range(BLOCKS_Z):
            at = ((r + SIDE_Y) * WIDE_Z + c + SIDE_Z) * ROWS_PADDED + MARGIN
            padded[pl.ds(at, BOX), :] = value(pl.ds((r * BLOCKS_Z + c) * 128, 128))
    fine_y, fine_z = dy & 7, dz & 15
    start = ((dy >> 3) + SIDE_Y) * WIDE_Z + (dz >> 4) + SIDE_Z
    base = start * ROWS_PADDED + MARGIN + dx
    lane = lax.broadcasted_iota(jnp.int32, (1, 128), 1)
    next_y = (lane >> 4) < fine_y
    next_z = (lane & 15) < fine_z
    carried = (lane & 15) + fine_z >= 16
    ahead = fine_y * 16 + fine_z
    turn = (128 - ahead) & 127
    turn_carried = (128 + 16 - ahead) & 127

    def block(r, c):
        return padded[pl.ds(base + (r * WIDE_Z + c) * ROWS_PADDED, BOX), :]

    for r in range(BLOCKS_Y):
        mixed = [jnp.where(next_y, block(r + 1, c), block(r, c)) for c in range(BLOCKS_Z + 1)]
        for c in range(BLOCKS_Z):
            source = jnp.where(next_z, mixed[c + 1], mixed[c])
            out = jnp.where(
                carried, pltpu.roll(source, turn_carried, 1), pltpu.roll(source, turn, 1)
            )
            put(pl.ds((r * BLOCKS_Z + c) * 128, 128), out)


def exchange_kernel(part, *refs):
    second = part > 0
    sets = 2 if second else 1
    given = GIVEN[part]
    carried = len(given) if part == 2 else 0
    n_in = sets * (SOURCES + 1)
    listing, *refs = refs
    boxes_in, refs = refs[:n_in], refs[n_in:]
    tables_in, refs = refs[:N_TABLES], refs[N_TABLES:]
    sums_in, refs = refs[:carried], refs[carried:]
    outs, refs = refs[: len(given)], refs[len(given) :]
    tables, refs = refs[:N_TABLES], refs[N_TABLES:]
    acc, stage, held, theirs, both, work, padded, mine, sems, table_sems, out_sems = refs

    mine[0] = 0
    for home in range(len(PLACES)):

        def check(pair, carry, home=home):
            row = (home * PAIRS_DEV + pair) * LIST_WIDTH
            for kind in (1, 2) if second else (0,):
                here = listing[row + 2 * kind] == home
                if second:
                    gives_far = jnp.bool_(home in FAR_PLACES)
                    if kind == 2:
                        source = listing[row + 2 * kind + 1]
                        gives_far = (source >= FAR_PLACES[0]) & (source <= FAR_PLACES[-1])
                    here &= gives_far if part == 1 else jnp.logical_not(gives_far)

                @pl.when(here)
                def _(kind=kind):
                    at = mine[0]
                    mine[0] = at + 1
                    task = (at + 1) * TASK_WIDTH
                    mine[task] = home
                    mine[task + 1] = listing[row + 2 * kind + 1]
                    for c in range(5):
                        mine[task + 2 + c] = listing[row + 6 + c]
                    mine[task + 7] = kind

            return carry

        lax.fori_loop(0, PAIRS_DEV, check, 0)

    count = mine[0]
    steps = (count + 1) >> 1
    begin, end = 0, steps

    def table_copies():
        return [
            pltpu.make_async_copy(tables_in[i], tables[i], table_sems.at[i])
            for i in range(N_TABLES)
        ]

    def fetch(group, source, slot, target, sem):
        refs_of = boxes_in[group * (SOURCES + 1) : (group + 1) * (SOURCES + 1)]

        def start(ref, row):
            row = pl.multiple_of(row, 16)
            pltpu.make_async_copy(ref.at[pl.ds(row, BOX)], target, sem).start()

        for s in range(SOURCES):
            if s == 3:
                for part_of in range(2):

                    @pl.when((source == s) & ((slot >> 1) == part_of))
                    def _(part_of=part_of):
                        start(refs_of[3 + part_of], (slot & 1) * BOX)
            else:
                at = s if s < 3 else s + 1

                @pl.when(source == s)
                def _(at=at):
                    start(refs_of[at], slot * BOX)

    def each_load(step, act):
        for i in range(2):
            task = (step * 2 + i + 1) * TASK_WIDTH

            @pl.when(step * 2 + i < count)
            def _(i=i, task=task):
                kind = mine[task + 7]
                act(kind == 1, mine[task], mine[task + 2], 2 * i)
                act(kind == 2, mine[task + 1], mine[task + 3], 2 * i + 1)

    def start_loads(step, buffer):
        def act(of_trial, source, slot, i):
            if second:

                @pl.when(of_trial)
                def _():
                    fetch(1, source, slot, held.at[buffer, i], sems.at[buffer, i])

                @pl.when(jnp.logical_not(of_trial))
                def _():
                    fetch(0, source, slot, held.at[buffer, i], sems.at[buffer, i])
            else:
                fetch(0, source, slot, held.at[buffer, i], sems.at[buffer, i])

        each_load(step, act)

    def wait_loads(step, buffer):
        def act(of_trial, source, slot, i):
            pltpu.make_async_copy(
                boxes_in[0].at[pl.ds(0, BOX)], held.at[buffer, i], sems.at[buffer, i]
            ).wait()

        each_load(step, act)

    def sum_copies(into):
        copies = []
        for i, source in enumerate(given):
            vmem = stage.at[pl.ds(source * SET_ROWS, SET_ROWS)]
            if into:
                copies.append(pltpu.make_async_copy(sums_in[i], vmem, out_sems.at[i]))
            else:
                copies.append(pltpu.make_async_copy(vmem, outs[i], out_sems.at[i]))
        return copies

    @pl.when(begin < end)
    def _():
        start_loads(begin, begin & 1)
        for copy in table_copies():
            copy.start()

    if carried:
        for copy in sum_copies(True):
            copy.start()
    padded[...] = jnp.zeros(padded.shape, F32)

    def box_rows(i):
        return pl.ds(pl.multiple_of(i * BOX, BOX), BOX)

    if carried:
        for copy in sum_copies(True):
            copy.wait()

    def prepare(i, carry):
        if carried:
            keep = stage[box_rows(i), :].astype(F32)
            is_given = (i < 3 * ORB_DEV) | (i >= REGION_SOURCE * ORB_DEV)
            acc[box_rows(i), :] = jnp.where(is_given, keep, 0.0)
        else:
            acc[box_rows(i), :] = jnp.zeros((BOX, PLANE), F32)
        return carry

    lax.fori_loop(0, SOURCES * ORB_DEV, prepare, 0)

    def add(source, slot, lanes, value):
        at = box_rows(source * ORB_DEV + slot)
        acc[at, lanes] = acc[at, lanes] + value

    def one_step(step, carry):
        buffer = step & 1

        @pl.when(step + 1 < end)
        def _():
            start_loads(step + 1, 1 - buffer)

        wait_loads(step, buffer)
        for i in range(2):
            task = (step * 2 + i + 1) * TASK_WIDTH

            @pl.when(step * 2 + i < count)
            def _(i=i, task=task):
                def value(lanes):
                    return held[buffer, 2 * i + 1, :, lanes].astype(F32)

                def put(lanes, block):
                    theirs[i, :, lanes] = block

                shift_box(padded, value, put, mine[task + 4], mine[task + 5], mine[task + 6])

        @pl.when(step == begin)
        def _():
            for copy in table_copies():
                copy.wait()

        def density(b, some, r, c):
            lanes = pl.ds((r * BLOCKS_Z + c) * 128, 128)
            return held[buffer, 2 * b, some, lanes].astype(F32) * theirs[b, some, lanes]

        solve(density, both, work, *tables, 2)
        for i in range(2):
            task = (step * 2 + i + 1) * TASK_WIDTH
            there = step * 2 + i < count
            kind = mine[task + 7]

            @pl.when(there & (kind != 2))
            def _(i=i, task=task):
                near = rounded(work[pl.ds(i * BOX, BOX), :] * theirs[i])
                add(mine[task], mine[task + 2], pl.ds(0, PLANE), near)

            @pl.when(there & (kind != 1))
            def _(i=i, task=task):
                def value(lanes):
                    mine_box = held[buffer, 2 * i, :, lanes].astype(F32)
                    return rounded(work[pl.ds(i * BOX, BOX), lanes] * mine_box)

                def put(lanes, block):
                    add(mine[task + 1], mine[task + 3], lanes, block)

                shift_box(padded, value, put, -mine[task + 4], -mine[task + 5], -mine[task + 6])

        return carry

    lax.fori_loop(begin, end, one_step, 0)

    copies = sum_copies(False)
    for copy, source in zip(copies, given):

        def put(i, carry):
            stage[box_rows(i), :] = acc[box_rows(i), :].astype(BF16)
            return carry

        lax.fori_loop(source * ORB_DEV, (source + 1) * ORB_DEV, put, 0)
        copy.start()
    for copy in copies:
        copy.wait()


def exchange(part, listing, boxes, tables, sums=()):
    any_space = pl.BlockSpec(memory_space=pl.ANY)
    smem = pl.BlockSpec(memory_space=pltpu.SMEM)
    outs = [
        jax.ShapeDtypeStruct((SET_ROWS, PLANE), BF16) for _ in GIVEN[part]
    ]

    def kernel(*refs):
        exchange_kernel(part, *refs)

    return pl.pallas_call(
        kernel,
        out_shape=outs,
        in_specs=[smem] + [any_space] * (len(boxes) + len(tables) + len(sums)),
        out_specs=[any_space] * len(outs),
        scratch_shapes=[
            *[pltpu.VMEM(t.shape, t.dtype) for t in tables],
            pltpu.VMEM((SOURCES * ORB_DEV * BOX, PLANE), F32),
            pltpu.VMEM((SOURCES * ORB_DEV * BOX, PLANE), BF16),
            pltpu.VMEM((2, 4, BOX, PLANE), BF16),
            pltpu.VMEM((2, BOX, PLANE), F32),
            pltpu.VMEM((4 * BOX, PLANE), BF16),
            pltpu.VMEM((2 * BOX, PLANE), F32),
            pltpu.VMEM((WIDE_Y * WIDE_Z * ROWS_PADDED, 128), F32),
            pltpu.SMEM(((MAX_TASKS + 3) * TASK_WIDTH,), jnp.int32),
            pltpu.SemaphoreType.DMA((2, 4)),
            pltpu.SemaphoreType.DMA((N_TABLES,)),
            pltpu.SemaphoreType.DMA((SOURCES,)),
        ],
        compiler_params=pltpu.CompilerParams(vmem_limit_bytes=56 * 1024 * 1024),
        cost_estimate=pl.CostEstimate(
            flops=10_000_000_000, bytes_accessed=30_000_000, transcendentals=0
        ),
        name=("first_application", "second_early", "second_late")[part],
    )(listing, *boxes, *tables, *sums)


def reorder_kernel(with_notes, box, *refs):
    order, out = refs[-2:]
    for r in range(BLOCKS_Y):
        lanes = pl.ds(r * CHUNK, CHUNK)
        moved = jnp.dot(box[:, lanes], order[...], preferred_element_type=F32)
        out[pl.ds(0, SET_ROWS), lanes] = moved.astype(BF16)
    if with_notes:
        out[pl.ds(SET_ROWS, NOTE_ROWS), :] = refs[0][...]


def reorder(boxes, order, notes=()):
    rows = SET_ROWS + NOTE_ROWS * len(notes)

    def kernel(*refs):
        reorder_kernel(bool(notes), *refs)

    return pl.pallas_call(
        kernel,
        out_shape=jax.ShapeDtypeStruct((rows, PLANE), BF16),
        name="reorder",
        compiler_params=pltpu.CompilerParams(vmem_limit_bytes=32 * 1024 * 1024),
    )(boxes, *notes, order)


def total_kernel(*refs):
    *parts, order, out = refs
    for r in range(BLOCKS_Y):
        lanes = pl.ds(r * CHUNK, CHUNK)
        result = parts[0][:, lanes].astype(F32)
        for part in parts[1:]:
            result += part[:, lanes].astype(F32)
        moved = jnp.dot((-result).astype(BF16), order[...], preferred_element_type=F32)
        out[:, lanes] = moved.astype(BF16)


def total(parts, order):
    half = SET_ROWS // 2
    whole = pl.BlockSpec((CHUNK, CHUNK), lambda i: (0, 0))
    some = pl.BlockSpec((half, PLANE), lambda i: (i, 0))
    return pl.pallas_call(
        total_kernel,
        grid=(2,),
        out_shape=jax.ShapeDtypeStruct((SET_ROWS, PLANE), BF16),
        in_specs=[some] * len(parts) + [whole],
        out_specs=some,
        name="total",
        compiler_params=pltpu.CompilerParams(vmem_limit_bytes=32 * 1024 * 1024),
    )(*parts, order)


def moves(n_region):
    def step(dx, dz):
        pairs = []
        for region in range(n_region):
            sign = 1 - 2 * (region % 2)
            for x in range(GRID):
                for z in range(GRID):
                    to = (x + sign * dx) % GRID * GRID + (z + sign * dz) % GRID
                    pairs.append((region * N_SUB + x * GRID + z, region * N_SUB + to))

        def move(block):
            return lax.ppermute(block, ("region", "sub"), pairs)

        return move

    def across(distance):
        pairs = [(i, (i + distance) % n_region) for i in range(n_region)]

        def move(block):
            return lax.ppermute(block, "region", pairs)

        return move

    return step, across


def per_device(orbitals, trial_set, own_slot, partner_route, partner_slot, offsets):
    n_region = lax.axis_size("region")
    region = lax.axis_index("region")
    sub = lax.axis_index("sub")
    step, across = moves(n_region)
    tables = transform_tables()
    tables = [
        jnp.asarray(tables[k])
        for k in TABLES
    ]
    order, order_back = jnp.asarray(order_table()), jnp.asarray(order_table().T.copy())
    table, most = meeting_table()
    meta = jnp.concatenate([own_slot, partner_route[:, 0], partner_slot])
    where = jnp.stack([region, sub, jnp.int32(n_region)]).astype(jnp.int32)
    smem = pl.BlockSpec(memory_space=pltpu.SMEM)

    def planner(*refs):
        plan_kernel(most, *refs)

    chosen = pl.pallas_call(
        planner,
        out_shape=jax.ShapeDtypeStruct((LISTED,), jnp.int32),
        in_specs=[smem] * 4,
        out_specs=smem,
        scratch_shapes=[pltpu.SMEM((2 * len(PLACES),), jnp.int32)],
        name="plan",
    )(where, meta, offsets.reshape(-1), jnp.asarray(table))

    def near_places(boxes):
        return step(0, 1)(boxes), step(1, 0)(boxes), across(-1)(boxes)

    def cut(b01, b10):
        return b01[: 2 * BOX], b10[2 * BOX :]

    def far_places(b01, b10, halves):
        low, high = halves
        return step(1, 0)(low), step(0, 1)(high), step(0, -1)(b10), step(-1, 0)(b01)

    def begin_back(parts):
        return step(-1, 0)(parts[3]), step(0, 1)(parts[4]), step(1, 0)(parts[5])

    def merge(c01, c10, arrived):
        r11, r13, r31 = arrived
        m01 = (c01.astype(F32) + r31.astype(F32) + r11.astype(F32)).astype(BF16)
        m10 = (c10.astype(F32) + r13.astype(F32)).astype(BF16)
        return step(0, -1)(m01), step(-1, 0)(m10)

    def finish(own, abroad, merged):
        result = total([own, abroad, *merged], order_back)
        return result.reshape(ORB_DEV, BOX, PLANE)

    ordered = lax.optimization_barrier
    notes = jnp.pad(chosen.astype(BF16)[None], ((0, NOTE_ROWS - 1), (0, PLANE - LISTED)))
    trials = reorder(trial_set.reshape(SET_ROWS, PLANE), order)
    boxes = reorder(orbitals.reshape(SET_ROWS, PLANE), order, (notes,))
    t01, t10, t_abroad = near_places(trials)
    boxes, t01, t10, t_abroad = ordered((boxes, t01, t10, t_abroad))
    t_cut = cut(t01, t10)
    o01, o10, o_abroad = near_places(boxes)
    o01, o10, o_abroad, t_cut = ordered((o01, o10, o_abroad, t_cut))
    o_far = far_places(o01, o10, cut(o01, o10))
    t01, t10, t_cut, o_far = ordered((t01, t10, t_cut, o_far))
    t_far = far_places(t01, t10, t_cut)
    orbital_boxes = [boxes, o01, o10, *o_far, o_abroad]
    notes = [boxes, o01, o10, o_far[1], o_far[2], o_far[3]]
    listing = jnp.concatenate([n[-NOTE_ROWS, :LISTED] for n in notes]).astype(jnp.int32)
    first = exchange(0, listing, orbital_boxes, tables)
    arrived_first = begin_back(first)
    abroad_first = across(1)(first[6])
    first, listing, t_far = ordered((first, listing, t_far))
    all_boxes = orbital_boxes + [trials, t01, t10, *t_far, t_abroad]
    early = exchange(1, listing, all_boxes, tables)
    early, first, arrived_first, abroad_first = ordered((early, first, arrived_first, abroad_first))
    merged_first = merge(first[1], first[2], arrived_first)
    arrived_second = begin_back(early)
    late = exchange(2, listing, all_boxes, tables, [early[i] for i in GIVEN[2]])
    late, merged_first, arrived_second = ordered((late, merged_first, arrived_second))
    own, c01, c10, c_abroad = late
    abroad_second = across(1)(c_abroad)
    merged_second = merge(c01, c10, arrived_second)
    result_first = finish(first[0], abroad_first, merged_first)
    return result_first, finish(own, abroad_second, merged_second)


def solution(mesh):
    in_specs = (
        P(("region", "sub"), None, None),
        P(("region", "sub"), None, None),
        P(("region", "sub")),
        P(("region", "sub"), None),
        P(("region", "sub")),
        P(),
    )
    out_specs = (P(("region", "sub"), None, None), P(("region", "sub"), None, None))
    return jax.shard_map(
        per_device, mesh=mesh, in_specs=in_specs, out_specs=out_specs, check_vma=False
    )
```

```python
import math

import jax
import jax.numpy as jnp
import ml_dtypes
import numpy as np
from jax import lax
from jax.experimental import pallas as pl
from jax.experimental.pallas import tpu as pltpu
from jax.sharding import PartitionSpec as P

BOX = 48
PLANE = BOX * BOX
CHUNK = PLANE // 6
SCREEN = 0.5
GRID = 4
N_SUB = GRID * GRID
ORB_DEV = 4
PAIRS_DEV = 4
N_PAIRS = N_SUB * PAIRS_DEV

PLACES = ((0, 0), (0, 1), (1, 0), (1, 1), (1, 3), (3, 1))
REGION_SOURCE = len(PLACES)
SOURCES = len(PLACES) + 1
LIST_WIDTH = 16
TASK_WIDTH = 8
LISTED = PAIRS_DEV * LIST_WIDTH
NOTE_ROWS = 16
SET_ROWS = ORB_DEV * BOX
GIVEN = (tuple(range(SOURCES)), tuple(range(SOURCES)), (0, 1, 2, REGION_SOURCE))
FAR_PLACES = (3, 4, 5)
N_TABLES = 4
BLOCKS_Y = 6
BLOCKS_Z = 3
MARGIN = 24
ROWS_PADDED = BOX + 2 * MARGIN
SIDE_Y = 3
SIDE_Z = 2
WIDE_Y = BLOCKS_Y + 2 * SIDE_Y
WIDE_Z = BLOCKS_Z + 2 * SIDE_Z
MAX_TASKS = 2 * len(PLACES) * PAIRS_DEV
HALF_ROOT3 = math.sqrt(3.0) / 2.0
F32 = jnp.float32
BF16 = jnp.bfloat16


def meeting_table():
    found = [[] for _ in range(N_SUB)]
    for i, (ax, az) in enumerate(PLACES):
        for j, (bx, bz) in enumerate(PLACES):
            delta = (ax - bx) % GRID * GRID + (az - bz) % GRID
            found[delta].append(i + 8 * j)
    most = max(len(f) for f in found)
    codes = np.array([f + [f[-1]] * (most - len(f)) for f in found], np.int32)
    counts = np.array([len(f) for f in found], np.int32)
    return np.concatenate([counts, codes.reshape(-1)]), most


def high_low(matrix):
    high = matrix.astype(ml_dtypes.bfloat16)
    low = (matrix - high.astype(np.float64)).astype(ml_dtypes.bfloat16)
    return np.stack([high, low])


def cas(angles):
    return np.cos(angles) + np.sin(angles)


def transform_tables():
    turn = 2.0 * math.pi / BOX
    n = np.arange(BOX)
    line = cas(turn * (n[:, None] * n[None, :] % BOX))
    q, w = np.arange(8), np.arange(16)

    def angle_y(j):
        return turn * (q[:, None] * (6 * q[None, :] + j) % BOX)

    def angle_z(j):
        return turn * (w[:, None] * (3 * w[None, :] + j) % BOX)

    def both_parts(angle):
        c, s = np.cos(angle), np.sin(angle)
        return np.block([[c, -s], [s, c]])

    def planes(y, z, sign):
        whole = angle_y(y)[:, None, :, None] + sign * angle_z(z)[None, :, None, :]
        return both_parts(whole.reshape(128, 128))

    def real_complex(y):
        z = both_parts(angle_z(1)).reshape(2, 16, 2, 16)
        return np.einsum("qm,awbn->aqwbmn", cas(angle_y(y)), z).reshape(256, 256)

    def complex_real(y):
        return np.kron(both_parts(angle_y(y)), cas(angle_z(0)))

    zero = np.zeros((128, 128))
    real = [np.kron(cas(angle_y(y)), cas(angle_z(0))) for y in (0, 3)]
    waves = [np.block([[real[0], zero], [zero, real[1]]]), real_complex(0), real_complex(3)]
    waves += [complex_real(1), complex_real(2)]
    for y in (1, 2):
        waves += [planes(y, 1, 1), planes(y, 1, -1)]
    waves = np.stack(waves)
    lam = 4.0 * np.sin(math.pi * n / BOX) ** 2

    def spectrum(y, z, weight):
        ky, kz = 6 * q + y, 3 * w + z
        total = lam[:, None, None] + lam[ky][None, :, None] + lam[kz][None, None, :] + SCREEN
        return (weight * 4.0 * math.pi / total / float(BOX**3)).reshape(BOX, 128)

    order = [(0, 0, 1.0), (3, 0, 1.0)]
    for y, z in ((0, 1), (3, 1), (1, 0), (2, 0), (1, 1), (1, 1), (2, 1), (2, 1)):
        order += [(y, z, 2.0)] * 2
    green = np.concatenate([spectrum(*o) for o in order], axis=1)
    rows = high_low(line)
    rows = np.block([[rows[0], rows[0]], [rows[1], np.zeros_like(rows[1])]])
    return dict(
        waves=high_low(waves),
        waves_back=high_low(waves.transpose(0, 2, 1)),
        green=green.astype(np.float32),
        rows=rows,
    )


TABLES = ("waves", "waves_back", "green", "rows")


def order_table():
    lane = np.arange(8 * BOX)
    q, c, w = lane // BOX, lane % BOX // 16, lane % 16
    table = np.zeros((8 * BOX, 8 * BOX), np.float32)
    table[lane, c * 128 + q * 16 + w] = 1.0
    return table.astype(ml_dtypes.bfloat16)


def plan_kernel(most, where, meta, offsets, table, chosen, used):
    region, sub, n_region = where[0], where[1], where[2]
    sign = 1 - 2 * (region & 1)
    next_region = jnp.where(region + 1 == n_region, 0, region + 1)
    for i in range(2 * len(PLACES)):
        used[i] = 0

    def place(pair, turn):
        own_slot = meta[pair]
        route = meta[PAIRS_DEV + pair]
        partner_slot = meta[2 * PAIRS_DEV + pair]
        abroad = route == N_SUB
        other = jnp.where(abroad, sub, route)
        dx = (sign * ((other >> 2) - (sub >> 2))) & 3
        dz = (sign * ((other & 3) - (sub & 3))) & 3
        delta = dx * GRID + dz
        count = jnp.where(abroad, 1, table[delta])

        @pl.when(jnp.where(count == 1, 0, 1) == turn)
        def _():
            row = pair * LIST_WIDTH
            for kind in range(3):
                load_of = len(PLACES) * min(kind, 1)
                best_load = jnp.int32(1 << 20)
                best_code = jnp.int32(0)
                for k in range(most):
                    code = table[N_SUB + delta * most + k]
                    load = used[load_of + (code & 7)]
                    better = load < best_load
                    best_load = jnp.where(better, load, best_load)
                    best_code = jnp.where(better, code, best_code)
                at = jnp.where(abroad, 0, best_code & 7)
                used[load_of + at] = used[load_of + at] + 1
                chosen[row + 2 * kind] = at
                chosen[row + 2 * kind + 1] = jnp.where(
                    abroad, REGION_SOURCE, (best_code >> 3) & 7
                )
            first = (region * N_SUB + sub) * ORB_DEV + own_slot
            second_region = jnp.where(abroad, next_region, region)
            second = (second_region * N_SUB + other) * ORB_DEV + partner_slot
            chosen[row + 6] = own_slot
            chosen[row + 7] = partner_slot
            for c in range(3):
                chosen[row + 8 + c] = offsets[first * 3 + c] - offsets[second * 3 + c]
            for c in range(11, LIST_WIDTH):
                chosen[row + c] = 0

    for turn in range(2):
        for pair in range(PAIRS_DEV):
            place(pair, turn)


def three_dots(high, low, weights, index):
    boxes_high = jnp.concatenate([high, low], axis=0)
    half = high.shape[0]
    wide = jnp.dot(boxes_high, weights[0, index], preferred_element_type=F32)
    rest = jnp.dot(high, weights[1, index], preferred_element_type=F32)
    return wide[:half] + wide[half:] + rest


def split(value):
    high = value.astype(BF16)
    return high, (value - high.astype(F32)).astype(BF16)


def six_points(x):
    u = [x[r] + x[r + 3] for r in range(3)]
    v = [x[r] - x[r + 3] for r in range(3)]
    return (
        u[0] + u[1] + u[2],
        v[0] - v[1] + v[2],
        v[0] + 0.5 * (v[1] - v[2]),
        -HALF_ROOT3 * (v[1] + v[2]),
        u[0] - 0.5 * (u[1] + u[2]),
        -HALF_ROOT3 * (u[1] - u[2]),
    )


def six_points_back(t0, t3, t1r, t1i, t2r, t2i):
    a0 = t0 + t2r
    t2h = t0 - 0.5 * t2r
    t2s = HALF_ROOT3 * t2i
    a1 = t2h - t2s
    a2 = t2h + t2s
    t1s = HALF_ROOT3 * t1i
    b0 = t3 + t1r
    b1 = 0.5 * t1r - t3 - t1s
    b2 = t3 - 0.5 * t1r - t1s
    return a0 + b0, a1 + b1, a2 + b2, a0 - b0, a1 - b1, a2 - b2


def three_points(x):
    total = x[1] + x[2]
    return x[0] + total, x[0] - 0.5 * total, -HALF_ROOT3 * (x[1] - x[2])


def three_points_back(s0, s1r, s1i):
    low = s0 - 0.5 * s1r
    turned = HALF_ROOT3 * s1i
    return s0 + s1r, low - turned, low + turned


def solve(density, both, work, waves, waves_back, green, rows, boxes):
    for b in range(boxes):
        for g in range(BOX // 16):
            some = pl.ds(b * BOX + g * 16, 16)
            low_some = pl.ds((boxes + b) * BOX + g * 16, 16)
            columns = []
            for c in range(BLOCKS_Z):
                x = [density(b, pl.ds(g * 16, 16), r, c) for r in range(BLOCKS_Y)]
                columns.append(six_points(x))
            t = [three_points([columns[c][j] for c in range(BLOCKS_Z)]) for j in range(6)]
            parts = [t[0][0], t[1][0], t[0][1], t[0][2], t[1][1], t[1][2]]
            parts += [t[2][0], t[3][0], t[4][0], t[5][0]]
            for j in (2, 4):
                (_, rr, ri), (_, ir, ii) = t[j], t[j + 1]
                parts += [rr - ii, ri + ir, rr + ii, ir - ri]
            for i, part in enumerate(parts):
                high, low = split(part)
                both[some, pl.ds(i * 128, 128)] = high
                both[low_some, pl.ds(i * 128, 128)] = low

    def row_pass(value):
        stacked = jnp.concatenate(split(value), axis=0)
        result = jnp.dot(rows[...], stacked, preferred_element_type=F32)
        return result[:BOX] + result[BOX:]

    def plane_pass(weights):
        for group in range(9):
            lanes = pl.ds(group * 256, 256)
            high = both[pl.ds(0, boxes * BOX), lanes]
            low = both[pl.ds(boxes * BOX, boxes * BOX), lanes]
            work[:, lanes] = three_dots(high, low, weights, group)

    places = [
        (pl.ds(b * BOX, BOX), pl.ds((boxes + b) * BOX, BOX), pl.ds(group * 256, 256))
        for b in range(boxes)
        for group in range(9)
    ]
    plane_pass(waves)
    for some, _, lanes in places:
        work[some, lanes] = row_pass(work[some, lanes]) * green[:, lanes]
    for some, low_some, lanes in places:
        both[some, lanes], both[low_some, lanes] = split(row_pass(work[some, lanes]))
    plane_pass(waves_back)

    for b in range(boxes):
        for g in range(BOX // 16):
            some = pl.ds(b * BOX + g * 16, 16)
            p = [work[some, pl.ds(i * 128, 128)] for i in range(18)]
            t = [[p[0], p[2], p[3]], [p[1], p[4], p[5]]]
            for j in range(2):
                pr, pi, mr, mi = p[10 + 4 * j : 14 + 4 * j]
                t.append([p[6 + 2 * j], pr + mr, pi - mi])
                t.append([p[7 + 2 * j], pi + mi, mr - pr])
            t = [three_points_back(*parts) for parts in t]
            for c in range(BLOCKS_Z):
                values = six_points_back(*[t[j][c] for j in range(6)])
                for r, value in enumerate(values):
                    work[some, pl.ds((r * BLOCKS_Z + c) * 128, 128)] = value


def rounded(value):
    return value.astype(BF16).astype(F32)


def shift_box(padded, value, put, dx, dy, dz):
    for r in range(BLOCKS_Y):
        for c in range(BLOCKS_Z):
            at = ((r + SIDE_Y) * WIDE_Z + c + SIDE_Z) * ROWS_PADDED + MARGIN
            padded[pl.ds(at, BOX), :] = value(pl.ds((r * BLOCKS_Z + c) * 128, 128))
    fine_y, fine_z = dy & 7, dz & 15
    start = ((dy >> 3) + SIDE_Y) * WIDE_Z + (dz >> 4) + SIDE_Z
    base = start * ROWS_PADDED + MARGIN + dx
    lane = lax.broadcasted_iota(jnp.int32, (1, 128), 1)
    next_y = (lane >> 4) < fine_y
    next_z = (lane & 15) < fine_z
    carried = (lane & 15) + fine_z >= 16
    ahead = fine_y * 16 + fine_z
    turn = (128 - ahead) & 127
    turn_carried = (128 + 16 - ahead) & 127

    def block(r, c):
        return padded[pl.ds(base + (r * WIDE_Z + c) * ROWS_PADDED, BOX), :]

    for r in range(BLOCKS_Y):
        mixed = [jnp.where(next_y, block(r + 1, c), block(r, c)) for c in range(BLOCKS_Z + 1)]
        for c in range(BLOCKS_Z):
            source = jnp.where(next_z, mixed[c + 1], mixed[c])
            out = jnp.where(
                carried, pltpu.roll(source, turn_carried, 1), pltpu.roll(source, turn, 1)
            )
            put(pl.ds((r * BLOCKS_Z + c) * 128, 128), out)


def exchange_kernel(part, *refs):
    second = part > 0
    sets = 2 if second else 1
    given = GIVEN[part]
    carried = len(given) if part == 2 else 0
    n_in = sets * (SOURCES + 1)
    listing, *refs = refs
    boxes_in, refs = refs[:n_in], refs[n_in:]
    tables_in, refs = refs[:N_TABLES], refs[N_TABLES:]
    sums_in, refs = refs[:carried], refs[carried:]
    outs, refs = refs[: len(given)], refs[len(given) :]
    tables, refs = refs[:N_TABLES], refs[N_TABLES:]
    acc, stage, held, theirs, both, work, padded, mine, sems, table_sems, out_sems = refs

    mine[0] = 0
    for home in range(len(PLACES)):

        def check(pair, carry, home=home):
            row = (home * PAIRS_DEV + pair) * LIST_WIDTH
            for kind in (1, 2) if second else (0,):
                here = listing[row + 2 * kind] == home
                if second:
                    gives_far = jnp.bool_(home in FAR_PLACES)
                    if kind == 2:
                        source = listing[row + 2 * kind + 1]
                        gives_far = (source >= FAR_PLACES[0]) & (source <= FAR_PLACES[-1])
                    here &= gives_far if part == 1 else jnp.logical_not(gives_far)

                @pl.when(here)
                def _(kind=kind):
                    at = mine[0]
                    mine[0] = at + 1
                    task = (at + 1) * TASK_WIDTH
                    mine[task] = home
                    mine[task + 1] = listing[row + 2 * kind + 1]
                    for c in range(5):
                        mine[task + 2 + c] = listing[row + 6 + c]
                    mine[task + 7] = kind

            return carry

        lax.fori_loop(0, PAIRS_DEV, check, 0)

    count = mine[0]
    steps = (count + 1) >> 1
    begin, end = 0, steps

    def table_copies():
        return [
            pltpu.make_async_copy(tables_in[i], tables[i], table_sems.at[i])
            for i in range(N_TABLES)
        ]

    def fetch(group, source, slot, target, sem):
        refs_of = boxes_in[group * (SOURCES + 1) : (group + 1) * (SOURCES + 1)]

        def start(ref, row):
            row = pl.multiple_of(row, 16)
            pltpu.make_async_copy(ref.at[pl.ds(row, BOX)], target, sem).start()

        for s in range(SOURCES):
            if s == 3:
                for part_of in range(2):

                    @pl.when((source == s) & ((slot >> 1) == part_of))
                    def _(part_of=part_of):
                        start(refs_of[3 + part_of], (slot & 1) * BOX)
            else:
                at = s if s < 3 else s + 1

                @pl.when(source == s)
                def _(at=at):
                    start(refs_of[at], slot * BOX)

    def each_load(step, act):
        for i in range(2):
            task = (step * 2 + i + 1) * TASK_WIDTH

            @pl.when(step * 2 + i < count)
            def _(i=i, task=task):
                kind = mine[task + 7]
                act(kind == 1, mine[task], mine[task + 2], 2 * i)
                act(kind == 2, mine[task + 1], mine[task + 3], 2 * i + 1)

    def start_loads(step, buffer):
        def act(of_trial, source, slot, i):
            if second:

                @pl.when(of_trial)
                def _():
                    fetch(1, source, slot, held.at[buffer, i], sems.at[buffer, i])

                @pl.when(jnp.logical_not(of_trial))
                def _():
                    fetch(0, source, slot, held.at[buffer, i], sems.at[buffer, i])
            else:
                fetch(0, source, slot, held.at[buffer, i], sems.at[buffer, i])

        each_load(step, act)

    def wait_loads(step, buffer):
        def act(of_trial, source, slot, i):
            pltpu.make_async_copy(
                boxes_in[0].at[pl.ds(0, BOX)], held.at[buffer, i], sems.at[buffer, i]
            ).wait()

        each_load(step, act)

    def sum_copies(into):
        copies = []
        for i, source in enumerate(given):
            vmem = stage.at[pl.ds(source * SET_ROWS, SET_ROWS)]
            if into:
                copies.append(pltpu.make_async_copy(sums_in[i], vmem, out_sems.at[i]))
            else:
                copies.append(pltpu.make_async_copy(vmem, outs[i], out_sems.at[i]))
        return copies

    @pl.when(begin < end)
    def _():
        start_loads(begin, begin & 1)
        for copy in table_copies():
            copy.start()

    if carried:
        for copy in sum_copies(True):
            copy.start()
    padded[...] = jnp.zeros(padded.shape, F32)

    def box_rows(i):
        return pl.ds(pl.multiple_of(i * BOX, BOX), BOX)

    if carried:
        for copy in sum_copies(True):
            copy.wait()

    def prepare(i, carry):
        if carried:
            keep = stage[box_rows(i), :].astype(F32)
            is_given = (i < 3 * ORB_DEV) | (i >= REGION_SOURCE * ORB_DEV)
            acc[box_rows(i), :] = jnp.where(is_given, keep, 0.0)
        else:
            acc[box_rows(i), :] = jnp.zeros((BOX, PLANE), F32)
        return carry

    lax.fori_loop(0, SOURCES * ORB_DEV, prepare, 0)

    def add(source, slot, lanes, value):
        at = box_rows(source * ORB_DEV + slot)
        acc[at, lanes] = acc[at, lanes] + value

    def one_step(step, carry):
        buffer = step & 1

        @pl.when(step + 1 < end)
        def _():
            start_loads(step + 1, 1 - buffer)

        wait_loads(step, buffer)
        for i in range(2):
            task = (step * 2 + i + 1) * TASK_WIDTH

            @pl.when(step * 2 + i < count)
            def _(i=i, task=task):
                def value(lanes):
                    return held[buffer, 2 * i + 1, :, lanes].astype(F32)

                def put(lanes, block):
                    theirs[i, :, lanes] = block

                shift_box(padded, value, put, mine[task + 4], mine[task + 5], mine[task + 6])

        @pl.when(step == begin)
        def _():
            for copy in table_copies():
                copy.wait()

        def density(b, some, r, c):
            lanes = pl.ds((r * BLOCKS_Z + c) * 128, 128)
            return held[buffer, 2 * b, some, lanes].astype(F32) * theirs[b, some, lanes]

        solve(density, both, work, *tables, 2)
        for i in range(2):
            task = (step * 2 + i + 1) * TASK_WIDTH
            there = step * 2 + i < count
            kind = mine[task + 7]

            @pl.when(there & (kind != 2))
            def _(i=i, task=task):
                near = rounded(work[pl.ds(i * BOX, BOX), :] * theirs[i])
                add(mine[task], mine[task + 2], pl.ds(0, PLANE), near)

            @pl.when(there & (kind != 1))
            def _(i=i, task=task):
                def value(lanes):
                    mine_box = held[buffer, 2 * i, :, lanes].astype(F32)
                    return rounded(work[pl.ds(i * BOX, BOX), lanes] * mine_box)

                def put(lanes, block):
                    add(mine[task + 1], mine[task + 3], lanes, block)

                shift_box(padded, value, put, -mine[task + 4], -mine[task + 5], -mine[task + 6])

        return carry

    lax.fori_loop(begin, end, one_step, 0)

    copies = sum_copies(False)
    for copy, source in zip(copies, given):

        def put(i, carry):
            stage[box_rows(i), :] = acc[box_rows(i), :].astype(BF16)
            return carry

        lax.fori_loop(source * ORB_DEV, (source + 1) * ORB_DEV, put, 0)
        copy.start()
    for copy in copies:
        copy.wait()


def exchange(part, listing, boxes, tables, sums=()):
    any_space = pl.BlockSpec(memory_space=pl.ANY)
    smem = pl.BlockSpec(memory_space=pltpu.SMEM)
    outs = [
        jax.ShapeDtypeStruct((SET_ROWS, PLANE), BF16) for _ in GIVEN[part]
    ]

    def kernel(*refs):
        exchange_kernel(part, *refs)

    return pl.pallas_call(
        kernel,
        out_shape=outs,
        in_specs=[smem] + [any_space] * (len(boxes) + len(tables) + len(sums)),
        out_specs=[any_space] * len(outs),
        scratch_shapes=[
            *[pltpu.VMEM(t.shape, t.dtype) for t in tables],
            pltpu.VMEM((SOURCES * ORB_DEV * BOX, PLANE), F32),
            pltpu.VMEM((SOURCES * ORB_DEV * BOX, PLANE), BF16),
            pltpu.VMEM((2, 4, BOX, PLANE), BF16),
            pltpu.VMEM((2, BOX, PLANE), F32),
            pltpu.VMEM((4 * BOX, PLANE), BF16),
            pltpu.VMEM((2 * BOX, PLANE), F32),
            pltpu.VMEM((WIDE_Y * WIDE_Z * ROWS_PADDED, 128), F32),
            pltpu.SMEM(((MAX_TASKS + 3) * TASK_WIDTH,), jnp.int32),
            pltpu.SemaphoreType.DMA((2, 4)),
            pltpu.SemaphoreType.DMA((N_TABLES,)),
            pltpu.SemaphoreType.DMA((SOURCES,)),
        ],
        compiler_params=pltpu.CompilerParams(vmem_limit_bytes=62 * 1024 * 1024),
        cost_estimate=pl.CostEstimate(
            flops=10_000_000_000, bytes_accessed=30_000_000, transcendentals=0
        ),
        name=("first_application", "second_early", "second_late")[part],
    )(listing, *boxes, *tables, *sums)


def reorder_kernel(with_notes, box, *refs):
    order, out = refs[-2:]
    for r in range(BLOCKS_Y):
        lanes = pl.ds(r * CHUNK, CHUNK)
        moved = jnp.dot(box[:, lanes], order[...], preferred_element_type=F32)
        out[pl.ds(0, SET_ROWS), lanes] = moved.astype(BF16)
    if with_notes:
        out[pl.ds(SET_ROWS, NOTE_ROWS), :] = refs[0][...]


def reorder(boxes, order, notes=()):
    rows = SET_ROWS + NOTE_ROWS * len(notes)

    def kernel(*refs):
        reorder_kernel(bool(notes), *refs)

    return pl.pallas_call(
        kernel,
        out_shape=jax.ShapeDtypeStruct((rows, PLANE), BF16),
        name="reorder",
        compiler_params=pltpu.CompilerParams(vmem_limit_bytes=32 * 1024 * 1024),
    )(boxes, *notes, order)


def total_kernel(*refs):
    *parts, order, out = refs
    for r in range(BLOCKS_Y):
        lanes = pl.ds(r * CHUNK, CHUNK)
        result = parts[0][:, lanes].astype(F32)
        for part in parts[1:]:
            result += part[:, lanes].astype(F32)
        moved = jnp.dot((-result).astype(BF16), order[...], preferred_element_type=F32)
        out[:, lanes] = moved.astype(BF16)


def total(parts, order):
    half = SET_ROWS // 2
    whole = pl.BlockSpec((CHUNK, CHUNK), lambda i: (0, 0))
    some = pl.BlockSpec((half, PLANE), lambda i: (i, 0))
    return pl.pallas_call(
        total_kernel,
        grid=(2,),
        out_shape=jax.ShapeDtypeStruct((SET_ROWS, PLANE), BF16),
        in_specs=[some] * len(parts) + [whole],
        out_specs=some,
        name="total",
        compiler_params=pltpu.CompilerParams(vmem_limit_bytes=32 * 1024 * 1024),
    )(*parts, order)


def moves(n_region):
    def step(dx, dz):
        pairs = []
        for region in range(n_region):
            sign = 1 - 2 * (region % 2)
            for x in range(GRID):
                for z in range(GRID):
                    to = (x + sign * dx) % GRID * GRID + (z + sign * dz) % GRID
                    pairs.append((region * N_SUB + x * GRID + z, region * N_SUB + to))

        def move(block):
            return lax.ppermute(block, ("region", "sub"), pairs)

        return move

    def across(distance):
        pairs = [(i, (i + distance) % n_region) for i in range(n_region)]

        def move(block):
            return lax.ppermute(block, "region", pairs)

        return move

    return step, across


def per_device(orbitals, trial_set, own_slot, partner_route, partner_slot, offsets):
    n_region = lax.axis_size("region")
    region = lax.axis_index("region")
    sub = lax.axis_index("sub")
    step, across = moves(n_region)
    tables = transform_tables()
    tables = [
        jnp.asarray(tables[k])
        for k in TABLES
    ]
    order, order_back = jnp.asarray(order_table()), jnp.asarray(order_table().T.copy())
    table, most = meeting_table()
    meta = jnp.concatenate([own_slot, partner_route[:, 0], partner_slot])
    where = jnp.stack([region, sub, jnp.int32(n_region)]).astype(jnp.int32)
    smem = pl.BlockSpec(memory_space=pltpu.SMEM)

    def planner(*refs):
        plan_kernel(most, *refs)

    chosen = pl.pallas_call(
        planner,
        out_shape=jax.ShapeDtypeStruct((LISTED,), jnp.int32),
        in_specs=[smem] * 4,
        out_specs=smem,
        scratch_shapes=[pltpu.SMEM((2 * len(PLACES),), jnp.int32)],
        name="plan",
    )(where, meta, offsets.reshape(-1), jnp.asarray(table))

    def near_places(boxes):
        return step(0, 1)(boxes), step(1, 0)(boxes), across(-1)(boxes)

    def cut(b01, b10):
        return b01[: 2 * BOX], b10[2 * BOX :]

    def far_places(b01, b10, halves):
        low, high = halves
        return step(1, 0)(low), step(0, 1)(high), step(0, -1)(b10), step(-1, 0)(b01)

    def begin_back(parts):
        return step(-1, 0)(parts[3]), step(0, 1)(parts[4]), step(1, 0)(parts[5])

    def merge(c01, c10, arrived):
        r11, r13, r31 = arrived
        m01 = (c01.astype(F32) + r31.astype(F32) + r11.astype(F32)).astype(BF16)
        m10 = (c10.astype(F32) + r13.astype(F32)).astype(BF16)
        return step(0, -1)(m01), step(-1, 0)(m10)

    def finish(own, abroad, merged):
        result = total([own, abroad, *merged], order_back)
        return result.reshape(ORB_DEV, BOX, PLANE)

    ordered = lax.optimization_barrier
    notes = jnp.pad(chosen.astype(BF16)[None], ((0, NOTE_ROWS - 1), (0, PLANE - LISTED)))
    trials = reorder(trial_set.reshape(SET_ROWS, PLANE), order)
    boxes = reorder(orbitals.reshape(SET_ROWS, PLANE), order, (notes,))
    t01, t10, t_abroad = near_places(trials)
    boxes, t01, t10, t_abroad = ordered((boxes, t01, t10, t_abroad))
    t_cut = cut(t01, t10)
    o01, o10, o_abroad = near_places(boxes)
    o01, o10, o_abroad, t_cut = ordered((o01, o10, o_abroad, t_cut))
    o_far = far_places(o01, o10, cut(o01, o10))
    t01, t10, t_cut, o_far = ordered((t01, t10, t_cut, o_far))
    t_far = far_places(t01, t10, t_cut)
    orbital_boxes = [boxes, o01, o10, *o_far, o_abroad]
    notes = [boxes, o01, o10, o_far[1], o_far[2], o_far[3]]
    listing = jnp.concatenate([n[-NOTE_ROWS, :LISTED] for n in notes]).astype(jnp.int32)
    first = exchange(0, listing, orbital_boxes, tables)
    arrived_first = begin_back(first)
    abroad_first = across(1)(first[6])
    first, listing, t_far = ordered((first, listing, t_far))
    all_boxes = orbital_boxes + [trials, t01, t10, *t_far, t_abroad]
    early = exchange(1, listing, all_boxes, tables)
    early, first, arrived_first, abroad_first = ordered((early, first, arrived_first, abroad_first))
    merged_first = merge(first[1], first[2], arrived_first)
    arrived_second = begin_back(early)
    late = exchange(2, listing, all_boxes, tables, [early[i] for i in GIVEN[2]])
    late, merged_first, arrived_second = ordered((late, merged_first, arrived_second))
    own, c01, c10, c_abroad = late
    abroad_second = across(1)(c_abroad)
    merged_second = merge(c01, c10, arrived_second)
    result_first = finish(first[0], abroad_first, merged_first)
    return result_first, finish(own, abroad_second, merged_second)


def solution(mesh):
    in_specs = (
        P(("region", "sub"), None, None),
        P(("region", "sub"), None, None),
        P(("region", "sub")),
        P(("region", "sub"), None),
        P(("region", "sub")),
        P(),
    )
    out_specs = (P(("region", "sub"), None, None), P(("region", "sub"), None, None))
    return jax.shard_map(
        per_device, mesh=mesh, in_specs=in_specs, out_specs=out_specs, check_vma=False
    )
```
